32 devices in a mesh: groups: 2 (over x), basis: 16 (over z, y, core).
Axes of the slice: x: 2, y: 2, z: 4, core: 2. Of those that a mesh axis runs over, the one named last changes fastest.
Arguments:
- factors: bfloat16 [32, 30, 512, 128], P(('groups', 'basis')), parts along dimension 0, may hold values from -3 to 3
- coefs: bfloat16 [32, 30, 128], P(('groups', 'basis')), parts along dimension 0, may hold values from -0.0234375 to 0.0234375
- domains: int32 [32, 30], P('groups'), parts along dimension 0, may hold values from 0 to 89, as said below
- pairs: int32 [32, 4], P(('groups', 'basis')), parts along dimension 0, may hold values 0 or 1
Outputs:
- exchange_band: float32 [32, 9, 128, 128], P(('groups', 'basis')), parts along dimension 0
- coulomb_half: float32 [32, 30, 128], P(('groups', 'basis')), parts along dimension 0
The draws below stay inside these ranges and needn't reach their ends.
There are 2 independent parts, one for each index of `groups`. The reference program is written for one: setup_inputs(seed, part) draws one part's arguments, and reference() takes and returns one part's arrays. A program takes and returns all parts, laid end to end along the dimension named above; each array names one. Nothing has to cross between parts.
Inputs may be any that keep to these rules, and one draw needn't show every extreme that they name: `domains`: each row holds 30 different ids, all in [2 b, 2 b + 60) for block b, among them 2 b and 2 b + 2 * 30 - 1.
All inputs are finite; a program needn't handle non-finite values. No bound on the sum of `pairs` on one device may be relied on, other than what follows from the above.
Results may differ from the reference program's by a relative error of at most 0.003.
Values may be sent and summed in bfloat16 or wider, within the bound.
No kernel may reach another device: no remote copies, remote signals or barrier semaphores. Data moves between devices by JAX's collectives and lax.ppermute only.
A program may use at most 128 MiB of HBM per device.

```python
import jax
import jax.numpy as jnp
from jax import lax

BLOCK = 128
AUX = 512
DOMW = 30
DEPTH = 4
NBLK = 16


def draw_domains(key, part):
    key = jax.random.fold_in(key, 7)
    inner_key = jax.random.fold_in(key, 1)
    order_key = jax.random.fold_in(key, 2)
    inner_keys = jax.random.split(inner_key, NBLK)
    order_keys = jax.random.split(order_key, NBLK)
    inner = jax.vmap(lambda one: jax.random.permutation(one, 2 * DOMW - 2))(inner_keys)
    inner = inner[:, :DOMW - 2].astype(jnp.int32) + 1
    ends = jnp.broadcast_to(jnp.array([0, 2 * DOMW - 1], jnp.int32), (NBLK, 2))
    offsets = jnp.concatenate([ends, inner], axis=1)
    shuffled = jax.vmap(lambda one, row: jax.random.permutation(one, row))(order_keys, offsets)
    start = 2 * jnp.arange(NBLK, dtype=jnp.int32)
    return (start[:, None] + shuffled.astype(jnp.int32)).astype(jnp.int32)


def plant(values, stream_key, least, largest):
    extent = values.shape
    place = [jax.random.randint(jax.random.fold_in(stream_key, axis), (), 0, extent[axis]) for axis in range(len(extent))]
    values = values.at[tuple(place)].set(least)
    longest = extent.index(max(extent))
    place[longest] = (place[longest] + 1) % extent[longest]
    return values.at[tuple(place)].set(largest)


def level_of(key, extent, cuts, least, high):
    level, own = 1.0, jax.random.fold_in(key, 6)
    for position, shards_of in cuts:
        steps = jnp.exp(jax.random.uniform(jax.random.fold_in(own, position), (shards_of,), jnp.float32, least / len(cuts), high / len(cuts)))
        level = level * jnp.repeat(steps, extent[position] // shards_of).reshape([-1 if axis == position else 1 for axis in range(len(extent))])
    return level


def noise(stream_key, shape, deviation, bound, shards=(), held_as=jnp.bfloat16):
    values = jax.random.normal(stream_key, shape, jnp.float32) * deviation
    if len(shards) > 0:
        values = level_of(stream_key, shape, shards, -0.22, 0.18) * values
    return jnp.clip(values, min=-bound, max=bound).astype(held_as)


def setup_inputs(seed: int = 0, part: int = 0) -> dict:
    seeds = jax.random.split(jax.random.key(seed), 5)
    part_splits = jax.random.split(jax.random.fold_in(seeds[4], part), 5)
    factors = noise(part_splits[0], (NBLK, DOMW, AUX, BLOCK), (AUX ** -0.25), 3.0, ((0, 16),))
    coefs = noise(part_splits[1], (NBLK, DOMW, BLOCK), (NBLK * DOMW * BLOCK) ** -0.5, 0.0234375, ((0, 16),))
    domains = draw_domains(jax.random.fold_in(jax.random.fold_in(seeds[4], part), 71), part)
    pairs = plant((jax.random.randint(part_splits[3], (NBLK, DEPTH), 0, 2) < 1).astype(jnp.int32), jax.random.fold_in(part_splits[3], 1), 0, 1)
    return {"factors": factors, "coefs": coefs, "domains": domains, "pairs": pairs}


def contract(own, own_dom, remote, remote_dom):
    match = (own_dom[:, None] == remote_dom[None, :]).astype(jnp.float32)
    aligned = jnp.einsum("kl,lpm->kpm", match, remote.astype(jnp.float32))
    aligned = aligned.astype(jnp.bfloat16).astype(jnp.float32)
    left = own.astype(jnp.float32).reshape(-1, own.shape[-1])
    return jnp.dot(left.T, aligned.reshape(-1, own.shape[-1]))


def reference(factors, coefs, domains, pairs):
    def partial_term(index):
        blk = factors[index].astype(jnp.float32)
        return jnp.einsum("kpm,km->p", blk, coefs[index].astype(jnp.float32))

    gamma = jnp.sum(lax.map(partial_term, jnp.arange(NBLK, dtype=jnp.int32)), axis=0)
    gamma_low = gamma.astype(jnp.bfloat16).astype(jnp.float32)

    def coulomb_term(index):
        return jnp.einsum("kpm,p->km", factors[index].astype(jnp.float32), gamma_low)

    coulomb_half = lax.map(coulomb_term, jnp.arange(NBLK, dtype=jnp.int32))

    def forward(index):
        own = factors[index]
        own_dom = domains[index]
        blocks = [contract(own, own_dom, own, own_dom)]
        for offset in range(1, DEPTH + 1):
            other = jnp.minimum(index + offset, NBLK - 1).astype(jnp.int32)
            valid = jnp.logical_and(pairs[index, offset - 1] == 1, index + offset < NBLK)
            value = contract(own, own_dom, factors[other], domains[other])
            blocks.append(jnp.where(valid, value, jnp.zeros_like(value)))
        return jnp.stack(blocks)

    ahead = lax.map(forward, jnp.arange(NBLK, dtype=jnp.int32))
    band = [None] * (2 * DEPTH + 1)
    band[DEPTH] = ahead[:, 0]
    for offset in range(1, DEPTH + 1):
        band[DEPTH + offset] = ahead[:, offset]
        moved = jnp.swapaxes(ahead[:, offset], 1, 2)
        zeros = jnp.zeros((offset, BLOCK, BLOCK), jnp.float32)
        band[DEPTH - offset] = jnp.concatenate([zeros, moved[: NBLK - offset]], axis=0)
    return jnp.stack(band, axis=1), coulomb_half
```

```python
import functools

import jax
import jax.numpy as jnp
from jax import lax
from jax.experimental import pallas as pl
from jax.experimental.pallas import tpu as pltpu
from jax.sharding import PartitionSpec as P

F32 = jnp.float32
BF16 = jnp.bfloat16

XJ, XO, YJ, YO, FJ, FO, GJ, GO = range(8)
PRODUCTS = (
    (XJ, XJ, None),
    (XJ, XO, None),
    (XJ, YJ, "main"),
    (XJ, YO, "main"),
    (YJ, XO, "main"),
    (XJ, FJ, "main"),
    (None, None, "main"),
    (YJ, FJ, "main"),
    (YJ, FO, "main"),
    (FJ, YO, "main"),
    (XJ, GJ, "side"),
    (None, None, "side"),
)
FIRST_SHARED = 2
CROSS_F, CROSS_G = 6, 11
CUT = 192


def chip_route(count, target, swap=False):
    chips = count // 2
    route = []
    for chip in range(chips):
        to = target(chip)
        if 0 <= to < chips:
            for core in range(2):
                route.append((2 * chip + core, 2 * to + (1 - core if swap else core)))
    return route


def matches(left, right, valid):
    rows = left.shape[1]
    width = 32
    equal = jnp.logical_and(left[:, :, None] == right[:, None, :], valid[:, None, None])
    row = jnp.arange(rows, dtype=jnp.int32)
    partner = jnp.sum(jnp.where(equal, row[None, None, :], 0), axis=2)
    hit = jnp.sum(equal.astype(jnp.int32), axis=2)
    place = jnp.sum(jnp.where(row[None, None, :] < row[None, :, None], hit[:, None, :], 0), axis=2)
    slot = jnp.arange(width, dtype=jnp.int32)
    chosen = jnp.logical_and(place[:, None, :] == slot[None, :, None], hit[:, None, :] == 1)
    mine = jnp.sum(jnp.where(chosen, row[None, None, :], 0), axis=2)
    theirs = jnp.sum(jnp.where(chosen, partner[:, None, :], 0), axis=2)
    return jnp.sum(hit, axis=1), mine, theirs


def multiply(left, right):
    return lax.dot_general(left, right, (((0,), (0,)), ((), ())), preferred_element_type=F32)


def chunk_kernel(first, last, start, size, stack, *refs):
    refs = list(refs)
    place, number, mine, theirs = refs[:4]
    refs = refs[4:]
    before = None if first else refs.pop(0)
    blocks, outs = refs[:8], refs[8:]
    total = outs[0] if not last else outs[-1]
    if first:
        total[...] = jnp.zeros_like(total)
    else:
        total[...] = before[...]
    flag = place[2] == 1

    def rows_of(block, row, half):
        if block in (XJ, XO):
            offset = pl.multiple_of(place[0 if half == "main" else 1] + start, 16)
            return blocks[block][row, pl.ds(offset, size), :]
        return blocks[block][row]

    def operand(q, side, row):
        left_or_right = PRODUCTS[q][side]
        half = PRODUCTS[q][2]
        if left_or_right is not None:
            return rows_of(left_or_right, row, half)
        if q == CROSS_F:
            one, two = ((FJ, XJ), (XO, FO))[side]
        else:
            one, two = ((XJ, GJ), (GO, XO))[side]
        return jnp.where(flag, rows_of(one, row, half), rows_of(two, row, half))

    def add(q, group):
        lefts, rights = [], []
        for i in range(stack):
            slot = group * stack + i
            left = operand(q, 0, mine[q, slot])
            if stack > 1:
                left = jnp.where(slot < number[q], left, jnp.zeros_like(left))
            lefts.append(left)
            rights.append(operand(q, 1, theirs[q, slot]))
        if stack == 1:
            left = jnp.where(group < number[q], lefts[0], jnp.zeros_like(lefts[0]))
            total[q] += multiply(left, rights[0])
        else:
            total[q] += multiply(jnp.concatenate(lefts, axis=0), jnp.concatenate(rights, axis=0))

    shared = range(FIRST_SHARED, len(PRODUCTS))
    most = number[FIRST_SHARED]
    for q in shared:
        most = jnp.maximum(most, number[q])

    def step(group, carry):
        for q in shared:
            add(q, group)
        return carry

    lax.fori_loop(0, (most + stack - 1) // stack, step, 0)

    if first:
        def own(row, carry):
            left = blocks[XJ][row]
            total[0] += multiply(left, left)
            return carry

        lax.fori_loop(0, blocks[XJ].shape[0], own, 0)

        def inner(slot, carry):
            total[1] += multiply(blocks[XJ][mine[1, slot]], blocks[XO][theirs[1, slot]])
            return carry

        lax.fori_loop(0, number[1], inner, 0)

    if last:
        kept, to_y, to_f, to_g = outs[:4]
        for q, place_in in ((0, 0), (1, 1), (2, 2), (3, 3), (5, 4), (10, 5)):
            kept[place_in] = total[q]
        kept[6] = jnp.where(flag, total[CROSS_G], total[CROSS_F])
        to_y[0] = total[2].T
        to_y[1] = total[4]
        to_y[2] = total[7]
        to_y[3] = total[8]
        to_f[0] = total[5].T
        to_f[1] = jnp.where(flag, total[CROSS_F], 0.0)
        to_f[2] = total[7].T
        to_f[3] = total[9]
        to_g[0] = total[10].T
        to_g[1] = jnp.where(flag, 0.0, total[CROSS_G])


def chunk(first, last, start, size, stack, tables, before, blocks):
    width = blocks[0].shape[-1]
    square = lambda n: jax.ShapeDtypeStruct((n, width, width), F32)
    smem = pl.BlockSpec(memory_space=pltpu.SMEM)
    vmem = pl.BlockSpec(memory_space=pltpu.VMEM)
    inputs = list(tables) + ([] if first else [before]) + list(blocks)
    specs = [smem] * len(tables) + [vmem] * (len(inputs) - len(tables))
    products = len(PRODUCTS)
    if last:
        out_shape, out_specs = [square(7), square(4), square(4), square(2)], [vmem] * 4
        scratch = [pltpu.VMEM((products, width, width), F32)]
    else:
        out_shape, out_specs, scratch = square(products), vmem, []
    return pl.pallas_call(
        functools.partial(chunk_kernel, first, last, start, size, stack),
        out_shape=out_shape,
        in_specs=specs,
        out_specs=out_specs,
        scratch_shapes=scratch,
        compiler_params=pltpu.CompilerParams(vmem_limit_bytes=50 * 2**20),
        cost_estimate=pl.CostEstimate(
            flops=2 * width * width * size * 15 * products, bytes_accessed=8 * 30 * size * width * 2, transcendentals=0
        ),
    )(*inputs)


def band_kernel(depth, place, keep, kept, from_y, from_f, from_g, band):
    def put(slot, value):
        where = place[slot]
        band[where] = jnp.where(keep[where] == 1, value, 0.0)

    band[depth] = kept[0]
    put(0, kept[1])
    put(1, kept[2] + from_y[0])
    put(2, kept[3] + from_y[1])
    put(3, from_y[2] + from_f[2])
    put(4, from_y[3] + from_f[3])
    put(5, kept[4] + from_g[0])
    put(6, kept[5] + from_f[0])
    put(7, kept[6] + from_f[1] + from_g[1])


def finish(depth, place, keep, kept, from_y, from_f, from_g):
    width = kept.shape[-1]
    smem = pl.BlockSpec(memory_space=pltpu.SMEM)
    vmem = pl.BlockSpec(memory_space=pltpu.VMEM)
    return pl.pallas_call(
        functools.partial(band_kernel, depth),
        out_shape=jax.ShapeDtypeStruct((2 * depth + 1, width, width), F32),
        in_specs=[smem] * 2 + [vmem] * 4,
        out_specs=vmem,
        compiler_params=pltpu.CompilerParams(vmem_limit_bytes=50 * 2**20),
    )(place, keep, kept, from_y, from_f, from_g)


def summed(values, count):
    if count & (count - 1):
        return lax.psum(values, "basis")
    step = 1
    while step < count:
        values = values + lax.ppermute(values, "basis", [(i, i ^ step) for i in range(count)])
        step *= 2
    return values


def per_device(factors, coefs, domains, pairs):
    own = factors[0]
    coef = coefs[0]
    rows, aux, width = own.shape
    count = lax.axis_size("basis")
    depth = pairs.shape[1]
    me = lax.axis_index("basis")
    core, chip = me % 2, me // 2
    odd = chip % 2
    flag = core == odd
    half = aux // 2
    main, side = odd * half, (1 - odd) * half

    swap = chip_route(count, lambda c: c, swap=True)
    across = chip_route(count, lambda c: c ^ 1)
    f_route = chip_route(count, lambda c: c - 2 if c % 2 == 0 else c + 2)
    g_route = chip_route(count, lambda c: c + 2 if c % 2 == 0 else c - 2)
    f_back, g_back = [(b, a) for a, b in f_route], [(b, a) for a, b in g_route]
    send = lambda value, route: lax.ppermute(value, "basis", route)

    f_chip = jnp.where(odd == 0, chip + 2, chip - 2)
    g_chip = jnp.where(odd == 0, chip - 2, chip + 2)
    chips = count // 2
    ids, here = [], []
    for other in (chip, chip ^ 1, f_chip, g_chip):
        there = jnp.logical_and(other >= 0, other < chips)
        two = lax.dynamic_slice_in_dim(domains, 2 * jnp.clip(other, 0, chips - 1), 2, 0)
        ids += [jnp.where(core == 0, two[0], two[1]), jnp.where(core == 0, two[1], two[0])]
        here += [there, there]
    left, right, valid = [], [], []
    for q, (a, b, _) in enumerate(PRODUCTS):
        if a is None:
            (a, b), (c, d) = (((FJ, XO), (XJ, FO)) if q == CROSS_F else ((XJ, GO), (GJ, XO)))
            left.append(jnp.where(flag, ids[a], ids[c]))
            right.append(jnp.where(flag, ids[b], ids[d]))
        else:
            left.append(ids[a])
            right.append(ids[b])
        valid.append(jnp.logical_and(here[a], here[b]))
    number, mine, theirs = matches(jnp.stack(left), jnp.stack(right), jnp.stack(valid))
    place = jnp.stack([main, side, flag.astype(jnp.int32)]).astype(jnp.int32)
    tables = (place, number, mine, theirs)

    cuts = ((0, CUT), (CUT, half - CUT))
    part = lambda at, cut: lax.dynamic_slice_in_dim(own, at + cut[0], cut[1], 1)
    other = send(own, swap)
    pieces = []
    for cut in cuts:
        main_part, side_part = part(main, cut), part(side, cut)
        y = send(side_part, across)
        f = send(main_part, f_route)
        g = send(side_part, g_route)
        pieces.append((own, other, y, send(y, swap), f, send(f, swap), g, send(g, swap)))

    total = chunk(True, False, cuts[0][0], cuts[0][1], 2, tables, None, pieces[0])
    kept, to_y, to_f, to_g = chunk(False, True, cuts[1][0], cuts[1][1], 4, tables, total, pieces[1])
    from_y, from_f, from_g = send(to_y, across), send(to_f, f_back), send(to_g, g_back)

    partial_sum = jnp.einsum("kpm,km->p", own, coef, preferred_element_type=F32)
    marks = (jnp.arange(count)[:, None] == me).astype(F32) * pairs.astype(F32)
    gathered = summed(jnp.concatenate([partial_sum, marks.reshape(-1)]), count)
    gamma_low = gathered[:aux].astype(BF16)
    coulomb_half = jnp.einsum("kpm,p->km", own, gamma_low, preferred_element_type=F32)
    all_pairs = gathered[aux:].reshape(count, depth)

    keep = [jnp.int32(1)] * (2 * depth + 1)
    for r in range(1, depth + 1):
        keep[depth + r] = (pairs[0, r - 1] == 1).astype(jnp.int32)
        lower = lax.dynamic_slice_in_dim(all_pairs, jnp.maximum(me - r, 0), 1, 0)[0, r - 1]
        keep[depth - r] = (lower > 0.5).astype(jnp.int32)
    sign = 1 - 2 * odd
    cross = 1 - 2 * core
    y_at, f_at = 2 * sign, 4 * sign
    spots = [cross, y_at, y_at + cross, -y_at, -y_at + cross, f_at, -f_at, jnp.where(core == 0, -3, 3)]
    band = finish(depth, jnp.stack(spots).astype(jnp.int32) + depth, jnp.stack(keep), kept, from_y, from_f, from_g)
    return (band[None], coulomb_half[None])


def solution(mesh):
    placed = (
        P(("groups", "basis"), None, None, None),
        P(("groups", "basis"), None, None),
        P("groups", None),
        P(("groups", "basis"), None),
    )
    return jax.shard_map(
        per_device,
        mesh=mesh,
        in_specs=placed,
        out_specs=(P(("groups", "basis"), None, None, None), P(("groups", "basis"), None, None)),
        check_vma=False,
    )
```

```python
import functools

import jax
import jax.numpy as jnp
from jax import lax
from jax.experimental import pallas as pl
from jax.experimental.pallas import tpu as pltpu
from jax.sharding import PartitionSpec as P

F32 = jnp.float32
BF16 = jnp.bfloat16

XJ, XO, YJ, YO, YO_HIGH, FJ, GJ, XS = range(8)
XY, XYO, XF, YF, YOF, XG, CROSS = range(7)
PRODUCTS = ((XJ, YJ), (XO, YJ), (XJ, FJ), (YJ, FJ), (YO, FJ), (XJ, GJ), (XO, None))
OWN = len(PRODUCTS)
STACK, OWN_STACK = 9, 4
LIMIT = 12 * 2**20


def cost(*arrays):
    return pl.CostEstimate(flops=1, bytes_accessed=sum(a.size * a.dtype.itemsize for a in arrays), transcendentals=0)


def smem(n):
    return [pl.BlockSpec(memory_space=pltpu.SMEM)] * n


def vmem(n):
    return [pl.BlockSpec(memory_space=pltpu.VMEM)] * n


def squares(n, width):
    return jax.ShapeDtypeStruct((n, width, width), F32)


def multiply(left, right):
    return lax.dot_general(left, right, (((0,), (0,)), ((), ())), preferred_element_type=F32)


def chip_route(count, target, swap=False):
    chips = count // 2
    route = []
    for chip in range(chips):
        to = target(chip)
        if 0 <= to < chips:
            for core in range(2):
                route.append((2 * chip + core, 2 * to + (1 - core if swap else core)))
    return route


def place_of(me):
    core, chip = me & 1, me >> 1
    odd = chip & 1
    return core, chip, odd, core == odd, chip + 2 - 4 * odd, chip - 2 + 4 * odd


def cut_kernel(size, me, own, side, main, sems):
    odd = place_of(me[0])[2]
    copies = []
    for i, (out, start) in enumerate(((side, (1 - odd) * size), (main, odd * size))):
        rows = pl.ds(pl.multiple_of(start, 16), size)
        copies.append(pltpu.make_async_copy(own.at[:, rows, :], out, sems.at[i]))
    for copy in copies:
        copy.start()
    for copy in copies:
        copy.wait()


def cut(me, own):
    rows, aux, width = own.shape
    part = jax.ShapeDtypeStruct((rows, aux // 2, width), own.dtype)
    return pl.pallas_call(
        functools.partial(cut_kernel, aux // 2),
        out_shape=[part] * 2,
        in_specs=smem(1) + vmem(1),
        out_specs=vmem(2),
        scratch_shapes=[pltpu.SemaphoreType.DMA((2,))],
        compiler_params=pltpu.CompilerParams(vmem_limit_bytes=LIMIT),
        cost_estimate=cost(own, own),
    )(me, own)


def find_matches(here, domains, number, mine, theirs, spot):
    count, rows = domains.shape
    width = mine.shape[1]
    core, chip, odd, flag, f_chip, g_chip = place_of(here)
    cross_chip = jnp.where(flag, f_chip, g_chip)
    block = {XJ: (chip, core), XO: (chip, 1 - core), YJ: (chip ^ 1, core), YO: (chip ^ 1, 1 - core)}
    block |= {FJ: (f_chip, core), GJ: (g_chip, core), None: (cross_chip, core)}

    for q, (left, right) in enumerate(PRODUCTS + ((XJ, XO),)):
        there, ids = [], []
        for name in (left, right):
            at, one = block[name]
            there.append(jnp.logical_and(at >= 0, 2 * at < count))
            ids.append(2 * jnp.clip(at, 0, count // 2 - 1) + one)
        both = jnp.logical_and(*there)
        base = 2 * ids[1]

        def clear(i, carry):
            spot[i] = -1
            return carry

        def fill(row, carry):
            spot[domains[ids[1], row] - base] = row
            return carry

        def clean(slot, carry):
            mine[q, slot] = 0
            theirs[q, slot] = 0
            return carry

        def scan(row, found):
            away = domains[ids[0], row] - base
            inside = jnp.logical_and(away >= 0, away < 2 * rows)
            other_row = spot[jnp.clip(away, 0, 2 * rows - 1)]
            hit = jnp.logical_and(jnp.logical_and(inside, both), other_row >= 0)
            mine[q, found] = row
            theirs[q, found] = jnp.maximum(other_row, 0)
            return found + hit.astype(jnp.int32)

        lax.fori_loop(0, 2 * rows, clear, 0, unroll=10)
        lax.fori_loop(0, rows, fill, 0, unroll=10)
        lax.fori_loop(0, width, clean, 0, unroll=9)
        number[q] = lax.fori_loop(0, rows, scan, 0, unroll=5)


def own_kernel(me, domains, pairs, own, other, coef, out, share, number, mine, theirs, spot):
    rows, aux, width = own.shape
    here = me[0]
    find_matches(here, domains, number, mine, theirs, spot)
    out[...] = jnp.zeros_like(out)
    size = max(n for n in range(1, 11) if rows % n == 0)

    def square(step, carry):
        left = own[pl.ds(size * step, size)].reshape(size * aux, width)
        out[0] += multiply(left, left)
        return carry

    lax.fori_loop(0, rows // size, square, 0)

    def beside(step, carry):
        lefts, rights = [], []
        for i in range(OWN_STACK):
            slot = OWN_STACK * step + i
            left = own[mine[OWN, slot]]
            lefts.append(jnp.where(slot < number[OWN], left, jnp.zeros_like(left)))
            rights.append(other[theirs[OWN, slot]])
        out[1] += multiply(jnp.concatenate(lefts, axis=0), jnp.concatenate(rights, axis=0))
        return carry

    lax.fori_loop(0, (number[OWN] + OWN_STACK - 1) // OWN_STACK, beside, 0)

    tile = 128
    for start in range(0, aux, tile):
        total = jnp.zeros((tile, width), F32)
        for row in range(rows):
            total += own[row, start:start + tile, :].astype(F32) * coef[row:row + 1, :].astype(F32)
        share[:, start:start + tile] = jnp.sum(total.T, axis=0, keepdims=True)
    depth = pairs.shape[1]
    lane = lax.broadcasted_iota(jnp.int32, (1, share.shape[1] - aux), 1)
    marks = jnp.zeros(lane.shape, F32)
    for r in range(depth):
        marks = jnp.where(lane == here * depth + r, pairs[0, r].astype(F32), marks)
    share[:, aux:] = marks


def own_products(me, domains, pairs, own, other, coef):
    rows, aux, width = own.shape
    count = domains.shape[0]
    marks = -(-count * pairs.shape[1] // 128) * 128
    most = max(-(-rows // n) * n for n in (STACK, OWN_STACK))
    table = jax.ShapeDtypeStruct((OWN + 1, most), jnp.int32)
    return pl.pallas_call(
        own_kernel,
        out_shape=[
            squares(2, width),
            jax.ShapeDtypeStruct((1, aux + marks), F32),
            jax.ShapeDtypeStruct((OWN + 1,), jnp.int32),
            table,
            table,
        ],
        in_specs=smem(3) + vmem(3),
        out_specs=vmem(2) + smem(3),
        scratch_shapes=[pltpu.SMEM((2 * rows,), jnp.int32)],
        compiler_params=pltpu.CompilerParams(vmem_limit_bytes=LIMIT),
        cost_estimate=cost(own, other),
    )(me, domains, pairs, own, other, coef)


def relay_kernel(value, *refs):
    shares, (low, high, total, sems) = refs[:-4], refs[-4:]
    size = low.shape[1]
    copies = [
        pltpu.make_async_copy(value.at[:, :size, :], low, sems.at[0]),
        pltpu.make_async_copy(value.at[:, size:, :], high, sems.at[1]),
    ]
    for copy in copies:
        copy.start()
    total[...] = sum(share[...] for share in shares)
    for copy in copies:
        copy.wait()


def relay(value, shares):
    rows, size, width = value.shape
    part = jax.ShapeDtypeStruct((rows, size // 2, width), value.dtype)
    return pl.pallas_call(
        relay_kernel,
        out_shape=[part, part, jax.ShapeDtypeStruct(shares[0].shape, F32)],
        in_specs=vmem(1 + len(shares)),
        out_specs=vmem(3),
        scratch_shapes=[pltpu.SemaphoreType.DMA((2,))],
        compiler_params=pltpu.CompilerParams(vmem_limit_bytes=LIMIT),
        cost_estimate=cost(value, value),
    )(value, *shares)


def shared_kernel(me, number, mine, theirs, *refs):
    blocks, shares = refs[:8], refs[8:-8]
    kept, to_y, to_f, to_g, to_mate, coulomb, summed, total = refs[-8:]
    rows, size, _ = blocks[XJ].shape
    _, _, odd, flag, _, _ = place_of(me[0])
    main_half = pl.ds(pl.multiple_of(odd * size, 16), size)
    cross_half = pl.ds(pl.multiple_of(jnp.where(flag, odd, 1 - odd) * size, 16), size)
    total[...] = jnp.zeros_like(total)

    def add(q, group):
        lefts, rights = [], []
        left_block, right_block = PRODUCTS[q]
        if q == XG:
            left_block = XS
        for i in range(STACK):
            slot = group * STACK + i
            row, other_row = mine[q, slot], theirs[q, slot]
            if left_block == XO:
                left = blocks[XO][row, cross_half if q == CROSS else main_half, :]
            elif left_block == YO:
                left = jnp.concatenate([blocks[YO][row], blocks[YO_HIGH][row]], axis=0)
            else:
                left = blocks[left_block][row]
            lefts.append(jnp.where(slot < number[q], left, jnp.zeros_like(left)))
            if q == CROSS:
                rights.append(jnp.where(flag, blocks[FJ][other_row], blocks[GJ][other_row]))
            else:
                rights.append(blocks[right_block][other_row])
        total[q] += multiply(jnp.concatenate(lefts, axis=0), jnp.concatenate(rights, axis=0))

    products = range(len(PRODUCTS))
    most = number[0]
    for q in products:
        most = jnp.maximum(most, number[q])

    def step(group, carry):
        for q in products:
            add(q, group)
        return carry

    lax.fori_loop(0, (most + STACK - 1) // STACK, step, 0)

    kept[0] = total[XY]
    kept[1] = total[XF]
    kept[2] = total[XG]
    to_y[0] = total[XY].T
    to_y[1] = total[XYO].T
    to_y[2] = total[YF]
    to_y[3] = total[YOF]
    to_f[0] = total[XF].T
    to_f[1] = jnp.where(flag, total[CROSS].T, 0.0)
    to_f[2] = total[YF].T
    to_f[3] = total[YOF].T
    to_g[0] = total[XG].T
    to_g[1] = jnp.where(flag, 0.0, total[CROSS].T)
    to_mate[0] = total[XYO]
    to_mate[1] = total[CROSS]

    gathered = sum(share[...] for share in shares)
    summed[...] = gathered
    low, high = gathered[:, :size], gathered[:, size:2 * size]
    main_gamma = jnp.where(odd == 1, high, low).astype(BF16)
    side_gamma = jnp.where(odd == 1, low, high).astype(BF16)
    for row in range(rows):
        part = jnp.dot(main_gamma, blocks[XJ][row], preferred_element_type=F32)
        coulomb[0, row:row + 1, :] = part + jnp.dot(side_gamma, blocks[XS][row], preferred_element_type=F32)


def shared_products(me, tables, blocks, shares):
    rows, _, width = blocks[0].shape
    flat = jax.ShapeDtypeStruct
    return pl.pallas_call(
        shared_kernel,
        out_shape=[squares(n, width) for n in (3, 4, 4, 2, 2)]
        + [flat((1, rows, width), F32), flat(shares[0].shape, F32)],
        in_specs=smem(1 + len(tables)) + vmem(len(blocks) + len(shares)),
        out_specs=vmem(7),
        scratch_shapes=[pltpu.VMEM((len(PRODUCTS), width, width), F32)],
        compiler_params=pltpu.CompilerParams(vmem_limit_bytes=2 * LIMIT),
        cost_estimate=cost(*blocks),
    )(me, *tables, *blocks, *shares)


def band_kernel(aux, me, pairs, summed, own, kept, from_y, from_f, from_g, from_mate, passed, band):
    depth = pairs.shape[1]
    here = me[0]
    core, _, odd, _, _, _ = place_of(here)
    sign, cross = 1 - 2 * odd, 1 - 2 * core

    def put(ahead, value):
        far = jnp.abs(ahead)
        lower = summed[0, aux + jnp.maximum(here - far, 0) * depth + far - 1] > 0.5
        upper = pairs[0, far - 1] == 1
        there = jnp.logical_or(jnp.logical_and(ahead > 0, upper), jnp.logical_and(ahead < 0, lower))
        band[depth + ahead] = jnp.where(there, value, 0.0)

    band[depth] = own[0]
    put(cross, own[1])
    put(2 * sign, kept[0] + from_y[0])
    put(2 * sign + cross, from_mate[0] + from_y[1])
    put(-2 * sign, from_y[2] + from_f[2])
    put(-2 * sign + cross, passed[0] + from_f[3])
    put(4 * sign, kept[1] + from_g[0])
    put(-4 * sign, kept[2] + from_f[0])
    put(-3 * cross, from_mate[1] + from_f[1] + from_g[1])


def finish(aux, me, pairs, summed, own, *partials):
    depth, width = pairs.shape[1], own.shape[-1]
    return pl.pallas_call(
        functools.partial(band_kernel, aux),
        out_shape=squares(2 * depth + 1, width),
        in_specs=smem(3) + vmem(1 + len(partials)),
        out_specs=vmem(1)[0],
        compiler_params=pltpu.CompilerParams(vmem_limit_bytes=LIMIT),
        cost_estimate=cost(own, *partials),
    )(me, pairs, summed, own, *partials)


def add_kernel(*refs):
    refs[-1][...] = sum(share[...] for share in refs[:-1])


def added(shares):
    return pl.pallas_call(
        add_kernel,
        out_shape=jax.ShapeDtypeStruct(shares[0].shape, F32),
        in_specs=vmem(len(shares)),
        out_specs=vmem(1)[0],
        cost_estimate=cost(*shares),
    )(*shares)


def shares_of(values, count, step, ways):
    every = [values]
    for way in range(1, ways):
        every.append(lax.ppermute(values, "basis", [(i, i ^ (step * way)) for i in range(count)]))
    return every


def per_device(factors, coefs, domains, pairs):
    own = factors[0]
    _, aux, _ = own.shape
    count = lax.axis_size("basis")
    me = lax.axis_index("basis").astype(jnp.int32).reshape(1)

    swap = chip_route(count, lambda c: c, swap=True)
    across = chip_route(count, lambda c: c ^ 1)
    f_route = chip_route(count, lambda c: c - 2 if c % 2 == 0 else c + 2)
    g_route = chip_route(count, lambda c: c + 2 if c % 2 == 0 else c - 2)
    f_back, g_back = [(b, a) for a, b in f_route], [(b, a) for a, b in g_route]
    send = lambda value, route: lax.ppermute(value, "basis", route)

    side_part, main_part = cut(me, own)
    y = send(side_part, across)
    f = send(main_part, f_route)
    g = send(side_part, g_route)
    other = send(own, swap)
    own_pairs, share, *tables = own_products(me, domains, pairs, own, other, coefs[0])
    y_low, y_high, share = relay(y, shares_of(share, count, 1, 4))
    step = 4
    shares = [share]
    while step < count:
        if len(shares) > 1:
            shares = [added(shares)]
        ways = 4 if 4 * step <= count else 2
        shares = shares_of(shares[0], count, step, ways)
        step *= ways
    blocks = (main_part, other, y, send(y_low, swap), send(y_high, swap), f, g, side_part)
    kept, to_y, to_f, to_g, to_mate, coulomb_half, summed = shared_products(me, tables, blocks, shares)
    from_y = send(to_y, across)
    from_mate = send(to_mate, swap)
    from_f, from_g = send(to_f, f_back), send(to_g, g_back)
    passed = send(from_y[3:], swap)
    band = finish(aux, me, pairs, summed, own_pairs, kept, from_y, from_f, from_g, from_mate, passed)
    return (band[None], coulomb_half)


def solution(mesh):
    placed = (
        P(("groups", "basis"), None, None, None),
        P(("groups", "basis"), None, None),
        P("groups", None),
        P(("groups", "basis"), None),
    )
    return jax.shard_map(
        per_device,
        mesh=mesh,
        in_specs=placed,
        out_specs=(P(("groups", "basis"), None, None, None), P(("groups", "basis"), None, None)),
        check_vma=False,
    )
```

```python
import functools

import jax
import jax.numpy as jnp
from jax import lax
from jax.experimental import pallas as pl
from jax.experimental.pallas import tpu as pltpu
from jax.sharding import PartitionSpec as P

F32 = jnp.float32
BF16 = jnp.bfloat16

XJ, XO, XJ_SIDE, XO_SIDE, YJ, YO, YO_HIGH, FJ, GJ = range(9)
XY, XYO, XF, YF, YOF, CROSS_F, XG, CROSS_G, OWN = range(9)
PRODUCTS = (
    (XJ, YJ), (XO, YJ), (XJ, FJ), (YJ, FJ), (YO, FJ), (XO, FJ), (XJ_SIDE, GJ), (XO_SIDE, GJ), (XJ, XO)
)
SHARED = (XF, CROSS_F, YF, YOF, XG, CROSS_G, XY, XYO)
STACK, OWN_STACK = 9, 4
LIMIT = 12 * 2**20


def cost(*arrays):
    return pl.CostEstimate(flops=1, bytes_accessed=sum(a.size * a.dtype.itemsize for a in arrays), transcendentals=0)


def smem(n):
    return [pl.BlockSpec(memory_space=pltpu.SMEM)] * n


def vmem(n):
    return [pl.BlockSpec(memory_space=pltpu.VMEM)] * n


def squares(n, width):
    return jax.ShapeDtypeStruct((n, width, width), F32)


def multiply(left, right):
    return lax.dot_general(left, right, (((0,), (0,)), ((), ())), preferred_element_type=F32)


def chip_route(count, target, swap=False):
    chips = count // 2
    route = []
    for chip in range(chips):
        to = target(chip)
        if 0 <= to < chips:
            for core in range(2):
                route.append((2 * chip + core, 2 * to + (1 - core if swap else core)))
    return route


def place_of_device():
    me = lax.axis_index("basis")
    core, chip = me & 1, me >> 1
    odd = chip & 1
    return me, core, chip, odd, core == odd, chip + 2 - 4 * odd, chip - 2 + 4 * odd, odd == ((chip >> 1) & 1)


def cut_kernel(size, own, side, main, near, far, sems):
    _, _, _, odd, _, _, _, f_near = place_of_device()
    side_start, main_start = (1 - odd) * size, odd * size
    near_start, far_start = jnp.where(f_near, side_start, main_start), jnp.where(f_near, main_start, side_start)
    copies = []
    for i, (out, start) in enumerate(
        ((side, side_start), (near, near_start), (far, far_start), (main, main_start))
    ):
        rows = pl.ds(pl.multiple_of(start, 16), size)
        copies.append(pltpu.make_async_copy(own.at[:, rows, :], out, sems.at[i]))
    for copy in copies:
        copy.start()
    for copy in copies:
        copy.wait()


def cut(own):
    rows, aux, width = own.shape
    part = jax.ShapeDtypeStruct((rows, aux // 2, width), own.dtype)
    return pl.pallas_call(
        functools.partial(cut_kernel, aux // 2),
        out_shape=[part] * 4,
        in_specs=vmem(1),
        out_specs=vmem(4),
        scratch_shapes=[pltpu.SemaphoreType.DMA((4,))],
        compiler_params=pltpu.CompilerParams(vmem_limit_bytes=LIMIT),
        cost_estimate=cost(own, own),
    )(own)


def find_matches(domains, number, mine, theirs, spot):
    count, rows = domains.shape
    width = mine.shape[1]
    _, core, chip, _, flag, f_chip, g_chip, _ = place_of_device()
    mine_first, other_first = (chip, core), (chip, 1 - core)
    block = {XJ: mine_first, XJ_SIDE: mine_first, XO: other_first, XO_SIDE: other_first}
    block |= {YJ: (chip ^ 1, core), YO: (chip ^ 1, 1 - core), FJ: (f_chip, core), GJ: (g_chip, core)}

    for q, (left, right) in enumerate(PRODUCTS):
        there, ids = [], []
        for name in (left, right):
            at, one = block[name]
            there.append(jnp.logical_and(at >= 0, 2 * at < count))
            ids.append(2 * jnp.clip(at, 0, count // 2 - 1) + one)
        both = jnp.logical_and(*there)
        if q in (CROSS_F, CROSS_G):
            both = jnp.logical_and(both, flag if q == CROSS_F else jnp.logical_not(flag))
        base = 2 * ids[1]

        def clear(i, carry):
            spot[i] = -1
            return carry

        def fill(row, carry):
            spot[domains[ids[1], row] - base] = row
            return carry

        def clean(slot, carry):
            mine[q, slot] = 0
            theirs[q, slot] = 0
            return carry

        def scan(row, found):
            away = domains[ids[0], row] - base
            inside = jnp.logical_and(away >= 0, away < 2 * rows)
            other_row = spot[jnp.clip(away, 0, 2 * rows - 1)]
            hit = jnp.logical_and(jnp.logical_and(inside, both), other_row >= 0)
            mine[q, found] = row
            theirs[q, found] = jnp.maximum(other_row, 0)
            return found + hit.astype(jnp.int32)

        lax.fori_loop(0, 2 * rows, clear, 0, unroll=10)
        lax.fori_loop(0, rows, fill, 0, unroll=10)
        lax.fori_loop(0, width, clean, 0, unroll=9)
        number[q] = lax.fori_loop(0, rows, scan, 0, unroll=5)


def own_kernel(domains, pairs, own, other, own_side, other_side, coef, out, share, number, mine, theirs, spot):
    rows, half, width = own.shape
    me, _, _, odd, _, _, _, _ = place_of_device()
    find_matches(domains, number, mine, theirs, spot)
    out[...] = jnp.zeros_like(out)
    size = max(n for n in range(1, 11) if rows % n == 0)

    def square(step, carry):
        for part in (own, own_side):
            left = part[pl.ds(size * step, size)].reshape(size * half, width)
            out[0] += multiply(left, left)
        return carry

    lax.fori_loop(0, rows // size, square, 0)

    def beside(step, carry):
        lefts, rights = [], []
        for i in range(OWN_STACK):
            slot = OWN_STACK * step + i
            for part, other_part in ((own, other), (own_side, other_side)):
                left = part[mine[OWN, slot]]
                lefts.append(jnp.where(slot < number[OWN], left, jnp.zeros_like(left)))
                rights.append(other_part[theirs[OWN, slot]])
        out[1] += multiply(jnp.concatenate(lefts, axis=0), jnp.concatenate(rights, axis=0))
        return carry

    lax.fori_loop(0, (number[OWN] + OWN_STACK - 1) // OWN_STACK, beside, 0)

    tile = 128
    parts = []
    for part in (own, own_side):
        sums = []
        for start in range(0, half, tile):
            total = jnp.zeros((tile, width), F32)
            for row in range(rows):
                total += part[row, start:start + tile, :].astype(F32) * coef[row:row + 1, :].astype(F32)
            sums.append(jnp.sum(total.T, axis=0, keepdims=True))
        parts.append(jnp.concatenate(sums, axis=1))
    share[:, :half] = jnp.where(odd == 1, parts[1], parts[0])
    share[:, half:2 * half] = jnp.where(odd == 1, parts[0], parts[1])
    depth = pairs.shape[1]
    lane = lax.broadcasted_iota(jnp.int32, (1, share.shape[1] - 2 * half), 1)
    marks = jnp.zeros(lane.shape, F32)
    for r in range(depth):
        marks = jnp.where(lane == me * depth + r, pairs[0, r].astype(F32), marks)
    share[:, 2 * half:] = marks


def own_products(domains, pairs, own, other, own_side, other_side, coef):
    rows, half, width = own.shape
    count = domains.shape[0]
    marks = -(-count * pairs.shape[1] // 128) * 128
    most = max(-(-rows // n) * n for n in (STACK, OWN_STACK))
    table = jax.ShapeDtypeStruct((len(PRODUCTS), most), jnp.int32)
    return pl.pallas_call(
        own_kernel,
        out_shape=[
            squares(2, width),
            jax.ShapeDtypeStruct((1, 2 * half + marks), F32),
            jax.ShapeDtypeStruct((len(PRODUCTS),), jnp.int32),
            table,
            table,
        ],
        in_specs=smem(2) + vmem(5),
        out_specs=vmem(2) + smem(3),
        scratch_shapes=[pltpu.SMEM((2 * rows,), jnp.int32)],
        compiler_params=pltpu.CompilerParams(vmem_limit_bytes=LIMIT),
        cost_estimate=cost(own, other, own_side, other_side),
    )(domains, pairs, own, other, own_side, other_side, coef)


def relay_kernel(value, token, low, high, sems):
    size = low.shape[1]
    copies = [
        pltpu.make_async_copy(value.at[:, :size, :], low, sems.at[0]),
        pltpu.make_async_copy(value.at[:, size:, :], high, sems.at[1]),
    ]
    for copy in copies:
        copy.start()
    for copy in copies:
        copy.wait()


def relay(value, token):
    rows, size, width = value.shape
    part = jax.ShapeDtypeStruct((rows, size // 2, width), value.dtype)
    return pl.pallas_call(
        relay_kernel,
        out_shape=[part, part],
        in_specs=vmem(2),
        out_specs=vmem(2),
        scratch_shapes=[pltpu.SemaphoreType.DMA((2,))],
        compiler_params=pltpu.CompilerParams(vmem_limit_bytes=LIMIT),
        cost_estimate=cost(value, value),
    )(value, token)


def add_products(listed, tables, block, total):
    number, mine, theirs = tables

    def add(at, q, group):
        lefts, rights = [], []
        left_block, right_block = PRODUCTS[q]
        for i in range(STACK):
            slot = group * STACK + i
            row, other_row = mine[q, slot], theirs[q, slot]
            left = block[left_block][row]
            if left_block == YO:
                left = jnp.concatenate([left, block[YO_HIGH][row]], axis=0)
            lefts.append(jnp.where(slot < number[q], left, jnp.zeros_like(left)))
            rights.append(block[right_block][other_row])
        total[at] += multiply(jnp.concatenate(lefts, axis=0), jnp.concatenate(rights, axis=0))

    most = number[listed[0]]
    for q in listed:
        most = jnp.maximum(most, number[q])

    def step(group, carry):
        for at, q in enumerate(listed):
            add(at, q, group)
        return carry

    lax.fori_loop(0, (most + STACK - 1) // STACK, step, 0)


def shared_kernel(number, mine, theirs, xj, xo, xj_side, xo_side, yj, yo, yo_high, near, far, total):
    f_near = place_of_device()[-1]
    total[...] = jnp.zeros_like(total)

    def all_products(fj, gj):
        block = {XJ: xj, XO: xo, XJ_SIDE: xj_side, XO_SIDE: xo_side, YJ: yj, YO: yo, YO_HIGH: yo_high}
        block |= {FJ: fj, GJ: gj}
        add_products(SHARED, (number, mine, theirs), block, total)

    @pl.when(f_near)
    def _():
        all_products(near, far)

    @pl.when(jnp.logical_not(f_near))
    def _():
        all_products(far, near)


def shared_products(tables, *blocks):
    return pl.pallas_call(
        shared_kernel,
        out_shape=squares(len(SHARED), blocks[0].shape[-1]),
        in_specs=smem(len(tables)) + vmem(len(blocks)),
        out_specs=vmem(1)[0],
        compiler_params=pltpu.CompilerParams(vmem_limit_bytes=2 * LIMIT),
        cost_estimate=cost(*blocks),
    )(*tables, *blocks)


def message_kernel(total, *refs):
    shares, (to_near, to_far, to_mate, to_y, summed) = refs[:-5], refs[-5:]
    f_near = place_of_device()[-1]
    width = total.shape[1]

    def to_f_and_g(to_f, to_g):
        for i in range(4):
            to_f[i] = total[i].T
        for i in range(2):
            to_g[i] = total[4 + i].T
            to_g[2 + i] = jnp.zeros_like(total[i])

    @pl.when(f_near)
    def _():
        to_f_and_g(to_near, to_far)

    @pl.when(jnp.logical_not(f_near))
    def _():
        to_f_and_g(to_far, to_near)

    to_mate[0] = total[7]
    to_mate[1] = total[1] + total[5]
    for i, value in enumerate((total[6].T, total[7].T, total[2], total[3])):
        to_y[i * width:(i + 1) * width, :] = value
    gathered = sum(share[...] for share in shares)
    summed[...] = gathered
    to_y[4 * width:, :] = jnp.zeros((to_y.shape[0] - 4 * width, width), F32)
    for i in range(gathered.shape[1] // width):
        to_y[4 * width + i:4 * width + i + 1, :] = gathered[:, i * width:(i + 1) * width]


def messages(total, shares):
    width = total.shape[-1]
    lines = -(-shares[0].shape[1] // width // 8) * 8
    flat = jax.ShapeDtypeStruct
    return pl.pallas_call(
        message_kernel,
        out_shape=[squares(n, width) for n in (4, 4, 2)]
        + [flat((4 * width + lines, width), F32), flat(shares[0].shape, F32)],
        in_specs=vmem(1 + len(shares)),
        out_specs=vmem(5),
        compiler_params=pltpu.CompilerParams(vmem_limit_bytes=LIMIT),
        cost_estimate=cost(total, total),
    )(total, *shares)


def coulomb_kernel(own, own_side, share, from_y, out, summed, passed):
    rows, half, width = own.shape
    odd = place_of_device()[3]
    lines = [from_y[4 * width + i:4 * width + i + 1, :] for i in range(share.shape[1] // width)]
    gathered = share[...] + jnp.concatenate(lines, axis=1)
    summed[...] = gathered
    passed[0] = from_y[3 * width:4 * width, :]
    low, high = gathered[:, :half], gathered[:, half:2 * half]
    gamma = jnp.where(odd == 1, high, low).astype(BF16)
    side_gamma = jnp.where(odd == 1, low, high).astype(BF16)
    for row in range(rows):
        part = jnp.dot(gamma, own[row], preferred_element_type=F32)
        out[row] = part + jnp.dot(side_gamma, own_side[row], preferred_element_type=F32)


def coulomb(own, own_side, share, from_y):
    rows, _, width = own.shape
    flat = jax.ShapeDtypeStruct
    out, summed, passed = pl.pallas_call(
        coulomb_kernel,
        out_shape=[flat((rows, 1, width), F32), flat(share.shape, F32), squares(1, width)],
        in_specs=vmem(4),
        out_specs=vmem(3),
        compiler_params=pltpu.CompilerParams(vmem_limit_bytes=LIMIT),
        cost_estimate=cost(own, own_side),
    )(own, own_side, share, from_y)
    return jnp.swapaxes(out, 0, 1), summed, passed


def band_kernel(aux, pairs, summed, own, total, from_y, from_near, from_far, from_mate, passed, band):
    depth, width = pairs.shape[1], band.shape[1]
    me, core, _, odd, _, _, _, f_near = place_of_device()
    sign, cross = 1 - 2 * odd, 1 - 2 * core

    def put(ahead, value):
        far = jnp.abs(ahead)
        lower = summed[0, aux + jnp.maximum(me - far, 0) * depth + far - 1] > 0.5
        upper = pairs[0, far - 1] == 1
        there = jnp.logical_or(jnp.logical_and(ahead > 0, upper), jnp.logical_and(ahead < 0, lower))
        band[depth + ahead] = jnp.where(there, value, 0.0)

    from_f = lambda i: jnp.where(f_near, from_far[i], from_near[i])
    from_g = lambda i: jnp.where(f_near, from_near[i], from_far[i])
    band[depth] = own[0]
    put(cross, own[1])
    put(2 * sign, total[6] + from_y[0 * width:0 * width + width, :])
    put(2 * sign + cross, from_mate[0] + from_y[1 * width:1 * width + width, :])
    put(-2 * sign, from_y[2 * width:2 * width + width, :] + from_f(2))
    put(-2 * sign + cross, passed[0] + from_f(3))
    put(4 * sign, total[0] + from_g(0))
    put(-4 * sign, total[4] + from_f(0))
    put(-3 * cross, from_mate[1] + from_f(1) + from_g(1))


def finish(aux, pairs, summed, own, *partials):
    depth, width = pairs.shape[1], own.shape[-1]
    return pl.pallas_call(
        functools.partial(band_kernel, aux),
        out_shape=squares(2 * depth + 1, width),
        in_specs=smem(2) + vmem(1 + len(partials)),
        out_specs=vmem(1)[0],
        compiler_params=pltpu.CompilerParams(vmem_limit_bytes=LIMIT),
        cost_estimate=cost(own, *partials),
    )(pairs, summed, own, *partials)


def add_kernel(*refs):
    refs[-1][...] = sum(share[...] for share in refs[:-1])


def added(shares):
    return pl.pallas_call(
        add_kernel,
        out_shape=jax.ShapeDtypeStruct(shares[0].shape, F32),
        in_specs=vmem(len(shares)),
        out_specs=vmem(1)[0],
        compiler_params=pltpu.CompilerParams(vmem_limit_bytes=LIMIT),
        cost_estimate=cost(*shares),
    )(*shares)


def shares_of(values, count, step, ways=2):
    every = [values]
    for way in range(1, ways):
        every.append(lax.ppermute(values, "basis", [(i, i ^ (step * way)) for i in range(count)]))
    return every


def per_device(factors, coefs, domains, pairs):
    own = factors[0]
    _, aux, _ = own.shape
    count = lax.axis_size("basis")

    swap = chip_route(count, lambda c: c, swap=True)
    across = chip_route(count, lambda c: c ^ 1)
    to_near = chip_route(count, lambda c: c ^ 2)
    to_far = chip_route(count, lambda c: c - 2 if c & 2 == 0 else c + 2)
    send = lambda value, route: lax.ppermute(value, "basis", route)

    xj_side, xj, for_near, for_far = cut(own)
    yj = send(xj_side, across)
    near, far = send(for_near, to_near), send(for_far, to_far)
    xo, xo_side = send(xj, swap), send(xj_side, swap)
    own_pairs, share, *tables = own_products(domains, pairs, xj, xo, xj_side, xo_side, coefs[0])
    share = added(shares_of(share, count, 1))
    y_low, y_high = relay(yj, share)
    yo, yo_high = send(y_low, swap), send(y_high, swap)
    shares, step = [share], 4
    while step < count:
        if len(shares) > 1:
            shares = [added(shares)]
        ways = 4 if 4 * step <= count else 2
        shares = shares_of(shares[0], count, step, ways)
        step *= ways
    total = shared_products(tables, xj, xo, xj_side, xo_side, yj, yo, yo_high, near, far)
    for_near, for_far, for_mate, for_y, share = messages(total, shares)
    from_y, from_near, from_far = send(for_y, across), send(for_near, to_near), send(for_far, to_far)
    from_mate = send(for_mate, swap)
    coulomb_half, summed, passed = coulomb(xj, xj_side, share, from_y)
    passed = send(passed, swap)
    band = finish(aux, pairs, summed, own_pairs, total, from_y, from_near, from_far, from_mate, passed)
    return (band[None], coulomb_half)


def solution(mesh):
    placed = (
        P(("groups", "basis"), None, None, None),
        P(("groups", "basis"), None, None),
        P("groups", None),
        P(("groups", "basis"), None),
    )
    return jax.shard_map(
        per_device,
        mesh=mesh,
        in_specs=placed,
        out_specs=(P(("groups", "basis"), None, None, None), P(("groups", "basis"), None, None)),
        check_vma=False,
    )
```

```python
import functools

import jax
import jax.numpy as jnp
from jax import lax
from jax.experimental import pallas as pl
from jax.experimental.pallas import tpu as pltpu
from jax.sharding import PartitionSpec as P

F32 = jnp.float32
BF16 = jnp.bfloat16

XJ, XO, XJ_SIDE, XO_SIDE, YJ, YO, YO_HIGH, FJ, GJ = range(9)
XY, XYO, XF, YF, YOF, CROSS_F, XG, CROSS_G, OWN = range(9)
PRODUCTS = (
    (XJ, YJ), (XO, YJ), (XJ, FJ), (YJ, FJ), (YO, FJ), (XO, FJ), (XJ_SIDE, GJ), (XO_SIDE, GJ), (XJ, XO)
)
SHARED = (XF, CROSS_F, YF, YOF, XG, CROSS_G, XY, XYO)
STACK, OWN_STACK = 20, 4
LIMIT = 12 * 2**20


def cost(*arrays):
    return pl.CostEstimate(flops=1, bytes_accessed=sum(a.size * a.dtype.itemsize for a in arrays), transcendentals=0)


def smem(n):
    return [pl.BlockSpec(memory_space=pltpu.SMEM)] * n


def vmem(n):
    return [pl.BlockSpec(memory_space=pltpu.VMEM)] * n


def squares(n, width):
    return jax.ShapeDtypeStruct((n, width, width), F32)


def multiply(left, right):
    return lax.dot_general(left, right, (((0,), (0,)), ((), ())), preferred_element_type=F32)


def chip_route(count, target, swap=False):
    chips = count // 2
    route = []
    for chip in range(chips):
        to = target(chip)
        if 0 <= to < chips:
            for core in range(2):
                route.append((2 * chip + core, 2 * to + (1 - core if swap else core)))
    return route


def place_of_device():
    me = lax.axis_index("basis")
    core, chip = me & 1, me >> 1
    odd = chip & 1
    return me, core, chip, odd, core == odd, chip + 2 - 4 * odd, chip - 2 + 4 * odd, odd == ((chip >> 1) & 1)


def cut_kernel(size, own, side, main, near, far, sems):
    _, _, _, odd, _, _, _, f_near = place_of_device()
    side_start, main_start = (1 - odd) * size, odd * size
    near_start, far_start = jnp.where(f_near, side_start, main_start), jnp.where(f_near, main_start, side_start)
    copies = []
    for i, (out, start) in enumerate(
        ((side, side_start), (near, near_start), (far, far_start), (main, main_start))
    ):
        rows = pl.ds(pl.multiple_of(start, 16), size)
        copies.append(pltpu.make_async_copy(own.at[:, rows, :], out, sems.at[i]))
    for copy in copies:
        copy.start()
    for copy in copies:
        copy.wait()


def cut(own):
    rows, aux, width = own.shape
    part = jax.ShapeDtypeStruct((rows, aux // 2, width), own.dtype)
    return pl.pallas_call(
        functools.partial(cut_kernel, aux // 2),
        out_shape=[part] * 4,
        in_specs=vmem(1),
        out_specs=vmem(4),
        scratch_shapes=[pltpu.SemaphoreType.DMA((4,))],
        compiler_params=pltpu.CompilerParams(vmem_limit_bytes=LIMIT),
        cost_estimate=cost(own, own),
    )(own)


def find_matches(domains, number, mine, theirs, spot):
    count, rows = domains.shape
    width = mine.shape[1]
    _, core, chip, _, flag, f_chip, g_chip, _ = place_of_device()
    mine_first, other_first = (chip, core), (chip, 1 - core)
    block = {XJ: mine_first, XJ_SIDE: mine_first, XO: other_first, XO_SIDE: other_first}
    block |= {YJ: (chip ^ 1, core), YO: (chip ^ 1, 1 - core), FJ: (f_chip, core), GJ: (g_chip, core)}

    for q, (left, right) in enumerate(PRODUCTS):
        there, ids = [], []
        for name in (left, right):
            at, one = block[name]
            there.append(jnp.logical_and(at >= 0, 2 * at < count))
            ids.append(2 * jnp.clip(at, 0, count // 2 - 1) + one)
        both = jnp.logical_and(*there)
        if q in (CROSS_F, CROSS_G):
            both = jnp.logical_and(both, flag if q == CROSS_F else jnp.logical_not(flag))
        base = 2 * ids[1]

        def clear(i, carry):
            spot[i] = -1
            return carry

        def fill(row, carry):
            spot[domains[ids[1], row] - base] = row
            return carry

        def clean(slot, carry):
            mine[q, slot] = 0
            theirs[q, slot] = 0
            return carry

        def scan(row, found):
            away = domains[ids[0], row] - base
            inside = jnp.logical_and(away >= 0, away < 2 * rows)
            other_row = spot[jnp.clip(away, 0, 2 * rows - 1)]
            hit = jnp.logical_and(jnp.logical_and(inside, both), other_row >= 0)
            mine[q, found] = row
            theirs[q, found] = jnp.maximum(other_row, 0)
            return found + hit.astype(jnp.int32)

        lax.fori_loop(0, 2 * rows, clear, 0, unroll=10)
        lax.fori_loop(0, rows, fill, 0, unroll=10)
        lax.fori_loop(0, width, clean, 0, unroll=9)
        number[q] = lax.fori_loop(0, rows, scan, 0, unroll=5)


def own_kernel(domains, pairs, own, other, own_side, other_side, coef, out, share, number, mine, theirs, spot):
    rows, half, width = own.shape
    me, _, _, odd, _, _, _, _ = place_of_device()
    find_matches(domains, number, mine, theirs, spot)
    out[...] = jnp.zeros_like(out)
    size = max(n for n in range(1, 11) if rows % n == 0)

    def square(step, carry):
        for part in (own, own_side):
            left = part[pl.ds(size * step, size)].reshape(size * half, width)
            out[0] += multiply(left, left)
        return carry

    lax.fori_loop(0, rows // size, square, 0)

    def beside(step, carry):
        lefts, rights = [], []
        for i in range(OWN_STACK):
            slot = OWN_STACK * step + i
            for part, other_part in ((own, other), (own_side, other_side)):
                left = part[mine[OWN, slot]]
                lefts.append(jnp.where(slot < number[OWN], left, jnp.zeros_like(left)))
                rights.append(other_part[theirs[OWN, slot]])
        out[1] += multiply(jnp.concatenate(lefts, axis=0), jnp.concatenate(rights, axis=0))
        return carry

    lax.fori_loop(0, (number[OWN] + OWN_STACK - 1) // OWN_STACK, beside, 0)

    tile = 128
    parts = []
    for part in (own, own_side):
        sums = []
        for start in range(0, half, tile):
            total = jnp.zeros((tile, width), F32)
            for row in range(rows):
                total += part[row, start:start + tile, :].astype(F32) * coef[row:row + 1, :].astype(F32)
            sums.append(jnp.sum(total.T, axis=0, keepdims=True))
        parts.append(jnp.concatenate(sums, axis=1))
    share[:, :half] = jnp.where(odd == 1, parts[1], parts[0])
    share[:, half:2 * half] = jnp.where(odd == 1, parts[0], parts[1])
    depth = pairs.shape[1]
    lane = lax.broadcasted_iota(jnp.int32, (1, share.shape[1] - 2 * half), 1)
    marks = jnp.zeros(lane.shape, F32)
    for r in range(depth):
        marks = jnp.where(lane == me * depth + r, pairs[0, r].astype(F32), marks)
    share[:, 2 * half:] = marks


def own_products(domains, pairs, own, other, own_side, other_side, coef):
    rows, half, width = own.shape
    count = domains.shape[0]
    marks = -(-count * pairs.shape[1] // 128) * 128
    most = max(-(-rows // n) * n for n in (STACK, OWN_STACK))
    table = jax.ShapeDtypeStruct((len(PRODUCTS), most), jnp.int32)
    return pl.pallas_call(
        own_kernel,
        out_shape=[
            squares(2, width),
            jax.ShapeDtypeStruct((1, 2 * half + marks), F32),
            jax.ShapeDtypeStruct((len(PRODUCTS),), jnp.int32),
            table,
            table,
        ],
        in_specs=smem(2) + vmem(5),
        out_specs=vmem(2) + smem(3),
        scratch_shapes=[pltpu.SMEM((2 * rows,), jnp.int32)],
        compiler_params=pltpu.CompilerParams(vmem_limit_bytes=LIMIT),
        cost_estimate=cost(own, other, own_side, other_side),
    )(domains, pairs, own, other, own_side, other_side, coef)


def relay_kernel(value, token, low, high, sems):
    size = low.shape[1]
    copies = [
        pltpu.make_async_copy(value.at[:, :size, :], low, sems.at[0]),
        pltpu.make_async_copy(value.at[:, size:, :], high, sems.at[1]),
    ]
    for copy in copies:
        copy.start()
    for copy in copies:
        copy.wait()


def relay(value, token):
    rows, size, width = value.shape
    part = jax.ShapeDtypeStruct((rows, size // 2, width), value.dtype)
    return pl.pallas_call(
        relay_kernel,
        out_shape=[part, part],
        in_specs=vmem(2),
        out_specs=vmem(2),
        scratch_shapes=[pltpu.SemaphoreType.DMA((2,))],
        compiler_params=pltpu.CompilerParams(vmem_limit_bytes=LIMIT),
        cost_estimate=cost(value, value),
    )(value, token)


def add_products(listed, tables, block, total):
    number, mine, theirs = tables

    def add(at, q, group):
        lefts, rights = [], []
        left_block, right_block = PRODUCTS[q]
        for i in range(STACK):
            slot = group * STACK + i
            row, other_row = mine[q, slot], theirs[q, slot]
            left = block[left_block][row]
            if left_block == YO:
                left = jnp.concatenate([left, block[YO_HIGH][row]], axis=0)
            lefts.append(jnp.where(slot < number[q], left, jnp.zeros_like(left)))
            rights.append(block[right_block][other_row])
        total[at] += multiply(jnp.concatenate(lefts, axis=0), jnp.concatenate(rights, axis=0))

    most = number[listed[0]]
    for q in listed:
        most = jnp.maximum(most, number[q])

    def step(group, carry):
        for at, q in enumerate(listed):
            add(at, q, group)
        return carry

    lax.fori_loop(0, (most + STACK - 1) // STACK, step, 0)


def shared_kernel(number, mine, theirs, xj, xo, xj_side, xo_side, yj, yo, yo_high, near, far, total):
    f_near = place_of_device()[-1]
    total[...] = jnp.zeros_like(total)

    def all_products(fj, gj):
        block = {XJ: xj, XO: xo, XJ_SIDE: xj_side, XO_SIDE: xo_side, YJ: yj, YO: yo, YO_HIGH: yo_high}
        block |= {FJ: fj, GJ: gj}
        add_products(SHARED, (number, mine, theirs), block, total)

    @pl.when(f_near)
    def _():
        all_products(near, far)

    @pl.when(jnp.logical_not(f_near))
    def _():
        all_products(far, near)


def shared_products(tables, *blocks):
    return pl.pallas_call(
        shared_kernel,
        out_shape=squares(len(SHARED), blocks[0].shape[-1]),
        in_specs=smem(len(tables)) + vmem(len(blocks)),
        out_specs=vmem(1)[0],
        compiler_params=pltpu.CompilerParams(vmem_limit_bytes=2 * LIMIT),
        cost_estimate=cost(*blocks),
    )(*tables, *blocks)


def message_kernel(total, *refs):
    shares, (to_near, to_far, to_mate, to_y, summed) = refs[:-5], refs[-5:]
    f_near = place_of_device()[-1]
    width = total.shape[1]

    def to_f_and_g(to_f, to_g):
        for i in range(4):
            to_f[i] = total[i].T.astype(BF16)
        for i in range(2):
            to_g[i] = total[4 + i].T.astype(BF16)
            to_g[2 + i] = jnp.zeros(to_g.shape[1:], BF16)

    @pl.when(f_near)
    def _():
        to_f_and_g(to_near, to_far)

    @pl.when(jnp.logical_not(f_near))
    def _():
        to_f_and_g(to_far, to_near)

    to_mate[0] = total[7]
    to_mate[1] = total[1] + total[5]
    for i, value in enumerate((total[6].T, total[7].T, total[2], total[3])):
        to_y[i * width:(i + 1) * width, :] = value.astype(BF16)
    gathered = sum(share[...] for share in shares)
    summed[...] = gathered
    lines = gathered.shape[1] // width
    rest, rows = gathered, []
    for _ in range(3):
        part = rest.astype(BF16)
        rest = rest - part.astype(F32)
        rows += [part[:, i * width:(i + 1) * width].astype(F32) for i in range(lines)]
    rows.append(jnp.zeros((to_y.shape[0] - 4 * width - 3 * lines, width), F32))
    to_y[4 * width:, :] = jnp.concatenate(rows, axis=0).astype(BF16)


def messages(total, shares):
    width = total.shape[-1]
    lines = -(-3 * shares[0].shape[1] // width // 16) * 16
    flat = jax.ShapeDtypeStruct
    return pl.pallas_call(
        message_kernel,
        out_shape=[flat((4, width, width), BF16)] * 2
        + [squares(2, width), flat((4 * width + lines, width), BF16), flat(shares[0].shape, F32)],
        in_specs=vmem(1 + len(shares)),
        out_specs=vmem(5),
        compiler_params=pltpu.CompilerParams(vmem_limit_bytes=LIMIT),
        cost_estimate=cost(total, total),
    )(total, *shares)


def coulomb_kernel(own, own_side, share, from_y, out, summed):
    rows, half, width = own.shape
    odd = place_of_device()[3]
    lines = share.shape[1] // width
    parts = from_y[4 * width:, :].astype(F32)
    line = lambda i: jnp.concatenate([parts[i * lines + j:i * lines + j + 1] for j in range(lines)], axis=1)
    gathered = share[...] + (line(0) + line(1) + line(2))
    summed[...] = gathered
    low, high = gathered[:, :half], gathered[:, half:2 * half]
    gamma = jnp.where(odd == 1, high, low).astype(BF16)
    side_gamma = jnp.where(odd == 1, low, high).astype(BF16)
    for row in range(rows):
        part = jnp.dot(gamma, own[row], preferred_element_type=F32)
        out[row] = part + jnp.dot(side_gamma, own_side[row], preferred_element_type=F32)


def coulomb(own, own_side, share, from_y):
    rows, _, width = own.shape
    flat = jax.ShapeDtypeStruct
    out, summed = pl.pallas_call(
        coulomb_kernel,
        out_shape=[flat((rows, 1, width), F32), flat(share.shape, F32)],
        in_specs=vmem(4),
        out_specs=vmem(2),
        compiler_params=pltpu.CompilerParams(vmem_limit_bytes=LIMIT),
        cost_estimate=cost(own, own_side),
    )(own, own_side, share, from_y)
    return jnp.swapaxes(out, 0, 1), summed


def band_kernel(aux, pairs, summed, own, total, from_y, from_near, from_far, from_mate, passed, band):
    depth, width = pairs.shape[1], band.shape[1]
    me, core, _, odd, _, _, _, f_near = place_of_device()
    count = lax.axis_size("basis")
    sign, cross = 1 - 2 * odd, 1 - 2 * core

    def put(ahead, value):
        far = jnp.abs(ahead)
        lower = summed[0, aux + jnp.maximum(me - far, 0) * depth + far - 1] > 0.5
        upper = pairs[0, far - 1] == 1
        there = jnp.logical_or(jnp.logical_and(ahead > 0, upper), jnp.logical_and(ahead < 0, lower))
        there = jnp.logical_and(there, jnp.logical_and(me + ahead >= 0, me + ahead < count))
        band[depth + ahead] = jnp.where(there, value, 0.0)

    from_f = lambda i: jnp.where(f_near, from_far[i].astype(F32), from_near[i].astype(F32))
    from_g = lambda i: jnp.where(f_near, from_near[i].astype(F32), from_far[i].astype(F32))
    y_block = lambda i: from_y[i * width:(i + 1) * width, :].astype(F32)
    band[depth] = own[0]
    put(cross, own[1])
    put(2 * sign, total[6] + y_block(0))
    put(2 * sign + cross, from_mate[0] + y_block(1))
    put(-2 * sign, y_block(2) + from_f(2))
    put(-2 * sign + cross, passed[...].astype(F32) + from_f(3))
    put(4 * sign, total[0] + from_g(0))
    put(-4 * sign, total[4] + from_f(0))
    put(-3 * cross, from_mate[1] + from_f(1) + from_g(1))


def finish(aux, pairs, summed, own, *partials):
    depth, width = pairs.shape[1], own.shape[-1]
    return pl.pallas_call(
        functools.partial(band_kernel, aux),
        out_shape=squares(2 * depth + 1, width),
        in_specs=smem(2) + vmem(1 + len(partials)),
        out_specs=vmem(1)[0],
        compiler_params=pltpu.CompilerParams(vmem_limit_bytes=LIMIT),
        cost_estimate=cost(own, *partials),
    )(pairs, summed, own, *partials)


def add_kernel(*refs):
    refs[-1][...] = sum(share[...] for share in refs[:-1])


def added(shares):
    return pl.pallas_call(
        add_kernel,
        out_shape=jax.ShapeDtypeStruct(shares[0].shape, F32),
        in_specs=vmem(len(shares)),
        out_specs=vmem(1)[0],
        compiler_params=pltpu.CompilerParams(vmem_limit_bytes=LIMIT),
        cost_estimate=cost(*shares),
    )(*shares)


def shares_of(values, count, step, ways=2):
    every = [values]
    for way in range(1, ways):
        every.append(lax.ppermute(values, "basis", [(i, i ^ (step * way)) for i in range(count)]))
    return every


def per_device(factors, coefs, domains, pairs):
    own = factors[0]
    _, aux, _ = own.shape
    count = lax.axis_size("basis")

    swap = chip_route(count, lambda c: c, swap=True)
    across = chip_route(count, lambda c: c ^ 1)
    to_near = chip_route(count, lambda c: c ^ 2)
    to_far = chip_route(count, lambda c: c - 2 if c & 2 == 0 else c + 2)
    senders = {source for source, _ in to_far}
    to_far += [(i, i ^ 1) for i in range(count) if i not in senders]
    send = lambda value, route: lax.ppermute(value, "basis", route)

    xj_side, xj, for_near, for_far = cut(own)
    yj = send(xj_side, across)
    near, far = send(for_near, to_near), send(for_far, to_far)
    xo, xo_side = send(xj, swap), send(xj_side, swap)
    own_pairs, share, *tables = own_products(domains, pairs, xj, xo, xj_side, xo_side, coefs[0])
    share = added(shares_of(share, count, 1))
    y_low, y_high = relay(yj, share)
    yo, yo_high = send(y_low, swap), send(y_high, swap)
    shares, step = [share], 4
    while step < count:
        if len(shares) > 1:
            shares = [added(shares)]
        ways = 4 if 4 * step <= count else 2
        shares = shares_of(shares[0], count, step, ways)
        step *= ways
    total = shared_products(tables, xj, xo, xj_side, xo_side, yj, yo, yo_high, near, far)
    for_near, for_far, for_mate, for_y, share = messages(total, shares)
    from_y, from_near, from_far = send(for_y, across), send(for_near, to_near), send(for_far, to_far)
    from_mate = send(for_mate, swap)
    width = own.shape[2]
    passed = send(from_y[3 * width:4 * width], swap)
    coulomb_half, summed = coulomb(xj, xj_side, share, from_y)
    band = finish(aux, pairs, summed, own_pairs, total, from_y, from_near, from_far, from_mate, passed)
    return (band[None], coulomb_half)


def solution(mesh):
    placed = (
        P(("groups", "basis"), None, None, None),
        P(("groups", "basis"), None, None),
        P("groups", None),
        P(("groups", "basis"), None),
    )
    return jax.shard_map(
        per_device,
        mesh=mesh,
        in_specs=placed,
        out_specs=(P(("groups", "basis"), None, None, None), P(("groups", "basis"), None, None)),
        check_vma=False,
    )
```

```python
import functools

import jax
import jax.numpy as jnp
from jax import lax
from jax.experimental import pallas as pl
from jax.experimental.pallas import tpu as pltpu
from jax.sharding import PartitionSpec as P

F32 = jnp.float32
BF16 = jnp.bfloat16

XJ, XO, XJ_SIDE, YJ, YO, YO_HIGH, FJ, GJ = range(8)
XF, YF, YOF, XG, XY, XYO, CROSS, OWN = range(8)
PRODUCTS = ((XJ, FJ), (YJ, FJ), (YO, FJ), (XJ_SIDE, GJ), (XJ, YJ), (XO, YJ), (XO, None), (XJ, XO))
SHARED = (XF, YF, YOF, XG, XY, XYO, CROSS)
STACK, OWN_STACK = 10, 4
LIMIT = 12 * 2**20


def cost(*arrays):
    return pl.CostEstimate(flops=1, bytes_accessed=sum(a.size * a.dtype.itemsize for a in arrays), transcendentals=0)


def smem(n):
    return [pl.BlockSpec(memory_space=pltpu.SMEM)] * n


def vmem(n):
    return [pl.BlockSpec(memory_space=pltpu.VMEM)] * n


def squares(n, width):
    return jax.ShapeDtypeStruct((n, width, width), F32)


def multiply(left, right):
    return lax.dot_general(left, right, (((0,), (0,)), ((), ())), preferred_element_type=F32)


def chip_route(count, target, swap=False):
    chips = count // 2
    route = []
    for chip in range(chips):
        to = target(chip)
        if 0 <= to < chips:
            for core in range(2):
                route.append((2 * chip + core, 2 * to + (1 - core if swap else core)))
    return route


def place_of_device():
    me = lax.axis_index("basis")
    core, chip = me & 1, me >> 1
    odd = chip & 1
    return me, core, chip, odd, core == odd, chip + 2 - 4 * odd, chip - 2 + 4 * odd, odd == ((chip >> 1) & 1)


def cut_kernel(size, own, side, main, near, far, sems):
    _, _, _, odd, _, _, _, f_near = place_of_device()
    side_start, main_start = (1 - odd) * size, odd * size
    near_start, far_start = jnp.where(f_near, side_start, main_start), jnp.where(f_near, main_start, side_start)
    copies = []
    for i, (out, start) in enumerate(
        ((side, side_start), (near, near_start), (far, far_start), (main, main_start))
    ):
        rows = pl.ds(pl.multiple_of(start, 16), size)
        copies.append(pltpu.make_async_copy(own.at[:, rows, :], out, sems.at[i]))
    for copy in copies:
        copy.start()
    for copy in copies:
        copy.wait()


def cut(own):
    rows, aux, width = own.shape
    part = jax.ShapeDtypeStruct((rows, aux // 2, width), own.dtype)
    return pl.pallas_call(
        functools.partial(cut_kernel, aux // 2),
        out_shape=[part] * 4,
        in_specs=vmem(1),
        out_specs=vmem(4),
        scratch_shapes=[pltpu.SemaphoreType.DMA((4,))],
        compiler_params=pltpu.CompilerParams(vmem_limit_bytes=LIMIT),
        cost_estimate=cost(own, own),
    )(own)


def find_matches(domains, number, mine, theirs, spot):
    count, rows = domains.shape
    width = mine.shape[1]
    _, core, chip, _, flag, f_chip, g_chip, _ = place_of_device()
    mine_first, other_first = (chip, core), (chip, 1 - core)
    block = {XJ: mine_first, XJ_SIDE: mine_first, XO: other_first, None: (jnp.where(flag, f_chip, g_chip), core)}
    block |= {YJ: (chip ^ 1, core), YO: (chip ^ 1, 1 - core), FJ: (f_chip, core), GJ: (g_chip, core)}

    for q, (left, right) in enumerate(PRODUCTS):
        there, ids = [], []
        for name in (left, right):
            at, one = block[name]
            there.append(jnp.logical_and(at >= 0, 2 * at < count))
            ids.append(2 * jnp.clip(at, 0, count // 2 - 1) + one)
        both = jnp.logical_and(*there)
        base = 2 * ids[1]

        def clear(i, carry):
            spot[i] = -1
            return carry

        def fill(row, carry):
            spot[domains[ids[1], row] - base] = row
            return carry

        def clean(slot, carry):
            mine[q, slot] = 0
            theirs[q, slot] = 0
            return carry

        def scan(row, found):
            away = domains[ids[0], row] - base
            inside = jnp.logical_and(away >= 0, away < 2 * rows)
            other_row = spot[jnp.clip(away, 0, 2 * rows - 1)]
            hit = jnp.logical_and(jnp.logical_and(inside, both), other_row >= 0)
            mine[q, found] = row
            theirs[q, found] = jnp.maximum(other_row, 0)
            return found + hit.astype(jnp.int32)

        lax.fori_loop(0, 2 * rows, clear, 0, unroll=10)
        lax.fori_loop(0, rows, fill, 0, unroll=10)
        lax.fori_loop(0, width, clean, 0, unroll=9)
        number[q] = lax.fori_loop(0, rows, scan, 0, unroll=5)


def own_kernel(domains, pairs, own, own_side, other, coef, out, share, number, mine, theirs, spot):
    rows, half, width = own.shape
    me, _, _, odd, _, _, _, _ = place_of_device()
    find_matches(domains, number, mine, theirs, spot)
    out[...] = jnp.zeros_like(out)
    size = max(n for n in range(1, 11) if rows % n == 0)

    def square(step, carry):
        for part in (own, own_side):
            left = part[pl.ds(size * step, size)].reshape(size * half, width)
            out[0] += multiply(left, left)
        return carry

    lax.fori_loop(0, rows // size, square, 0)

    def beside(step, carry):
        lefts, rights = [], []
        for i in range(OWN_STACK):
            slot = OWN_STACK * step + i
            for part, start in ((own, odd * half), (own_side, (1 - odd) * half)):
                left = part[mine[OWN, slot]]
                lefts.append(jnp.where(slot < number[OWN], left, jnp.zeros_like(left)))
                rights.append(other[theirs[OWN, slot], pl.ds(pl.multiple_of(start, 16), half), :])
        out[1] += multiply(jnp.concatenate(lefts, axis=0), jnp.concatenate(rights, axis=0))
        return carry

    lax.fori_loop(0, (number[OWN] + OWN_STACK - 1) // OWN_STACK, beside, 0)

    tile = 128
    parts = []
    for part in (own, own_side):
        sums = []
        for start in range(0, half, tile):
            total = jnp.zeros((tile, width), F32)
            for row in range(rows):
                total += part[row, start:start + tile, :].astype(F32) * coef[row:row + 1, :].astype(F32)
            sums.append(jnp.sum(total.T, axis=0, keepdims=True))
        parts.append(jnp.concatenate(sums, axis=1))
    share[:, :half] = jnp.where(odd == 1, parts[1], parts[0])
    share[:, half:2 * half] = jnp.where(odd == 1, parts[0], parts[1])
    depth = pairs.shape[1]
    lane = lax.broadcasted_iota(jnp.int32, (1, share.shape[1] - 2 * half), 1)
    marks = jnp.zeros(lane.shape, F32)
    for r in range(depth):
        marks = jnp.where(lane == me * depth + r, pairs[0, r].astype(F32), marks)
    share[:, 2 * half:] = marks


def own_products(domains, pairs, own, own_side, other, coef):
    rows, half, width = own.shape
    count = domains.shape[0]
    marks = -(-count * pairs.shape[1] // 128) * 128
    most = max(-(-rows // n) * n for n in (STACK, OWN_STACK))
    table = jax.ShapeDtypeStruct((len(PRODUCTS), most), jnp.int32)
    return pl.pallas_call(
        own_kernel,
        out_shape=[
            squares(2, width),
            jax.ShapeDtypeStruct((1, 2 * half + marks), F32),
            jax.ShapeDtypeStruct((len(PRODUCTS),), jnp.int32),
            table,
            table,
        ],
        in_specs=smem(2) + vmem(4),
        out_specs=vmem(2) + smem(3),
        scratch_shapes=[pltpu.SMEM((2 * rows,), jnp.int32)],
        compiler_params=pltpu.CompilerParams(vmem_limit_bytes=LIMIT),
        cost_estimate=cost(own, own_side, other),
    )(domains, pairs, own, own_side, other, coef)


def relay_kernel(value, token, low, high, sems):
    size = low.shape[1]
    copies = [
        pltpu.make_async_copy(value.at[:, :size, :], low, sems.at[0]),
        pltpu.make_async_copy(value.at[:, size:, :], high, sems.at[1]),
    ]
    for copy in copies:
        copy.start()
    for copy in copies:
        copy.wait()


def relay(value, token):
    rows, size, width = value.shape
    part = jax.ShapeDtypeStruct((rows, size // 2, width), value.dtype)
    return pl.pallas_call(
        relay_kernel,
        out_shape=[part, part],
        in_specs=vmem(2),
        out_specs=vmem(2),
        scratch_shapes=[pltpu.SemaphoreType.DMA((2,))],
        compiler_params=pltpu.CompilerParams(vmem_limit_bytes=LIMIT),
        cost_estimate=cost(value, value),
    )(value, token)


def shared_kernel(number, mine, theirs, xj, xj_side, xo, yj, yo, yo_high, near, far, total):
    _, _, _, odd, flag, _, _, f_near = place_of_device()
    half = xj.shape[1]
    main = pl.ds(pl.multiple_of(odd * half, 16), half)
    cross = pl.ds(pl.multiple_of(jnp.where(flag, odd, 1 - odd) * half, 16), half)

    def product(q, group, block):
        lefts, rights = [], []
        left_block, right_block = PRODUCTS[q]
        for i in range(STACK):
            slot = group * STACK + i
            row, other_row = mine[q, slot], theirs[q, slot]
            if left_block == XO:
                left = xo[row, cross if q == CROSS else main, :]
            elif left_block == YO:
                left = jnp.concatenate([yo[row], yo_high[row]], axis=0)
            else:
                left = block[left_block][row]
            lefts.append(jnp.where(slot < number[q], left, jnp.zeros_like(left)))
            if q == CROSS:
                rights.append(jnp.where(flag, block[FJ][other_row], block[GJ][other_row]))
            else:
                rights.append(block[right_block][other_row])
        return multiply(jnp.concatenate(lefts, axis=0), jnp.concatenate(rights, axis=0))

    def all_products(fj, gj):
        block = {XJ: xj, XJ_SIDE: xj_side, YJ: yj, FJ: fj, GJ: gj}
        most = number[SHARED[0]]
        for at, q in enumerate(SHARED):
            most = jnp.maximum(most, number[q])
            total[at] = product(q, 0, block)

        def step(group, carry):
            for at, q in enumerate(SHARED):
                total[at] += product(q, group, block)
            return carry

        lax.fori_loop(1, (most + STACK - 1) // STACK, step, 0)

    @pl.when(f_near)
    def _():
        all_products(near, far)

    @pl.when(jnp.logical_not(f_near))
    def _():
        all_products(far, near)


def shared_products(tables, *blocks):
    return pl.pallas_call(
        shared_kernel,
        out_shape=squares(len(SHARED), blocks[0].shape[-1]),
        in_specs=smem(len(tables)) + vmem(len(blocks)),
        out_specs=vmem(1)[0],
        compiler_params=pltpu.CompilerParams(vmem_limit_bytes=2 * LIMIT),
        cost_estimate=cost(*blocks),
    )(*tables, *blocks)


def message_kernel(total, *refs):
    shares, (to_near, to_far, to_mate, to_y, summed) = refs[:-5], refs[-5:]
    _, _, _, _, flag, _, _, f_near = place_of_device()
    width = total.shape[1]

    def to_f_and_g(to_f, to_g):
        cross = total[CROSS].T
        nothing = jnp.zeros_like(cross)
        from_total = (total[XF].T, jnp.where(flag, cross, nothing), total[YF].T, total[YOF].T)
        for i, value in enumerate(from_total):
            to_f[i] = value.astype(BF16)
        for i, value in enumerate((total[XG].T, jnp.where(flag, nothing, cross), nothing, nothing)):
            to_g[i] = value.astype(BF16)

    @pl.when(f_near)
    def _():
        to_f_and_g(to_near, to_far)

    @pl.when(jnp.logical_not(f_near))
    def _():
        to_f_and_g(to_far, to_near)

    to_mate[0] = total[XYO]
    to_mate[1] = total[CROSS]
    for i, value in enumerate((total[XY].T, total[XYO].T, total[YF], total[YOF])):
        to_y[i * width:(i + 1) * width, :] = value.astype(BF16)
    gathered = sum(share[...] for share in shares)
    summed[...] = gathered
    lines = gathered.shape[1] // width
    rest, rows = gathered, []
    for _ in range(3):
        part = rest.astype(BF16)
        rest = rest - part.astype(F32)
        rows += [part[:, i * width:(i + 1) * width].astype(F32) for i in range(lines)]
    rows.append(jnp.zeros((to_y.shape[0] - 4 * width - 3 * lines, width), F32))
    to_y[4 * width:, :] = jnp.concatenate(rows, axis=0).astype(BF16)


def messages(total, shares):
    width = total.shape[-1]
    lines = -(-3 * shares[0].shape[1] // width // 16) * 16
    flat = jax.ShapeDtypeStruct
    return pl.pallas_call(
        message_kernel,
        out_shape=[flat((4, width, width), BF16)] * 2
        + [squares(2, width), flat((4 * width + lines, width), BF16), flat(shares[0].shape, F32)],
        in_specs=vmem(1 + len(shares)),
        out_specs=vmem(5),
        compiler_params=pltpu.CompilerParams(vmem_limit_bytes=LIMIT),
        cost_estimate=cost(total, total),
    )(total, *shares)


def coulomb_kernel(own, own_side, share, from_y, out, summed):
    rows, half, width = own.shape
    odd = place_of_device()[3]
    lines = share.shape[1] // width
    parts = from_y[4 * width:, :].astype(F32)
    line = lambda i: jnp.concatenate([parts[i * lines + j:i * lines + j + 1] for j in range(lines)], axis=1)
    gathered = share[...] + (line(0) + line(1) + line(2))
    summed[...] = gathered
    low, high = gathered[:, :half], gathered[:, half:2 * half]
    gamma = jnp.where(odd == 1, high, low).astype(BF16)
    side_gamma = jnp.where(odd == 1, low, high).astype(BF16)
    for row in range(rows):
        part = jnp.dot(gamma, own[row], preferred_element_type=F32)
        out[row] = part + jnp.dot(side_gamma, own_side[row], preferred_element_type=F32)


def coulomb(own, own_side, share, from_y):
    rows, _, width = own.shape
    flat = jax.ShapeDtypeStruct
    out, summed = pl.pallas_call(
        coulomb_kernel,
        out_shape=[flat((rows, 1, width), F32), flat(share.shape, F32)],
        in_specs=vmem(4),
        out_specs=vmem(2),
        compiler_params=pltpu.CompilerParams(vmem_limit_bytes=LIMIT),
        cost_estimate=cost(own, own_side),
    )(own, own_side, share, from_y)
    return jnp.swapaxes(out, 0, 1), summed


def band_kernel(aux, pairs, summed, own, total, from_y, from_near, from_far, from_mate, passed, band, made, sems):
    depth, width = pairs.shape[1], band.shape[1]
    me, core, _, odd, _, _, _, f_near = place_of_device()
    count = lax.axis_size("basis")
    sign, cross = 1 - 2 * odd, 1 - 2 * core
    copies = []

    def put(ahead, value):
        far = jnp.abs(ahead)
        slot = len(copies)
        if slot == 0:
            made[slot] = value
        else:
            lower = summed[0, aux + jnp.maximum(me - far, 0) * depth + far - 1] > 0.5
            upper = pairs[0, far - 1] == 1
            there = jnp.logical_or(jnp.logical_and(ahead > 0, upper), jnp.logical_and(ahead < 0, lower))
            there = jnp.logical_and(there, jnp.logical_and(me + ahead >= 0, me + ahead < count))
            made[slot] = jnp.where(there, value, 0.0)
        copies.append(pltpu.make_async_copy(made.at[slot], band.at[depth + ahead], sems.at[slot]))
        copies[-1].start()

    from_f = lambda i: jnp.where(f_near, from_far[i].astype(F32), from_near[i].astype(F32))
    from_g = lambda i: jnp.where(f_near, from_near[i].astype(F32), from_far[i].astype(F32))
    y_block = lambda i: from_y[i * width:(i + 1) * width, :].astype(F32)
    put(0, own[0])
    put(cross, own[1])
    put(2 * sign, total[XY] + y_block(0))
    put(2 * sign + cross, from_mate[0] + y_block(1))
    put(-2 * sign, y_block(2) + from_f(2))
    put(-2 * sign + cross, passed[...].astype(F32) + from_f(3))
    put(4 * sign, total[XF] + from_g(0))
    put(-4 * sign, total[XG] + from_f(0))
    put(-3 * cross, from_mate[1] + from_f(1) + from_g(1))
    for copy in copies:
        copy.wait()


def finish(aux, pairs, summed, own, *partials):
    depth, width = pairs.shape[1], own.shape[-1]
    size = 2 * depth + 1
    return pl.pallas_call(
        functools.partial(band_kernel, aux),
        out_shape=squares(size, width),
        in_specs=smem(2) + vmem(1 + len(partials)),
        out_specs=pl.BlockSpec(memory_space=pl.ANY),
        scratch_shapes=[pltpu.VMEM((size, width, width), F32), pltpu.SemaphoreType.DMA((size,))],
        compiler_params=pltpu.CompilerParams(vmem_limit_bytes=LIMIT),
        cost_estimate=cost(own, *partials),
    )(pairs, summed, own, *partials)


def add_kernel(*refs):
    refs[-1][...] = sum(share[...] for share in refs[:-1])


def added(shares):
    return pl.pallas_call(
        add_kernel,
        out_shape=jax.ShapeDtypeStruct(shares[0].shape, F32),
        in_specs=vmem(len(shares)),
        out_specs=vmem(1)[0],
        compiler_params=pltpu.CompilerParams(vmem_limit_bytes=LIMIT),
        cost_estimate=cost(*shares),
    )(*shares)


def shares_of(values, count, step, ways=2):
    every = [values]
    for way in range(1, ways):
        every.append(lax.ppermute(values, "basis", [(i, i ^ (step * way)) for i in range(count)]))
    return every


def per_device(factors, coefs, domains, pairs):
    own = factors[0]
    _, aux, _ = own.shape
    count = lax.axis_size("basis")

    swap = chip_route(count, lambda c: c, swap=True)
    across = chip_route(count, lambda c: c ^ 1)
    to_near = chip_route(count, lambda c: c ^ 2)
    to_far = chip_route(count, lambda c: c - 2 if c & 2 == 0 else c + 2)
    senders = {source for source, _ in to_far}
    to_far += [(i, i ^ 1) for i in range(count) if i not in senders]
    send = lambda value, route: lax.ppermute(value, "basis", route)

    xo = send(own, swap)
    xj_side, xj, for_near, for_far = cut(own)
    yj = send(xj_side, across)
    near, far = send(for_near, to_near), send(for_far, to_far)
    own_pairs, share, *tables = own_products(domains, pairs, xj, xj_side, xo, coefs[0])
    share = added(shares_of(share, count, 1))
    y_low, y_high = relay(yj, share)
    yo, yo_high = send(y_low, swap), send(y_high, swap)
    shares, step = [share], 4
    while step < count:
        if len(shares) > 1:
            shares = [added(shares)]
        ways = 4 if 4 * step <= count else 2
        shares = shares_of(shares[0], count, step, ways)
        step *= ways
    total = shared_products(tables, xj, xj_side, xo, yj, yo, yo_high, near, far)
    for_near, for_far, for_mate, for_y, share = messages(total, shares)
    from_y, from_near, from_far = send(for_y, across), send(for_near, to_near), send(for_far, to_far)
    from_mate = send(for_mate, swap)
    width = own.shape[2]
    passed = send(from_y[3 * width:4 * width], swap)
    coulomb_half, summed = coulomb(xj, xj_side, share, from_y)
    band = finish(aux, pairs, summed, own_pairs, total, from_y, from_near, from_far, from_mate, passed)
    return (band[None], coulomb_half)


def solution(mesh):
    placed = (
        P(("groups", "basis"), None, None, None),
        P(("groups", "basis"), None, None),
        P("groups", None),
        P(("groups", "basis"), None),
    )
    return jax.shard_map(
        per_device,
        mesh=mesh,
        in_specs=placed,
        out_specs=(P(("groups", "basis"), None, None, None), P(("groups", "basis"), None, None)),
        check_vma=False,
    )
```

```python
import functools

import jax
import jax.numpy as jnp
from jax import lax
from jax.experimental import pallas as pl
from jax.experimental.pallas import tpu as pltpu
from jax.sharding import PartitionSpec as P

F32 = jnp.float32
BF16 = jnp.bfloat16

XJ, XO, XJ_SIDE, YJ, YO, YO_HIGH, FJ, GJ = range(8)
XF, YF, YOF, XG, XY, XYO, CROSS, OWN = range(8)
PRODUCTS = ((XJ, FJ), (YJ, FJ), (YO, FJ), (XJ_SIDE, GJ), (XJ, YJ), (XO, YJ), (XO, None), (XJ, XO))
SHARED = (XF, YF, YOF, XG, XY, XYO, CROSS)
STACK, SHORT_STACK, OWN_STACK = 10, 8, 4
LIMIT = 12 * 2**20


def cost(*arrays):
    return pl.CostEstimate(flops=1, bytes_accessed=sum(a.size * a.dtype.itemsize for a in arrays), transcendentals=0)


def smem(n):
    return [pl.BlockSpec(memory_space=pltpu.SMEM)] * n


def vmem(n):
    return [pl.BlockSpec(memory_space=pltpu.VMEM)] * n


def squares(n, width):
    return jax.ShapeDtypeStruct((n, width, width), F32)


def multiply(left, right):
    return lax.dot_general(left, right, (((0,), (0,)), ((), ())), preferred_element_type=F32)


def chip_route(count, target, swap=False):
    chips = count // 2
    route = []
    for chip in range(chips):
        to = target(chip)
        if 0 <= to < chips:
            for core in range(2):
                route.append((2 * chip + core, 2 * to + (1 - core if swap else core)))
    return route


def place_of_device():
    me = lax.axis_index("basis")
    core, chip = me & 1, me >> 1
    odd = chip & 1
    return me, core, chip, odd, core == odd, chip + 2 - 4 * odd, chip - 2 + 4 * odd, odd == ((chip >> 1) & 1)


def cut_kernel(size, own, side, main, near, far, sems):
    _, _, _, odd, _, _, _, f_near = place_of_device()
    side_start, main_start = (1 - odd) * size, odd * size
    near_start, far_start = jnp.where(f_near, side_start, main_start), jnp.where(f_near, main_start, side_start)
    copies = []
    for i, (out, start) in enumerate(
        ((side, side_start), (near, near_start), (far, far_start), (main, main_start))
    ):
        rows = pl.ds(pl.multiple_of(start, 16), size)
        copies.append(pltpu.make_async_copy(own.at[:, rows, :], out, sems.at[i]))
    for copy in copies:
        copy.start()
    for copy in copies:
        copy.wait()


def cut(own):
    rows, aux, width = own.shape
    part = jax.ShapeDtypeStruct((rows, aux // 2, width), own.dtype)
    return pl.pallas_call(
        functools.partial(cut_kernel, aux // 2),
        out_shape=[part] * 4,
        in_specs=vmem(1),
        out_specs=vmem(4),
        scratch_shapes=[pltpu.SemaphoreType.DMA((4,))],
        compiler_params=pltpu.CompilerParams(vmem_limit_bytes=LIMIT),
        cost_estimate=cost(own, own),
    )(own)


def find_matches(domains, number, mine, theirs, spot):
    count, rows = domains.shape
    width = mine.shape[1]
    _, core, chip, _, flag, f_chip, g_chip, _ = place_of_device()
    mine_first, other_first = (chip, core), (chip, 1 - core)
    block = {XJ: mine_first, XJ_SIDE: mine_first, XO: other_first, None: (jnp.where(flag, f_chip, g_chip), core)}
    block |= {YJ: (chip ^ 1, core), YO: (chip ^ 1, 1 - core), FJ: (f_chip, core), GJ: (g_chip, core)}

    for q, (left, right) in enumerate(PRODUCTS):
        there, ids = [], []
        for name in (left, right):
            at, one = block[name]
            there.append(jnp.logical_and(at >= 0, 2 * at < count))
            ids.append(2 * jnp.clip(at, 0, count // 2 - 1) + one)
        both = jnp.logical_and(*there)
        base = 2 * ids[1]

        def clear(i, carry):
            spot[i] = -1
            return carry

        def fill(row, carry):
            spot[domains[ids[1], row] - base] = row
            return carry

        def clean(slot, carry):
            mine[q, slot] = 0
            theirs[q, slot] = 0
            return carry

        def scan(row, found):
            away = domains[ids[0], row] - base
            inside = jnp.logical_and(away >= 0, away < 2 * rows)
            other_row = spot[jnp.clip(away, 0, 2 * rows - 1)]
            hit = jnp.logical_and(jnp.logical_and(inside, both), other_row >= 0)
            mine[q, found] = row
            theirs[q, found] = jnp.maximum(other_row, 0)
            return found + hit.astype(jnp.int32)

        lax.fori_loop(0, 2 * rows, clear, 0, unroll=10)
        lax.fori_loop(0, rows, fill, 0, unroll=10)
        lax.fori_loop(0, width, clean, 0, unroll=9)
        number[q] = lax.fori_loop(0, rows, scan, 0, unroll=5)


def own_kernel(domains, pairs, own, own_side, other, coef, out, share, number, mine, theirs, spot):
    rows, half, width = own.shape
    me, _, _, odd, _, _, _, _ = place_of_device()
    find_matches(domains, number, mine, theirs, spot)
    out[...] = jnp.zeros_like(out)
    size = max(n for n in range(1, 11) if rows % n == 0)

    def square(step, carry):
        for part in (own, own_side):
            left = part[pl.ds(size * step, size)].reshape(size * half, width)
            out[0] += multiply(left, left)
        return carry

    lax.fori_loop(0, rows // size, square, 0)

    def beside(step, carry):
        lefts, rights = [], []
        for i in range(OWN_STACK):
            slot = OWN_STACK * step + i
            for part, start in ((own, odd * half), (own_side, (1 - odd) * half)):
                left = part[mine[OWN, slot]]
                lefts.append(jnp.where(slot < number[OWN], left, jnp.zeros_like(left)))
                rights.append(other[theirs[OWN, slot], pl.ds(pl.multiple_of(start, 16), half), :])
        out[1] += multiply(jnp.concatenate(lefts, axis=0), jnp.concatenate(rights, axis=0))
        return carry

    lax.fori_loop(0, (number[OWN] + OWN_STACK - 1) // OWN_STACK, beside, 0)

    tile = 128
    parts = []
    for part in (own, own_side):
        sums = []
        for start in range(0, half, tile):
            total = jnp.zeros((tile, width), F32)
            for row in range(rows):
                total += part[row, start:start + tile, :].astype(F32) * coef[row:row + 1, :].astype(F32)
            sums.append(jnp.sum(total.T, axis=0, keepdims=True))
        parts.append(jnp.concatenate(sums, axis=1))
    share[:, :half] = jnp.where(odd == 1, parts[1], parts[0])
    share[:, half:2 * half] = jnp.where(odd == 1, parts[0], parts[1])
    depth = pairs.shape[1]
    lane = lax.broadcasted_iota(jnp.int32, (1, share.shape[1] - 2 * half), 1)
    marks = jnp.zeros(lane.shape, F32)
    for r in range(depth):
        marks = jnp.where(lane == me * depth + r, pairs[0, r].astype(F32), marks)
    share[:, 2 * half:] = marks


def own_products(domains, pairs, own, own_side, other, coef):
    rows, half, width = own.shape
    count = domains.shape[0]
    marks = -(-count * pairs.shape[1] // 128) * 128
    most = max(-(-rows // n) * n for n in (STACK, OWN_STACK))
    table = jax.ShapeDtypeStruct((len(PRODUCTS), most), jnp.int32)
    return pl.pallas_call(
        own_kernel,
        out_shape=[
            squares(2, width),
            jax.ShapeDtypeStruct((1, 2 * half + marks), F32),
            jax.ShapeDtypeStruct((len(PRODUCTS),), jnp.int32),
            table,
            table,
        ],
        in_specs=smem(2) + vmem(4),
        out_specs=vmem(2) + smem(3),
        scratch_shapes=[pltpu.SMEM((2 * rows,), jnp.int32)],
        compiler_params=pltpu.CompilerParams(vmem_limit_bytes=LIMIT),
        cost_estimate=cost(own, own_side, other),
    )(domains, pairs, own, own_side, other, coef)


def relay_kernel(value, *refs):
    shares, (low, high, total, sems) = refs[:-4], refs[-4:]
    size = low.shape[1]
    copies = [
        pltpu.make_async_copy(value.at[:, :size, :], low, sems.at[0]),
        pltpu.make_async_copy(value.at[:, size:, :], high, sems.at[1]),
    ]
    for copy in copies:
        copy.start()
    total[...] = sum(share[...] for share in shares)
    for copy in copies:
        copy.wait()


def relay(value, shares):
    rows, size, width = value.shape
    part = jax.ShapeDtypeStruct((rows, size // 2, width), value.dtype)
    return pl.pallas_call(
        relay_kernel,
        out_shape=[part, part, jax.ShapeDtypeStruct(shares[0].shape, F32)],
        in_specs=vmem(1 + len(shares)),
        out_specs=vmem(3),
        scratch_shapes=[pltpu.SemaphoreType.DMA((2,))],
        compiler_params=pltpu.CompilerParams(vmem_limit_bytes=LIMIT),
        cost_estimate=cost(value, value),
    )(value, *shares)


def shared_kernel(number, mine, theirs, xj, xj_side, xo, yj, yo, yo_high, near, far, total):
    _, _, _, odd, flag, _, _, f_near = place_of_device()
    half = xj.shape[1]
    main = pl.ds(pl.multiple_of(odd * half, 16), half)
    cross = pl.ds(pl.multiple_of(jnp.where(flag, odd, 1 - odd) * half, 16), half)

    def product(q, first, size, block):
        lefts, rights = [], []
        left_block, right_block = PRODUCTS[q]
        for i in range(size):
            slot = first + i
            row, other_row = mine[q, slot], theirs[q, slot]
            if left_block == XO:
                left = xo[row, cross if q == CROSS else main, :]
            elif left_block == YO:
                left = jnp.concatenate([yo[row], yo_high[row]], axis=0)
            else:
                left = block[left_block][row]
            lefts.append(jnp.where(slot < number[q], left, jnp.zeros_like(left)))
            if q == CROSS:
                rights.append(jnp.where(flag, block[FJ][other_row], block[GJ][other_row]))
            else:
                rights.append(block[right_block][other_row])
        return multiply(jnp.concatenate(lefts, axis=0), jnp.concatenate(rights, axis=0))

    def all_products(fj, gj):
        block = {XJ: xj, XJ_SIDE: xj_side, YJ: yj, FJ: fj, GJ: gj}
        most = number[SHARED[0]]
        for at, q in enumerate(SHARED):
            most = jnp.maximum(most, number[q])
            total[at] = product(q, 0, STACK, block)

        def steps(size):
            def step(i, carry):
                for at, q in enumerate(SHARED):
                    total[at] += product(q, STACK + i * size, size, block)
                return carry

            return step

        short = most <= STACK + SHORT_STACK
        more = jnp.maximum(most - STACK, 0)
        lax.fori_loop(0, jnp.where(short, jnp.minimum(more, 1), 0), steps(SHORT_STACK), 0)
        lax.fori_loop(0, jnp.where(short, 0, (more + STACK - 1) // STACK), steps(STACK), 0)

    @pl.when(f_near)
    def _():
        all_products(near, far)

    @pl.when(jnp.logical_not(f_near))
    def _():
        all_products(far, near)


def shared_products(tables, *blocks):
    return pl.pallas_call(
        shared_kernel,
        out_shape=squares(len(SHARED), blocks[0].shape[-1]),
        in_specs=smem(len(tables)) + vmem(len(blocks)),
        out_specs=vmem(1)[0],
        compiler_params=pltpu.CompilerParams(vmem_limit_bytes=2 * LIMIT),
        cost_estimate=cost(*blocks),
    )(*tables, *blocks)


def message_kernel(total, *refs):
    shares, (to_near, to_far, to_mate, to_y, to_y_other, summed) = refs[:-6], refs[-6:]
    _, _, _, _, flag, _, _, f_near = place_of_device()
    width = total.shape[1]

    def put(out, values):
        for i, value in enumerate(values):
            out[i * width:(i + 1) * width, :] = value.astype(BF16)

    def to_f_and_g(to_f, to_g):
        cross = total[CROSS].T
        nothing = jnp.zeros_like(cross)
        put(to_f, (total[XF].T, jnp.where(flag, cross, nothing), total[YF].T, total[YOF].T))
        put(to_g, (total[XG].T, jnp.where(flag, nothing, cross), nothing, nothing))

    @pl.when(f_near)
    def _():
        to_f_and_g(to_near, to_far)

    @pl.when(jnp.logical_not(f_near))
    def _():
        to_f_and_g(to_far, to_near)

    put(to_y, (total[XY].T, total[XYO].T, total[YF]))
    to_y[3 * width:, :] = jnp.zeros((to_y.shape[0] - 3 * width, width), BF16)
    put(to_y_other, (total[YOF],))
    to_mate[0] = total[XYO]
    to_mate[1] = total[CROSS]
    gathered = sum(share[...] for share in shares)
    summed[...] = gathered
    lines = gathered.shape[1] // width
    rest, rows = gathered, []
    for _ in range(3):
        part = rest.astype(BF16)
        rest = rest - part.astype(F32)
        rows += [part[:, i * width:(i + 1) * width].astype(F32) for i in range(lines)]
    rows.append(jnp.zeros((to_near.shape[0] - 4 * width - 3 * lines, width), F32))
    to_near[4 * width:, :] = jnp.concatenate(rows, axis=0).astype(BF16)


def messages(total, shares):
    width = total.shape[-1]
    lines = -(-3 * shares[0].shape[1] // width // 16) * 16
    flat = jax.ShapeDtypeStruct
    sent = lambda rows: flat((rows, width), BF16)
    return pl.pallas_call(
        message_kernel,
        out_shape=[
            sent(4 * width + lines + 16), sent(4 * width), squares(2, width), sent(4 * width + 16), sent(width),
            flat(shares[0].shape, F32),
        ],
        in_specs=vmem(1 + len(shares)),
        out_specs=vmem(6),
        compiler_params=pltpu.CompilerParams(vmem_limit_bytes=LIMIT),
        cost_estimate=cost(total, total),
    )(total, *shares)


def coulomb_kernel(own, own_side, share, from_near, out, summed):
    rows, half, width = own.shape
    odd = place_of_device()[3]
    lines = share.shape[1] // width
    parts = from_near[4 * width:, :].astype(F32)
    line = lambda i: jnp.concatenate([parts[i * lines + j:i * lines + j + 1] for j in range(lines)], axis=1)
    gathered = share[...] + (line(0) + line(1) + line(2))
    summed[...] = gathered
    low, high = gathered[:, :half], gathered[:, half:2 * half]
    gamma = jnp.where(odd == 1, high, low).astype(BF16)
    side_gamma = jnp.where(odd == 1, low, high).astype(BF16)
    for row in range(rows):
        part = jnp.dot(gamma, own[row], preferred_element_type=F32)
        out[row] = part + jnp.dot(side_gamma, own_side[row], preferred_element_type=F32)


def coulomb(own, own_side, share, from_near):
    rows, _, width = own.shape
    flat = jax.ShapeDtypeStruct
    out, summed = pl.pallas_call(
        coulomb_kernel,
        out_shape=[flat((rows, 1, width), F32), flat(share.shape, F32)],
        in_specs=vmem(4),
        out_specs=vmem(2),
        compiler_params=pltpu.CompilerParams(vmem_limit_bytes=LIMIT),
        cost_estimate=cost(own, own_side),
    )(own, own_side, share, from_near)
    return jnp.swapaxes(out, 0, 1), summed


def band_kernel(aux, pairs, summed, own, total, from_y, from_near, from_far, from_mate, from_y_other, band, made, sems):
    depth, width = pairs.shape[1], band.shape[1]
    me, core, _, odd, _, _, _, f_near = place_of_device()
    count = lax.axis_size("basis")
    sign, cross = 1 - 2 * odd, 1 - 2 * core
    copies = []

    def put(ahead, value):
        far = jnp.abs(ahead)
        slot = len(copies)
        if slot == 0:
            made[slot] = value
        else:
            lower = summed[0, aux + jnp.maximum(me - far, 0) * depth + far - 1] > 0.5
            upper = pairs[0, far - 1] == 1
            there = jnp.logical_or(jnp.logical_and(ahead > 0, upper), jnp.logical_and(ahead < 0, lower))
            there = jnp.logical_and(there, jnp.logical_and(me + ahead >= 0, me + ahead < count))
            made[slot] = jnp.where(there, value, 0.0)
        copies.append(pltpu.make_async_copy(made.at[slot], band.at[depth + ahead], sems.at[slot]))
        copies[-1].start()

    block = lambda ref, i: ref[i * width:(i + 1) * width, :].astype(F32)
    from_f = lambda i: jnp.where(f_near, block(from_far, i), block(from_near, i))
    from_g = lambda i: jnp.where(f_near, block(from_near, i), block(from_far, i))
    put(0, own[0])
    put(cross, own[1])
    put(2 * sign, total[XY] + block(from_y, 0))
    put(2 * sign + cross, from_mate[0] + block(from_y, 1))
    put(-2 * sign, block(from_y, 2) + from_f(2))
    put(-2 * sign + cross, block(from_y_other, 0) + from_f(3))
    put(4 * sign, total[XF] + from_g(0))
    put(-4 * sign, total[XG] + from_f(0))
    put(-3 * cross, from_mate[1] + from_f(1) + from_g(1))
    for copy in copies:
        copy.wait()


def finish(aux, pairs, summed, own, *partials):
    depth, width = pairs.shape[1], own.shape[-1]
    size = 2 * depth + 1
    return pl.pallas_call(
        functools.partial(band_kernel, aux),
        out_shape=squares(size, width),
        in_specs=smem(2) + vmem(1 + len(partials)),
        out_specs=pl.BlockSpec(memory_space=pl.ANY),
        scratch_shapes=[pltpu.VMEM((size, width, width), F32), pltpu.SemaphoreType.DMA((size,))],
        compiler_params=pltpu.CompilerParams(vmem_limit_bytes=LIMIT),
        cost_estimate=cost(own, *partials),
    )(pairs, summed, own, *partials)


def add_kernel(*refs):
    refs[-1][...] = sum(share[...] for share in refs[:-1])


def added(shares):
    return pl.pallas_call(
        add_kernel,
        out_shape=jax.ShapeDtypeStruct(shares[0].shape, F32),
        in_specs=vmem(len(shares)),
        out_specs=vmem(1)[0],
        compiler_params=pltpu.CompilerParams(vmem_limit_bytes=LIMIT),
        cost_estimate=cost(*shares),
    )(*shares)


def shares_of(values, count, step):
    return [values, lax.ppermute(values, "basis", [(i, i ^ step) for i in range(count)])]


def per_device(factors, coefs, domains, pairs):
    own = factors[0]
    _, aux, _ = own.shape
    count = lax.axis_size("basis")

    swap = chip_route(count, lambda c: c, swap=True)
    across = chip_route(count, lambda c: c ^ 1)
    to_near = chip_route(count, lambda c: c ^ 2)
    to_far = chip_route(count, lambda c: c - 2 if c & 2 == 0 else c + 2)
    senders = {source for source, _ in to_far}
    to_far += [(i, i ^ 1) for i in range(count) if i not in senders]
    send = lambda value, route: lax.ppermute(value, "basis", route)

    xo = send(own, swap)
    xj_side, xj, for_near, for_far = cut(own)
    yj = send(xj_side, across)
    near, far = send(for_near, to_near), send(for_far, to_far)
    own_pairs, share, *tables = own_products(domains, pairs, xj, xj_side, xo, coefs[0])
    share = added(shares_of(share, count, 1))
    y_low, y_high, share = relay(yj, shares_of(share, count, 2))
    yo, yo_high = send(y_low, swap), send(y_high, swap)
    shares, step = [share], 8
    while step < count:
        if len(shares) > 1:
            shares = [added(shares)]
        shares = shares_of(shares[0], count, step)
        step *= 2
    total = shared_products(tables, xj, xj_side, xo, yj, yo, yo_high, near, far)
    for_near, for_far, for_mate, for_y, for_y_other, share = messages(total, shares)
    from_near, from_far = send(for_near, to_near), send(for_far, to_far)
    from_y, from_y_other = send(for_y, across), send(for_y_other, chip_route(count, lambda c: c ^ 1, swap=True))
    from_mate = send(for_mate, swap)
    coulomb_half, summed = coulomb(xj, xj_side, share, from_near)
    band = finish(aux, pairs, summed, own_pairs, total, from_y, from_near, from_far, from_mate, from_y_other)
    return (band[None], coulomb_half)


def solution(mesh):
    placed = (
        P(("groups", "basis"), None, None, None),
        P(("groups", "basis"), None, None),
        P("groups", None),
        P(("groups", "basis"), None),
    )
    return jax.shard_map(
        per_device,
        mesh=mesh,
        in_specs=placed,
        out_specs=(P(("groups", "basis"), None, None, None), P(("groups", "basis"), None, None)),
        check_vma=False,
    )
```

```python
import functools

import jax
import jax.numpy as jnp
from jax import lax
from jax.experimental import pallas as pl
from jax.experimental.pallas import tpu as pltpu
from jax.sharding import PartitionSpec as P

F32 = jnp.float32
BF16 = jnp.bfloat16

XJ, XO, XJ_SIDE, YJ, YO, YO_HIGH, FJ, GJ = range(8)
XF, YF, YOF, XG, XY, XYO, CROSS, OWN = range(8)
PRODUCTS = ((XJ, FJ), (YJ, FJ), (YO, FJ), (XJ_SIDE, GJ), (XJ, YJ), (XO, YJ), (XO, None), (XJ, XO))
SHARED, WITH_Y = (XF, YF, YOF, XG, CROSS), (XY, XYO)
STACK, SHORT_STACK, OWN_STACK = 10, 8, 4
LIMIT = 12 * 2**20


def cost(*arrays):
    return pl.CostEstimate(flops=1, bytes_accessed=sum(a.size * a.dtype.itemsize for a in arrays), transcendentals=0)


def smem(n):
    return [pl.BlockSpec(memory_space=pltpu.SMEM)] * n


def vmem(n):
    return [pl.BlockSpec(memory_space=pltpu.VMEM)] * n


def squares(n, width):
    return jax.ShapeDtypeStruct((n, width, width), F32)


def multiply(left, right):
    return lax.dot_general(left, right, (((0,), (0,)), ((), ())), preferred_element_type=F32)


def chip_route(count, target, swap=False):
    chips = count // 2
    route = []
    for chip in range(chips):
        to = target(chip)
        if 0 <= to < chips:
            for core in range(2):
                route.append((2 * chip + core, 2 * to + (1 - core if swap else core)))
    return route


def place_of_device():
    me = lax.axis_index("basis")
    core, chip = me & 1, me >> 1
    odd = chip & 1
    return me, core, chip, odd, core == odd, chip + 2 - 4 * odd, chip - 2 + 4 * odd, odd == ((chip >> 1) & 1)


def cut_kernel(size, own, side, main, near, far, sems):
    _, _, _, odd, _, _, _, f_near = place_of_device()
    side_start, main_start = (1 - odd) * size, odd * size
    near_start, far_start = jnp.where(f_near, side_start, main_start), jnp.where(f_near, main_start, side_start)
    copies = []
    for i, (out, start) in enumerate(
        ((side, side_start), (near, near_start), (far, far_start), (main, main_start))
    ):
        rows = pl.ds(pl.multiple_of(start, 16), size)
        copies.append(pltpu.make_async_copy(own.at[:, rows, :], out, sems.at[i]))
    for copy in copies:
        copy.start()
    for copy in copies:
        copy.wait()


def cut(own):
    rows, aux, width = own.shape
    part = jax.ShapeDtypeStruct((rows, aux // 2, width), own.dtype)
    return pl.pallas_call(
        functools.partial(cut_kernel, aux // 2),
        out_shape=[part] * 4,
        in_specs=vmem(1),
        out_specs=vmem(4),
        scratch_shapes=[pltpu.SemaphoreType.DMA((4,))],
        compiler_params=pltpu.CompilerParams(vmem_limit_bytes=LIMIT),
        cost_estimate=cost(own, own),
    )(own)


def lists_of(table):
    width = table.shape[1] // 2 - 4
    return lambda q: table[q, 2 * width], lambda q, slot: table[q, slot], lambda q, slot: table[q, width + slot]


def find_matches(domains, table, spot):
    count, rows = domains.shape
    width = table.shape[1] // 2 - 4
    _, core, chip, _, flag, f_chip, g_chip, _ = place_of_device()
    mine_first, other_first = (chip, core), (chip, 1 - core)
    block = {XJ: mine_first, XJ_SIDE: mine_first, XO: other_first, None: (jnp.where(flag, f_chip, g_chip), core)}
    block |= {YJ: (chip ^ 1, core), YO: (chip ^ 1, 1 - core), FJ: (f_chip, core), GJ: (g_chip, core)}

    for q, (left, right) in enumerate(PRODUCTS):
        there, ids = [], []
        for name in (left, right):
            at, one = block[name]
            there.append(jnp.logical_and(at >= 0, 2 * at < count))
            ids.append(2 * jnp.clip(at, 0, count // 2 - 1) + one)
        both = jnp.logical_and(*there)
        base = 2 * ids[1]

        def clear(i, carry):
            spot[i] = -1
            return carry

        def fill(row, carry):
            spot[domains[ids[1], row] - base] = row
            return carry

        def clean(slot, carry):
            table[q, slot] = 0
            table[q, width + slot] = 0
            return carry

        def scan(row, found):
            away = domains[ids[0], row] - base
            inside = jnp.logical_and(away >= 0, away < 2 * rows)
            other_row = spot[jnp.clip(away, 0, 2 * rows - 1)]
            hit = jnp.logical_and(jnp.logical_and(inside, both), other_row >= 0)
            table[q, found] = row
            table[q, width + found] = jnp.maximum(other_row, 0)
            return found + hit.astype(jnp.int32)

        lax.fori_loop(0, 2 * rows, clear, 0, unroll=10)
        lax.fori_loop(0, rows, fill, 0, unroll=10)
        lax.fori_loop(0, width, clean, 0, unroll=9)
        table[q, 2 * width] = lax.fori_loop(0, rows, scan, 0, unroll=5)


def own_kernel(domains, pairs, own, own_side, other, coef, out, share, table, spot):
    rows, half, width = own.shape
    me, _, _, odd, _, _, _, _ = place_of_device()
    find_matches(domains, table, spot)
    number, mine, theirs = lists_of(table)
    out[...] = jnp.zeros_like(out)
    size = max(n for n in range(1, 11) if rows % n == 0)

    def square(step, carry):
        for part in (own, own_side):
            left = part[pl.ds(size * step, size)].reshape(size * half, width)
            out[0] += multiply(left, left)
        return carry

    lax.fori_loop(0, rows // size, square, 0)

    def beside(step, carry):
        lefts, rights = [], []
        for i in range(OWN_STACK):
            slot = OWN_STACK * step + i
            for part, start in ((own, odd * half), (own_side, (1 - odd) * half)):
                left = part[mine(OWN, slot)]
                lefts.append(jnp.where(slot < number(OWN), left, jnp.zeros_like(left)))
                rights.append(other[theirs(OWN, slot), pl.ds(pl.multiple_of(start, 16), half), :])
        out[1] += multiply(jnp.concatenate(lefts, axis=0), jnp.concatenate(rights, axis=0))
        return carry

    lax.fori_loop(0, (number(OWN) + OWN_STACK - 1) // OWN_STACK, beside, 0)

    tile = 128
    parts = []
    for part in (own, own_side):
        sums = []
        for start in range(0, half, tile):
            total = jnp.zeros((tile, width), F32)
            for row in range(rows):
                total += part[row, start:start + tile, :].astype(F32) * coef[row:row + 1, :].astype(F32)
            sums.append(jnp.sum(total.T, axis=0, keepdims=True))
        parts.append(jnp.concatenate(sums, axis=1))
    share[:, :half] = jnp.where(odd == 1, parts[1], parts[0])
    share[:, half:2 * half] = jnp.where(odd == 1, parts[0], parts[1])
    depth = pairs.shape[1]
    lane = lax.broadcasted_iota(jnp.int32, (1, share.shape[1] - 2 * half), 1)
    marks = jnp.zeros(lane.shape, F32)
    for r in range(depth):
        marks = jnp.where(lane == me * depth + r, pairs[0, r].astype(F32), marks)
    share[:, 2 * half:] = marks


def own_products(domains, pairs, own, own_side, other, coef):
    rows, half, width = own.shape
    count = domains.shape[0]
    marks = -(-count * pairs.shape[1] // 128) * 128
    most = max(-(-rows // n) * n for n in (STACK, OWN_STACK))
    table = jax.ShapeDtypeStruct((len(PRODUCTS), 2 * most + 8), jnp.int32)
    return pl.pallas_call(
        own_kernel,
        out_shape=[
            squares(2, width),
            jax.ShapeDtypeStruct((1, 2 * half + marks), F32),
            table,
        ],
        in_specs=smem(2) + vmem(4),
        out_specs=vmem(2) + smem(1),
        scratch_shapes=[pltpu.SMEM((2 * rows,), jnp.int32)],
        compiler_params=pltpu.CompilerParams(vmem_limit_bytes=LIMIT),
        cost_estimate=cost(own, own_side, other),
    )(domains, pairs, own, own_side, other, coef)


def relay_kernel(value, *refs):
    shares, (low, high, total, sems) = refs[:-4], refs[-4:]
    size = low.shape[1]
    copies = [
        pltpu.make_async_copy(value.at[:, :size, :], low, sems.at[0]),
        pltpu.make_async_copy(value.at[:, size:, :], high, sems.at[1]),
    ]
    for copy in copies:
        copy.start()
    total[...] = sum(share[...] for share in shares)
    for copy in copies:
        copy.wait()


def relay(value, shares):
    rows, size, width = value.shape
    part = jax.ShapeDtypeStruct((rows, size // 2, width), value.dtype)
    return pl.pallas_call(
        relay_kernel,
        out_shape=[part, part, jax.ShapeDtypeStruct(shares[0].shape, F32)],
        in_specs=vmem(1 + len(shares)),
        out_specs=vmem(3),
        scratch_shapes=[pltpu.SemaphoreType.DMA((2,))],
        compiler_params=pltpu.CompilerParams(vmem_limit_bytes=LIMIT),
        cost_estimate=cost(value, value),
    )(value, *shares)


def add_products(listed, table, rows_of, total):
    number, mine, theirs = lists_of(table)

    def product(q, first, size):
        lefts, rights = [], []
        left_block, right_block = PRODUCTS[q]
        for i in range(size):
            slot = first + i
            left = rows_of(left_block, q, mine(q, slot))
            lefts.append(jnp.where(slot < number(q), left, jnp.zeros_like(left)))
            rights.append(rows_of(right_block, q, theirs(q, slot)))
        return multiply(jnp.concatenate(lefts, axis=0), jnp.concatenate(rights, axis=0))

    most = number(listed[0])
    for at, q in enumerate(listed):
        most = jnp.maximum(most, number(q))
        total[at] = product(q, 0, STACK)

    def steps(size):
        def step(i, carry):
            for at, q in enumerate(listed):
                total[at] += product(q, STACK + i * size, size)
            return carry

        return step

    short = most <= STACK + SHORT_STACK
    more = jnp.maximum(most - STACK, 0)
    lax.fori_loop(0, jnp.where(short, jnp.minimum(more, 1), 0), steps(SHORT_STACK), 0)
    lax.fori_loop(0, jnp.where(short, 0, (more + STACK - 1) // STACK), steps(STACK), 0)


def y_kernel(table, xj, xo, yj, total):
    odd, half = place_of_device()[3], xj.shape[1]
    main = pl.ds(pl.multiple_of(odd * half, 16), half)
    block = {XJ: lambda row: xj[row], YJ: lambda row: yj[row], XO: lambda row: xo[row, main, :]}
    add_products(WITH_Y, table, lambda name, q, row: block[name](row), total)


def shared_kernel(table, xj, xj_side, xo, yj, yo, yo_high, near, far, token, total):
    _, _, _, odd, flag, _, _, f_near = place_of_device()
    half = xj.shape[1]
    cross = pl.ds(pl.multiple_of(jnp.where(flag, odd, 1 - odd) * half, 16), half)
    block = {XJ: lambda row: xj[row], XJ_SIDE: lambda row: xj_side[row], YJ: lambda row: yj[row]}
    block[XO] = lambda row: xo[row, cross, :]
    block[YO] = lambda row: jnp.concatenate([yo[row], yo_high[row]], axis=0)

    def all_products(fj, gj):
        block[FJ], block[GJ] = lambda row: fj[row], lambda row: gj[row]
        block[None] = lambda row: jnp.where(flag, fj[row], gj[row])
        add_products(SHARED, table, lambda name, q, row: block[name](row), total)

    @pl.when(f_near)
    def _():
        all_products(near, far)

    @pl.when(jnp.logical_not(f_near))
    def _():
        all_products(far, near)


def products(kernel, listed, table, *blocks):
    return pl.pallas_call(
        kernel,
        out_shape=squares(len(listed), blocks[0].shape[-1]),
        in_specs=smem(1) + vmem(len(blocks)),
        out_specs=vmem(1)[0],
        compiler_params=pltpu.CompilerParams(vmem_limit_bytes=2 * LIMIT),
        cost_estimate=cost(*blocks),
    )(table, *blocks)


def message_kernel(total, with_y, *refs):
    shares, (to_near, to_far, to_mate, to_y, to_y_other, summed) = refs[:-6], refs[-6:]
    _, _, _, _, flag, _, _, f_near = place_of_device()
    width = total.shape[1]

    def put(out, values):
        for i, value in enumerate(values):
            out[i * width:(i + 1) * width, :] = value.astype(BF16)

    def to_f_and_g(to_f, to_g):
        cross = total[SHARED.index(CROSS)].T
        nothing = jnp.zeros_like(cross)
        put(to_f, (total[SHARED.index(XF)].T, jnp.where(flag, cross, nothing), total[SHARED.index(YF)].T, total[SHARED.index(YOF)].T))
        put(to_g, (total[SHARED.index(XG)].T, jnp.where(flag, nothing, cross), nothing, nothing))

    @pl.when(f_near)
    def _():
        to_f_and_g(to_near, to_far)

    @pl.when(jnp.logical_not(f_near))
    def _():
        to_f_and_g(to_far, to_near)

    put(to_y, (with_y[0].T, with_y[1].T, total[SHARED.index(YF)]))
    to_y[3 * width:, :] = jnp.zeros((to_y.shape[0] - 3 * width, width), BF16)
    put(to_y_other, (total[SHARED.index(YOF)],))
    to_mate[0] = with_y[1]
    to_mate[1] = total[SHARED.index(CROSS)]
    gathered = sum(share[...] for share in shares)
    summed[...] = gathered
    lines = gathered.shape[1] // width
    rest, rows = gathered, []
    for _ in range(3):
        part = rest.astype(BF16)
        rest = rest - part.astype(F32)
        rows += [part[:, i * width:(i + 1) * width].astype(F32) for i in range(lines)]
    rows.append(jnp.zeros((to_near.shape[0] - 4 * width - 3 * lines, width), F32))
    to_near[4 * width:, :] = jnp.concatenate(rows, axis=0).astype(BF16)


def messages(total, with_y, shares):
    width = total.shape[-1]
    lines = -(-3 * shares[0].shape[1] // width // 16) * 16
    flat = jax.ShapeDtypeStruct
    sent = lambda rows: flat((rows, width), BF16)
    return pl.pallas_call(
        message_kernel,
        out_shape=[
            sent(4 * width + lines + 16), sent(4 * width), squares(2, width), sent(4 * width + 16), sent(width),
            flat(shares[0].shape, F32),
        ],
        in_specs=vmem(2 + len(shares)),
        out_specs=vmem(6),
        compiler_params=pltpu.CompilerParams(vmem_limit_bytes=LIMIT),
        cost_estimate=cost(total, total),
    )(total, with_y, *shares)


def coulomb_kernel(own, own_side, share, from_near, out, summed):
    rows, half, width = own.shape
    odd = place_of_device()[3]
    lines = share.shape[1] // width
    parts = from_near[4 * width:, :].astype(F32)
    line = lambda i: jnp.concatenate([parts[i * lines + j:i * lines + j + 1] for j in range(lines)], axis=1)
    gathered = share[...] + (line(0) + line(1) + line(2))
    summed[...] = gathered
    low, high = gathered[:, :half], gathered[:, half:2 * half]
    gamma = jnp.where(odd == 1, high, low).astype(BF16)
    side_gamma = jnp.where(odd == 1, low, high).astype(BF16)
    for row in range(rows):
        part = jnp.dot(gamma, own[row], preferred_element_type=F32)
        out[row] = part + jnp.dot(side_gamma, own_side[row], preferred_element_type=F32)


def coulomb(own, own_side, share, from_near):
    rows, _, width = own.shape
    flat = jax.ShapeDtypeStruct
    out, summed = pl.pallas_call(
        coulomb_kernel,
        out_shape=[flat((rows, 1, width), F32), flat(share.shape, F32)],
        in_specs=vmem(4),
        out_specs=vmem(2),
        compiler_params=pltpu.CompilerParams(vmem_limit_bytes=LIMIT),
        cost_estimate=cost(own, own_side),
    )(own, own_side, share, from_near)
    return jnp.swapaxes(out, 0, 1), summed


def band_kernel(aux, pairs, summed, own, total, with_y, from_y, from_near, from_far, from_mate, from_y_other, band, made, sems):
    depth, width = pairs.shape[1], band.shape[1]
    me, core, _, odd, _, _, _, f_near = place_of_device()
    count = lax.axis_size("basis")
    sign, cross = 1 - 2 * odd, 1 - 2 * core
    copies = []

    def put(ahead, value):
        far = jnp.abs(ahead)
        slot = len(copies)
        if slot == 0:
            made[slot] = value
        else:
            lower = summed[0, aux + jnp.maximum(me - far, 0) * depth + far - 1] > 0.5
            upper = pairs[0, far - 1] == 1
            there = jnp.logical_or(jnp.logical_and(ahead > 0, upper), jnp.logical_and(ahead < 0, lower))
            there = jnp.logical_and(there, jnp.logical_and(me + ahead >= 0, me + ahead < count))
            made[slot] = jnp.where(there, value, 0.0)
        copies.append(pltpu.make_async_copy(made.at[slot], band.at[depth + ahead], sems.at[slot]))
        copies[-1].start()

    block = lambda ref, i: ref[i * width:(i + 1) * width, :].astype(F32)
    from_f = lambda i: jnp.where(f_near, block(from_far, i), block(from_near, i))
    from_g = lambda i: jnp.where(f_near, block(from_near, i), block(from_far, i))
    put(0, own[0])
    put(cross, own[1])
    put(2 * sign, with_y[0] + block(from_y, 0))
    put(2 * sign + cross, from_mate[0] + block(from_y, 1))
    put(-2 * sign, block(from_y, 2) + from_f(2))
    put(-2 * sign + cross, block(from_y_other, 0) + from_f(3))
    put(4 * sign, total[SHARED.index(XF)] + from_g(0))
    put(-4 * sign, total[SHARED.index(XG)] + from_f(0))
    put(-3 * cross, from_mate[1] + from_f(1) + from_g(1))
    for copy in copies:
        copy.wait()


def finish(aux, pairs, summed, own, *partials):
    depth, width = pairs.shape[1], own.shape[-1]
    size = 2 * depth + 1
    return pl.pallas_call(
        functools.partial(band_kernel, aux),
        out_shape=squares(size, width),
        in_specs=smem(2) + vmem(1 + len(partials)),
        out_specs=pl.BlockSpec(memory_space=pl.ANY),
        scratch_shapes=[pltpu.VMEM((size, width, width), F32), pltpu.SemaphoreType.DMA((size,))],
        compiler_params=pltpu.CompilerParams(vmem_limit_bytes=LIMIT),
        cost_estimate=cost(own, *partials),
    )(pairs, summed, own, *partials)


def add_kernel(*refs):
    refs[-1][...] = sum(share[...] for share in refs[:-1])


def added(shares):
    return pl.pallas_call(
        add_kernel,
        out_shape=jax.ShapeDtypeStruct(shares[0].shape, F32),
        in_specs=vmem(len(shares)),
        out_specs=vmem(1)[0],
        compiler_params=pltpu.CompilerParams(vmem_limit_bytes=LIMIT),
        cost_estimate=cost(*shares),
    )(*shares)


def shares_of(values, count, step):
    return [values, lax.ppermute(values, "basis", [(i, i ^ step) for i in range(count)])]


def per_device(factors, coefs, domains, pairs):
    own = factors[0]
    _, aux, _ = own.shape
    count = lax.axis_size("basis")

    swap = chip_route(count, lambda c: c, swap=True)
    across = chip_route(count, lambda c: c ^ 1)
    to_near = chip_route(count, lambda c: c ^ 2)
    to_far = chip_route(count, lambda c: c - 2 if c & 2 == 0 else c + 2)
    senders = {source for source, _ in to_far}
    to_far += [(i, i ^ 1) for i in range(count) if i not in senders]
    send = lambda value, route: lax.ppermute(value, "basis", route)

    xo = send(own, swap)
    xj_side, xj, for_near, for_far = cut(own)
    yj = send(xj_side, across)
    near, far = send(for_near, to_near), send(for_far, to_far)
    own_pairs, share, table = own_products(domains, pairs, xj, xj_side, xo, coefs[0])
    share = added(shares_of(share, count, 1))
    y_low, y_high, share = relay(yj, shares_of(share, count, 2))
    yo, yo_high = send(y_low, swap), send(y_high, swap)
    shares, step = [share], 8
    while step < count:
        if len(shares) > 1:
            shares = [added(shares)]
        shares = shares_of(shares[0], count, step)
        step *= 2
    with_y = products(y_kernel, WITH_Y, table, xj, xo, yj)
    total = products(shared_kernel, SHARED, table, xj, xj_side, xo, yj, yo, yo_high, near, far, with_y)
    for_near, for_far, for_mate, for_y, for_y_other, share = messages(total, with_y, shares)
    from_near, from_far = send(for_near, to_near), send(for_far, to_far)
    from_y, from_y_other = send(for_y, across), send(for_y_other, chip_route(count, lambda c: c ^ 1, swap=True))
    from_mate = send(for_mate, swap)
    coulomb_half, summed = coulomb(xj, xj_side, share, from_near)
    band = finish(aux, pairs, summed, own_pairs, total, with_y, from_y, from_near, from_far, from_mate, from_y_other)
    return (band[None], coulomb_half)


def solution(mesh):
    placed = (
        P(("groups", "basis"), None, None, None),
        P(("groups", "basis"), None, None),
        P("groups", None),
        P(("groups", "basis"), None),
    )
    return jax.shard_map(
        per_device,
        mesh=mesh,
        in_specs=placed,
        out_specs=(P(("groups", "basis"), None, None, None), P(("groups", "basis"), None, None)),
        check_vma=False,
    )
```

```python
import functools

import jax
import jax.numpy as jnp
from jax import lax
from jax.experimental import pallas as pl
from jax.experimental.pallas import tpu as pltpu
from jax.sharding import PartitionSpec as P

F32 = jnp.float32
BF16 = jnp.bfloat16

XJ, XO, XJ_SIDE, YJ, YO, FJ, GJ = range(7)
XF, YF, YOF, XG, XY, XYO, CROSS, OWN = range(8)
PRODUCTS = ((XJ, FJ), (YJ, FJ), (YO, FJ), (XJ_SIDE, GJ), (XJ, YJ), (XO, YJ), (XO, None), (XJ, XO))
SHARED = (XF, YF, YOF, XG, XY, XYO, CROSS)
STACK, SHORT_STACK, OWN_STACK = 10, 8, 4
LIMIT = 12 * 2**20
LATE = 144


def cost(*arrays):
    return pl.CostEstimate(flops=1, bytes_accessed=sum(a.size * a.dtype.itemsize for a in arrays), transcendentals=0)


def smem(n):
    return [pl.BlockSpec(memory_space=pltpu.SMEM)] * n


def vmem(n):
    return [pl.BlockSpec(memory_space=pltpu.VMEM)] * n


def squares(n, width):
    return jax.ShapeDtypeStruct((n, width, width), F32)


def multiply(left, right):
    return lax.dot_general(left, right, (((0,), (0,)), ((), ())), preferred_element_type=F32)


def chip_route(count, target, swap=False):
    chips = count // 2
    route = []
    for chip in range(chips):
        to = target(chip)
        if 0 <= to < chips:
            for core in range(2):
                route.append((2 * chip + core, 2 * to + (1 - core if swap else core)))
    return route


def place_of_device():
    me = lax.axis_index("basis")
    core, chip = me & 1, me >> 1
    odd = chip & 1
    return me, core, chip, odd, core == odd, chip + 2 - 4 * odd, chip - 2 + 4 * odd, odd == ((chip >> 1) & 1)


def cut_kernel(size, own, early, late, near, far, main, side, sems):
    _, _, _, odd, _, _, _, f_near = place_of_device()
    side_start, main_start = (1 - odd) * size, odd * size
    near_start, far_start = jnp.where(f_near, side_start, main_start), jnp.where(f_near, main_start, side_start)
    outs = (early, late, near, far, main, side)
    starts = (side_start, side_start + size - LATE, near_start, far_start, main_start, side_start)
    copies = []
    for i, (out, start) in enumerate(zip(outs, starts)):
        rows = pl.ds(pl.multiple_of(start, 16), out.shape[1])
        copies.append(pltpu.make_async_copy(own.at[:, rows, :], out, sems.at[i]))
    for copy in copies:
        copy.start()
    for copy in copies:
        copy.wait()


def cut(own):
    rows, aux, width = own.shape
    half = aux // 2
    sizes = (half - LATE, LATE, half, half, half, half)
    return pl.pallas_call(
        functools.partial(cut_kernel, half),
        out_shape=[jax.ShapeDtypeStruct((rows, size, width), own.dtype) for size in sizes],
        in_specs=vmem(1),
        out_specs=vmem(6),
        scratch_shapes=[pltpu.SemaphoreType.DMA((6,))],
        compiler_params=pltpu.CompilerParams(vmem_limit_bytes=LIMIT),
        cost_estimate=cost(own, own),
    )(own)


def lists_of(table):
    width = table.shape[1] // 2 - 4
    return lambda q: table[q, 2 * width], lambda q, slot: table[q, slot], lambda q, slot: table[q, width + slot]


def find_matches(domains, table, spot):
    count, rows = domains.shape
    width = table.shape[1] // 2 - 4
    _, core, chip, _, flag, f_chip, g_chip, _ = place_of_device()
    mine_first, other_first = (chip, core), (chip, 1 - core)
    block = {XJ: mine_first, XJ_SIDE: mine_first, XO: other_first, None: (jnp.where(flag, f_chip, g_chip), core)}
    block |= {YJ: (chip ^ 1, core), YO: (chip ^ 1, 1 - core), FJ: (f_chip, core), GJ: (g_chip, core)}

    for q, (left, right) in enumerate(PRODUCTS):
        there, ids = [], []
        for name in (left, right):
            at, one = block[name]
            there.append(jnp.logical_and(at >= 0, 2 * at < count))
            ids.append(2 * jnp.clip(at, 0, count // 2 - 1) + one)
        both = jnp.logical_and(*there)
        base = 2 * ids[1]

        def clear(i, carry):
            spot[i] = -1
            return carry

        def fill(row, carry):
            spot[domains[ids[1], row] - base] = row
            return carry

        def clean(slot, carry):
            table[q, slot] = 0
            table[q, width + slot] = 0
            return carry

        def scan(row, found):
            away = domains[ids[0], row] - base
            inside = jnp.logical_and(away >= 0, away < 2 * rows)
            other_row = spot[jnp.clip(away, 0, 2 * rows - 1)]
            hit = jnp.logical_and(jnp.logical_and(inside, both), other_row >= 0)
            table[q, found] = row
            table[q, width + found] = jnp.maximum(other_row, 0)
            return found + hit.astype(jnp.int32)

        lax.fori_loop(0, 2 * rows, clear, 0, unroll=10)
        lax.fori_loop(0, rows, fill, 0, unroll=10)
        lax.fori_loop(0, width, clean, 0, unroll=9)
        table[q, 2 * width] = lax.fori_loop(0, rows, scan, 0, unroll=5)


def own_kernel(domains, pairs, own, own_side, other, coef, out, share, table, spot):
    rows, half, width = own.shape
    me, _, _, odd, _, _, _, _ = place_of_device()
    find_matches(domains, table, spot)
    number, mine, theirs = lists_of(table)
    out[...] = jnp.zeros_like(out)
    size = max(n for n in range(1, 11) if rows % n == 0)

    def square(step, carry):
        for part in (own, own_side):
            left = part[pl.ds(size * step, size)].reshape(size * half, width)
            out[0] += multiply(left, left)
        return carry

    lax.fori_loop(0, rows // size, square, 0)

    def beside(step, carry):
        lefts, rights = [], []
        for i in range(OWN_STACK):
            slot = OWN_STACK * step + i
            for part, start in ((own, odd * half), (own_side, (1 - odd) * half)):
                left = part[mine(OWN, slot)]
                lefts.append(jnp.where(slot < number(OWN), left, jnp.zeros_like(left)))
                rights.append(other[theirs(OWN, slot), pl.ds(pl.multiple_of(start, 16), half), :])
        out[1] += multiply(jnp.concatenate(lefts, axis=0), jnp.concatenate(rights, axis=0))
        return carry

    lax.fori_loop(0, (number(OWN) + OWN_STACK - 1) // OWN_STACK, beside, 0)

    tile = 128
    parts = []
    for part in (own, own_side):
        sums = []
        for start in range(0, half, tile):
            total = jnp.zeros((tile, width), F32)
            for row in range(rows):
                total += part[row, start:start + tile, :].astype(F32) * coef[row:row + 1, :].astype(F32)
            sums.append(jnp.sum(total.T, axis=0, keepdims=True))
        parts.append(jnp.concatenate(sums, axis=1))
    share[:, :half] = jnp.where(odd == 1, parts[1], parts[0])
    share[:, half:2 * half] = jnp.where(odd == 1, parts[0], parts[1])
    depth = pairs.shape[1]
    lane = lax.broadcasted_iota(jnp.int32, (1, share.shape[1] - 2 * half), 1)
    marks = jnp.zeros(lane.shape, F32)
    for r in range(depth):
        marks = jnp.where(lane == me * depth + r, pairs[0, r].astype(F32), marks)
    share[:, 2 * half:] = marks


def own_products(domains, pairs, own, own_side, other, coef):
    rows, half, width = own.shape
    count = domains.shape[0]
    marks = -(-count * pairs.shape[1] // 128) * 128
    most = max(-(-rows // n) * n for n in (STACK, OWN_STACK))
    table = jax.ShapeDtypeStruct((len(PRODUCTS), 2 * most + 8), jnp.int32)
    return pl.pallas_call(
        own_kernel,
        out_shape=[
            squares(2, width),
            jax.ShapeDtypeStruct((1, 2 * half + marks), F32),
            table,
        ],
        in_specs=smem(2) + vmem(4),
        out_specs=vmem(2) + smem(1),
        scratch_shapes=[pltpu.SMEM((2 * rows,), jnp.int32)],
        compiler_params=pltpu.CompilerParams(vmem_limit_bytes=LIMIT),
        cost_estimate=cost(own, own_side, other),
    )(domains, pairs, own, own_side, other, coef)


def relay_kernel(count, parts, value, *refs):
    shares, (*outs, total, sems) = refs[:count], refs[-parts - 2:]
    copies, start = [], 0
    for i, out in enumerate(outs):
        size = out.shape[1]
        copies.append(pltpu.make_async_copy(value.at[:, start:start + size, :], out, sems.at[i]))
        start += size
    for copy in copies:
        copy.start()
    total[...] = sum(share[...] for share in shares)
    for copy in copies:
        copy.wait()


def relay(value, sizes, shares, *earlier):
    rows, _, width = value.shape
    parts = len(sizes)
    return pl.pallas_call(
        functools.partial(relay_kernel, len(shares), parts),
        out_shape=[jax.ShapeDtypeStruct((rows, size, width), value.dtype) for size in sizes] + [jax.ShapeDtypeStruct(shares[0].shape, F32)],
        in_specs=vmem(1 + len(shares) + len(earlier)),
        out_specs=vmem(parts + 1),
        scratch_shapes=[pltpu.SemaphoreType.DMA((parts,))],
        compiler_params=pltpu.CompilerParams(vmem_limit_bytes=LIMIT),
        cost_estimate=cost(value, value),
    )(value, *shares, *earlier)


def shared_kernel(table, xj, xj_side, xo, near, far, *refs):
    yj, yo, total = refs[:2], refs[2:-1], refs[-1]
    _, _, _, odd, flag, _, _, f_near = place_of_device()
    half = xj.shape[1]
    number, mine, theirs = lists_of(table)
    main = pl.ds(pl.multiple_of(odd * half, 16), half)
    cross = pl.ds(pl.multiple_of(jnp.where(flag, odd, 1 - odd) * half, 16), half)

    def product(q, first, size, block):
        lefts, rights = [], []
        left_block, right_block = PRODUCTS[q]
        for i in range(size):
            slot = first + i
            row, other_row = mine(q, slot), theirs(q, slot)
            if left_block == XO:
                left = xo[row, cross if q == CROSS else main, :]
            elif left_block == YO:
                left = jnp.concatenate([part[row] for part in yo], axis=0)
            elif left_block == YJ:
                left = jnp.concatenate([part[row] for part in yj], axis=0)
            else:
                left = block[left_block][row]
            lefts.append(jnp.where(slot < number(q), left, jnp.zeros_like(left)))
            if q == CROSS:
                rights.append(jnp.where(flag, block[FJ][other_row], block[GJ][other_row]))
            elif right_block == YJ:
                rights.append(jnp.concatenate([part[other_row] for part in yj], axis=0))
            else:
                rights.append(block[right_block][other_row])
        return multiply(jnp.concatenate(lefts, axis=0), jnp.concatenate(rights, axis=0))

    def all_products(fj, gj):
        block = {XJ: xj, XJ_SIDE: xj_side, FJ: fj, GJ: gj}
        most = number(SHARED[0])
        for at, q in enumerate(SHARED):
            most = jnp.maximum(most, number(q))
            total[at] = product(q, 0, STACK, block)

        def steps(size):
            def step(i, carry):
                for at, q in enumerate(SHARED):
                    total[at] += product(q, STACK + i * size, size, block)
                return carry

            return step

        short = most <= STACK + SHORT_STACK
        more = jnp.maximum(most - STACK, 0)
        lax.fori_loop(0, jnp.where(short, jnp.minimum(more, 1), 0), steps(SHORT_STACK), 0)
        lax.fori_loop(0, jnp.where(short, 0, (more + STACK - 1) // STACK), steps(STACK), 0)

    @pl.when(f_near)
    def _():
        all_products(near, far)

    @pl.when(jnp.logical_not(f_near))
    def _():
        all_products(far, near)


def shared_products(table, *blocks):
    return pl.pallas_call(
        shared_kernel,
        out_shape=squares(len(SHARED), blocks[0].shape[-1]),
        in_specs=smem(1) + vmem(len(blocks)),
        out_specs=vmem(1)[0],
        compiler_params=pltpu.CompilerParams(vmem_limit_bytes=2 * LIMIT),
        cost_estimate=cost(*blocks),
    )(table, *blocks)


def message_kernel(total, *refs):
    shares, (to_near, to_far, to_mate, to_y, to_y_other, summed) = refs[:-6], refs[-6:]
    _, _, _, _, flag, _, _, f_near = place_of_device()
    width = total.shape[1]

    def put(out, values):
        for i, value in enumerate(values):
            out[i * width:(i + 1) * width, :] = value.astype(BF16)

    def to_f_and_g(to_f, to_g):
        cross = total[CROSS].T
        nothing = jnp.zeros_like(cross)
        put(to_f, (total[XF].T, jnp.where(flag, cross, nothing), total[YF].T, total[YOF].T))
        put(to_g, (total[XG].T, jnp.where(flag, nothing, cross), nothing, nothing))

    @pl.when(f_near)
    def _():
        to_f_and_g(to_near, to_far)

    @pl.when(jnp.logical_not(f_near))
    def _():
        to_f_and_g(to_far, to_near)

    put(to_y, (total[XY].T, total[XYO].T, total[YF]))
    to_y[3 * width:, :] = jnp.zeros((to_y.shape[0] - 3 * width, width), BF16)
    put(to_y_other, (total[YOF],))
    to_mate[0] = total[XYO]
    to_mate[1] = total[CROSS]
    gathered = sum(share[...] for share in shares)
    summed[...] = gathered
    lines = gathered.shape[1] // width
    rest, rows = gathered, []
    for _ in range(3):
        part = rest.astype(BF16)
        rest = rest - part.astype(F32)
        rows += [part[:, i * width:(i + 1) * width].astype(F32) for i in range(lines)]
    rows.append(jnp.zeros((to_near.shape[0] - 4 * width - 3 * lines, width), F32))
    to_near[4 * width:, :] = jnp.concatenate(rows, axis=0).astype(BF16)


def messages(total, shares):
    width = total.shape[-1]
    lines = -(-3 * shares[0].shape[1] // width // 16) * 16
    flat = jax.ShapeDtypeStruct
    sent = lambda rows: flat((rows, width), BF16)
    return pl.pallas_call(
        message_kernel,
        out_shape=[
            sent(4 * width + lines + 16), sent(4 * width), squares(2, width), sent(4 * width + 16), sent(width),
            flat(shares[0].shape, F32),
        ],
        in_specs=vmem(1 + len(shares)),
        out_specs=vmem(6),
        compiler_params=pltpu.CompilerParams(vmem_limit_bytes=LIMIT),
        cost_estimate=cost(total, total),
    )(total, *shares)


def coulomb_kernel(own, own_side, share, from_near, out, summed):
    rows, half, width = own.shape
    odd = place_of_device()[3]
    lines = share.shape[1] // width
    parts = from_near[4 * width:, :].astype(F32)
    line = lambda i: jnp.concatenate([parts[i * lines + j:i * lines + j + 1] for j in range(lines)], axis=1)
    gathered = share[...] + (line(0) + line(1) + line(2))
    summed[...] = gathered
    low, high = gathered[:, :half], gathered[:, half:2 * half]
    gamma = jnp.where(odd == 1, high, low).astype(BF16)
    side_gamma = jnp.where(odd == 1, low, high).astype(BF16)
    for row in range(rows):
        part = jnp.dot(gamma, own[row], preferred_element_type=F32)
        out[row] = part + jnp.dot(side_gamma, own_side[row], preferred_element_type=F32)


def coulomb(own, own_side, share, from_near):
    rows, _, width = own.shape
    flat = jax.ShapeDtypeStruct
    out, summed = pl.pallas_call(
        coulomb_kernel,
        out_shape=[flat((rows, 1, width), F32), flat(share.shape, F32)],
        in_specs=vmem(4),
        out_specs=vmem(2),
        compiler_params=pltpu.CompilerParams(vmem_limit_bytes=LIMIT),
        cost_estimate=cost(own, own_side),
    )(own, own_side, share, from_near)
    return jnp.swapaxes(out, 0, 1), summed


def band_kernel(aux, pairs, summed, own, total, from_y, from_near, from_far, from_mate, from_y_other, band, made, sems):
    depth, width = pairs.shape[1], band.shape[1]
    me, core, _, odd, _, _, _, f_near = place_of_device()
    count = lax.axis_size("basis")
    sign, cross = 1 - 2 * odd, 1 - 2 * core
    copies = []

    def put(ahead, value):
        far = jnp.abs(ahead)
        slot = len(copies)
        if slot == 0:
            made[slot] = value
        else:
            lower = summed[0, aux + jnp.maximum(me - far, 0) * depth + far - 1] > 0.5
            upper = pairs[0, far - 1] == 1
            there = jnp.logical_or(jnp.logical_and(ahead > 0, upper), jnp.logical_and(ahead < 0, lower))
            there = jnp.logical_and(there, jnp.logical_and(me + ahead >= 0, me + ahead < count))
            made[slot] = jnp.where(there, value, 0.0)
        copies.append(pltpu.make_async_copy(made.at[slot], band.at[depth + ahead], sems.at[slot]))
        copies[-1].start()

    block = lambda ref, i: ref[i * width:(i + 1) * width, :].astype(F32)
    from_f = lambda i: jnp.where(f_near, block(from_far, i), block(from_near, i))
    from_g = lambda i: jnp.where(f_near, block(from_near, i), block(from_far, i))
    put(0, own[0])
    put(cross, own[1])
    put(2 * sign, total[XY] + block(from_y, 0))
    put(2 * sign + cross, from_mate[0] + block(from_y, 1))
    put(-2 * sign, block(from_y, 2) + from_f(2))
    put(-2 * sign + cross, block(from_y_other, 0) + from_f(3))
    put(4 * sign, total[XF] + from_g(0))
    put(-4 * sign, total[XG] + from_f(0))
    put(-3 * cross, from_mate[1] + from_f(1) + from_g(1))
    for copy in copies:
        copy.wait()


def finish(aux, pairs, summed, own, *partials):
    depth, width = pairs.shape[1], own.shape[-1]
    size = 2 * depth + 1
    return pl.pallas_call(
        functools.partial(band_kernel, aux),
        out_shape=squares(size, width),
        in_specs=smem(2) + vmem(1 + len(partials)),
        out_specs=pl.BlockSpec(memory_space=pl.ANY),
        scratch_shapes=[pltpu.VMEM((size, width, width), F32), pltpu.SemaphoreType.DMA((size,))],
        compiler_params=pltpu.CompilerParams(vmem_limit_bytes=LIMIT),
        cost_estimate=cost(own, *partials),
    )(pairs, summed, own, *partials)


def add_kernel(*refs):
    refs[-1][...] = sum(share[...] for share in refs[:-1])


def added(shares):
    return pl.pallas_call(
        add_kernel,
        out_shape=jax.ShapeDtypeStruct(shares[0].shape, F32),
        in_specs=vmem(len(shares)),
        out_specs=vmem(1)[0],
        compiler_params=pltpu.CompilerParams(vmem_limit_bytes=LIMIT),
        cost_estimate=cost(*shares),
    )(*shares)


def shares_of(values, count, step):
    return [values, lax.ppermute(values, "basis", [(i, i ^ step) for i in range(count)])]


def per_device(factors, coefs, domains, pairs):
    own = factors[0]
    _, aux, _ = own.shape
    count = lax.axis_size("basis")

    swap = chip_route(count, lambda c: c, swap=True)
    across = chip_route(count, lambda c: c ^ 1)
    to_near = chip_route(count, lambda c: c ^ 2)
    to_far = chip_route(count, lambda c: c - 2 if c & 2 == 0 else c + 2)
    senders = {source for source, _ in to_far}
    to_far += [(i, i ^ 1) for i in range(count) if i not in senders]
    send = lambda value, route: lax.ppermute(value, "basis", route)

    xo = send(own, swap)
    early, late, for_near, for_far, xj, xj_side = cut(own)
    yj = send(early, across), send(late, across)
    near, far = send(for_near, to_near), send(for_far, to_far)
    own_pairs, share, table = own_products(domains, pairs, xj, xj_side, xo, coefs[0])
    share = added(shares_of(share, count, 1))
    part, _ = relay(yj[0], (yj[0].shape[1],), [share])
    yo = [send(part, swap)]
    first = LATE // 32 * 16 + LATE % 32
    *parts, share = relay(yj[1], (first, LATE - first), shares_of(share, count, 2), *yo)
    yo += [send(part, swap) for part in parts]
    shares, step = [share], 8
    while step < count:
        if len(shares) > 1:
            shares = [added(shares)]
        shares = shares_of(shares[0], count, step)
        step *= 2
    total = shared_products(table, xj, xj_side, xo, near, far, *yj, *yo)
    for_near, for_far, for_mate, for_y, for_y_other, share = messages(total, shares)
    from_near, from_far = send(for_near, to_near), send(for_far, to_far)
    from_y, from_y_other = send(for_y, across), send(for_y_other, chip_route(count, lambda c: c ^ 1, swap=True))
    from_mate = send(for_mate, swap)
    coulomb_half, summed = coulomb(xj, xj_side, share, from_near)
    band = finish(aux, pairs, summed, own_pairs, total, from_y, from_near, from_far, from_mate, from_y_other)
    return (band[None], coulomb_half)


def solution(mesh):
    placed = (
        P(("groups", "basis"), None, None, None),
        P(("groups", "basis"), None, None),
        P("groups", None),
        P(("groups", "basis"), None),
    )
    return jax.shard_map(
        per_device,
        mesh=mesh,
        in_specs=placed,
        out_specs=(P(("groups", "basis"), None, None, None), P(("groups", "basis"), None, None)),
        check_vma=False,
    )
```

```python
import functools

import jax
import jax.numpy as jnp
from jax import lax
from jax.experimental import pallas as pl
from jax.experimental.pallas import tpu as pltpu
from jax.sharding import PartitionSpec as P

F32 = jnp.float32
BF16 = jnp.bfloat16

XJ, XO, XJ_SIDE, YJ, YO, FJ, GJ = range(7)
XF, YF, YOF, XG, XY, XYO, CROSS, OWN = range(8)
PRODUCTS = ((XJ, FJ), (YJ, FJ), (YO, FJ), (XJ_SIDE, GJ), (XJ, YJ), (XO, YJ), (XO, None), (XJ, XO))
SHARED = (XF, YF, YOF, XG, XY, XYO, CROSS)
STACK, SHORT_STACK, OWN_STACK = 10, 8, 4
LIMIT = 12 * 2**20
LATE = 144


def cost(*arrays):
    return pl.CostEstimate(flops=1, bytes_accessed=sum(a.size * a.dtype.itemsize for a in arrays), transcendentals=0)


def smem(n):
    return [pl.BlockSpec(memory_space=pltpu.SMEM)] * n


def vmem(n):
    return [pl.BlockSpec(memory_space=pltpu.VMEM)] * n


def squares(n, width):
    return jax.ShapeDtypeStruct((n, width, width), F32)


def multiply(left, right):
    return lax.dot_general(left, right, (((0,), (0,)), ((), ())), preferred_element_type=F32)


def chip_route(count, target, swap=False):
    chips = count // 2
    route = []
    for chip in range(chips):
        to = target(chip)
        if 0 <= to < chips:
            for core in range(2):
                route.append((2 * chip + core, 2 * to + (1 - core if swap else core)))
    return route


def place_of_device():
    me = lax.axis_index("basis")
    core, chip = me & 1, me >> 1
    odd = chip & 1
    return me, core, chip, odd, core == odd, chip + 2 - 4 * odd, chip - 2 + 4 * odd, odd == ((chip >> 1) & 1)


def cut_kernel(size, own, early, late, near, far, main, side, sems):
    _, _, _, odd, _, _, _, f_near = place_of_device()
    side_start, main_start = (1 - odd) * size, odd * size
    near_start, far_start = jnp.where(f_near, side_start, main_start), jnp.where(f_near, main_start, side_start)
    outs = (early, late, near, far, main, side)
    starts = (side_start, side_start + size - LATE, near_start, far_start, main_start, side_start)
    copies = []
    for i, (out, start) in enumerate(zip(outs, starts)):
        rows = pl.ds(pl.multiple_of(start, 16), out.shape[1])
        copies.append(pltpu.make_async_copy(own.at[:, rows, :], out, sems.at[i]))
    for copy in copies:
        copy.start()
    for copy in copies:
        copy.wait()


def cut(own):
    rows, aux, width = own.shape
    half = aux // 2
    sizes = (half - LATE, LATE, half, half, half, half)
    return pl.pallas_call(
        functools.partial(cut_kernel, half),
        out_shape=[jax.ShapeDtypeStruct((rows, size, width), own.dtype) for size in sizes],
        in_specs=vmem(1),
        out_specs=vmem(6),
        scratch_shapes=[pltpu.SemaphoreType.DMA((6,))],
        compiler_params=pltpu.CompilerParams(vmem_limit_bytes=LIMIT),
        cost_estimate=cost(own, own),
    )(own)


def lists_of(table):
    width = table.shape[1] // 2 - 4
    return lambda q: table[q, 2 * width], lambda q, slot: table[q, slot], lambda q, slot: table[q, width + slot]


def find_matches(domains, table, spot):
    count, rows = domains.shape
    width = table.shape[1] // 2 - 4
    _, core, chip, _, flag, f_chip, g_chip, _ = place_of_device()
    mine_first, other_first = (chip, core), (chip, 1 - core)
    block = {XJ: mine_first, XJ_SIDE: mine_first, XO: other_first, None: (jnp.where(flag, f_chip, g_chip), core)}
    block |= {YJ: (chip ^ 1, core), YO: (chip ^ 1, 1 - core), FJ: (f_chip, core), GJ: (g_chip, core)}

    for q, (left, right) in enumerate(PRODUCTS):
        there, ids = [], []
        for name in (left, right):
            at, one = block[name]
            there.append(jnp.logical_and(at >= 0, 2 * at < count))
            ids.append(2 * jnp.clip(at, 0, count // 2 - 1) + one)
        both = jnp.logical_and(*there)
        base = 2 * ids[1]

        def clear(i, carry):
            spot[i] = -1
            return carry

        def fill(row, carry):
            spot[domains[ids[1], row] - base] = row
            return carry

        def clean(slot, carry):
            table[q, slot] = 0
            table[q, width + slot] = 0
            return carry

        def scan(row, found):
            away = domains[ids[0], row] - base
            inside = jnp.logical_and(away >= 0, away < 2 * rows)
            other_row = spot[jnp.clip(away, 0, 2 * rows - 1)]
            hit = jnp.logical_and(jnp.logical_and(inside, both), other_row >= 0)
            table[q, found] = row
            table[q, width + found] = jnp.maximum(other_row, 0)
            return found + hit.astype(jnp.int32)

        lax.fori_loop(0, 2 * rows, clear, 0, unroll=10)
        lax.fori_loop(0, rows, fill, 0, unroll=10)
        lax.fori_loop(0, width, clean, 0, unroll=9)
        table[q, 2 * width] = lax.fori_loop(0, rows, scan, 0, unroll=5)


def own_kernel(domains, pairs, own, own_side, other, coef, out, share, table, spot):
    rows, half, width = own.shape
    me, _, _, odd, _, _, _, _ = place_of_device()
    find_matches(domains, table, spot)
    number, mine, theirs = lists_of(table)
    out[...] = jnp.zeros_like(out)
    size = max(n for n in range(1, 11) if rows % n == 0)

    def square(step, carry):
        for part in (own, own_side):
            left = part[pl.ds(size * step, size)].reshape(size * half, width)
            out[0] += multiply(left, left)
        return carry

    lax.fori_loop(0, rows // size, square, 0)

    def beside(step, carry):
        lefts, rights = [], []
        for i in range(OWN_STACK):
            slot = OWN_STACK * step + i
            for part, start in ((own, odd * half), (own_side, (1 - odd) * half)):
                left = part[mine(OWN, slot)]
                lefts.append(jnp.where(slot < number(OWN), left, jnp.zeros_like(left)))
                rights.append(other[theirs(OWN, slot), pl.ds(pl.multiple_of(start, 16), half), :])
        out[1] += multiply(jnp.concatenate(lefts, axis=0), jnp.concatenate(rights, axis=0))
        return carry

    lax.fori_loop(0, (number(OWN) + OWN_STACK - 1) // OWN_STACK, beside, 0)

    tile = 128
    parts = []
    for part in (own, own_side):
        sums = []
        for start in range(0, half, tile):
            total = jnp.zeros((tile, width), F32)
            for row in range(rows):
                total += part[row, start:start + tile, :].astype(F32) * coef[row:row + 1, :].astype(F32)
            sums.append(jnp.sum(total.T, axis=0, keepdims=True))
        parts.append(jnp.concatenate(sums, axis=1))
    share[:, :half] = jnp.where(odd == 1, parts[1], parts[0])
    share[:, half:2 * half] = jnp.where(odd == 1, parts[0], parts[1])
    depth = pairs.shape[1]
    lane = lax.broadcasted_iota(jnp.int32, (1, share.shape[1] - 2 * half), 1)
    marks = jnp.zeros(lane.shape, F32)
    for r in range(depth):
        marks = jnp.where(lane == me * depth + r, pairs[0, r].astype(F32), marks)
    share[:, 2 * half:] = marks


def own_products(domains, pairs, own, own_side, other, coef):
    rows, half, width = own.shape
    count = domains.shape[0]
    marks = -(-count * pairs.shape[1] // 128) * 128
    most = max(-(-rows // n) * n for n in (STACK, OWN_STACK))
    table = jax.ShapeDtypeStruct((len(PRODUCTS), 2 * most + 8), jnp.int32)
    return pl.pallas_call(
        own_kernel,
        out_shape=[
            squares(2, width),
            jax.ShapeDtypeStruct((1, 2 * half + marks), F32),
            table,
        ],
        in_specs=smem(2) + vmem(4),
        out_specs=vmem(2) + smem(1),
        scratch_shapes=[pltpu.SMEM((2 * rows,), jnp.int32)],
        compiler_params=pltpu.CompilerParams(vmem_limit_bytes=LIMIT),
        cost_estimate=cost(own, own_side, other),
    )(domains, pairs, own, own_side, other, coef)


def relay_kernel(count, parts, value, *refs):
    shares, (*outs, total, sems) = refs[:count], refs[-parts - 2:]
    copies, start = [], 0
    for i, out in enumerate(outs):
        size = out.shape[1]
        copies.append(pltpu.make_async_copy(value.at[:, start:start + size, :], out, sems.at[i]))
        start += size
    for copy in copies:
        copy.start()
    total[...] = sum(share[...] for share in shares)
    for copy in copies:
        copy.wait()


def relay(value, sizes, shares, *earlier):
    rows, _, width = value.shape
    parts = len(sizes)
    return pl.pallas_call(
        functools.partial(relay_kernel, len(shares), parts),
        out_shape=[jax.ShapeDtypeStruct((rows, size, width), value.dtype) for size in sizes] + [jax.ShapeDtypeStruct(shares[0].shape, F32)],
        in_specs=vmem(1 + len(shares) + len(earlier)),
        out_specs=vmem(parts + 1),
        scratch_shapes=[pltpu.SemaphoreType.DMA((parts,))],
        compiler_params=pltpu.CompilerParams(vmem_limit_bytes=LIMIT),
        cost_estimate=cost(value, value),
    )(value, *shares, *earlier)


def rows_product(table, q, first, size, left_of, right_of):
    number, mine, theirs = lists_of(table)
    lefts, rights = [], []
    for i in range(size):
        slot = first + i
        left = left_of(mine(q, slot))
        lefts.append(jnp.where(slot < number(q), left, jnp.zeros_like(left)))
        rights.append(right_of(theirs(q, slot)))
    return multiply(jnp.concatenate(lefts, axis=0), jnp.concatenate(rights, axis=0))


def early_kernel(table, xj, xo, yj, total):
    odd, (half, size) = place_of_device()[3], (xj.shape[1], yj.shape[1])
    main = pl.ds(pl.multiple_of(odd * half, 16), size)
    lefts = lambda row: xj[row, :size, :], lambda row: xo[row, main, :]
    number, _, _ = lists_of(table)
    for at, q in enumerate((XY, XYO)):
        total[at] = jnp.zeros(total.shape[1:], F32)

        def step(group, carry, at=at, q=q):
            total[at] += rows_product(table, q, group * STACK, STACK, lefts[at], lambda row: yj[row])
            return carry

        lax.fori_loop(0, (number(q) + STACK - 1) // STACK, step, 0)


def early_products(table, xj, xo, yj):
    return pl.pallas_call(
        early_kernel,
        out_shape=squares(2, xj.shape[-1]),
        in_specs=smem(1) + vmem(3),
        out_specs=vmem(1)[0],
        compiler_params=pltpu.CompilerParams(vmem_limit_bytes=2 * LIMIT),
        cost_estimate=cost(xj, xo, yj),
    )(table, xj, xo, yj)


def shared_kernel(table, xj, xj_side, xo, near, far, early, *refs):
    yj, yo, total = refs[:2], refs[2:-1], refs[-1]
    _, _, _, odd, flag, _, _, f_near = place_of_device()
    half, done = xj.shape[1], yj[0].shape[1]
    number, _, _ = lists_of(table)
    late = pl.ds(pl.multiple_of(odd * half + done, 16), half - done)
    cross = pl.ds(pl.multiple_of(jnp.where(flag, odd, 1 - odd) * half, 16), half)
    joined = lambda parts: lambda row: jnp.concatenate([part[row] for part in parts], axis=0)

    def product(q, first, size, block):
        left_of, right_of = {
            XF: (lambda row: xj[row], lambda row: block[FJ][row]),
            YF: (joined(yj), lambda row: block[FJ][row]),
            YOF: (joined(yo), lambda row: block[FJ][row]),
            XG: (lambda row: xj_side[row], lambda row: block[GJ][row]),
            XY: (lambda row: xj[row, done:, :], lambda row: yj[1][row]),
            XYO: (lambda row: xo[row, late, :], lambda row: yj[1][row]),
            CROSS: (lambda row: xo[row, cross, :], lambda row: jnp.where(flag, block[FJ][row], block[GJ][row])),
        }[q]
        return rows_product(table, q, first, size, left_of, right_of)

    def all_products(fj, gj):
        block = {FJ: fj, GJ: gj}
        most = number(SHARED[0])
        for at, q in enumerate(SHARED):
            most = jnp.maximum(most, number(q))
            total[at] = product(q, 0, STACK, block)
            if q in (XY, XYO):
                total[at] += early[(XY, XYO).index(q)]

        def steps(size):
            def step(i, carry):
                for at, q in enumerate(SHARED):
                    total[at] += product(q, STACK + i * size, size, block)
                return carry

            return step

        short = most <= STACK + SHORT_STACK
        more = jnp.maximum(most - STACK, 0)
        lax.fori_loop(0, jnp.where(short, jnp.minimum(more, 1), 0), steps(SHORT_STACK), 0)
        lax.fori_loop(0, jnp.where(short, 0, (more + STACK - 1) // STACK), steps(STACK), 0)

    @pl.when(f_near)
    def _():
        all_products(near, far)

    @pl.when(jnp.logical_not(f_near))
    def _():
        all_products(far, near)


def shared_products(table, *blocks):
    return pl.pallas_call(
        shared_kernel,
        out_shape=squares(len(SHARED), blocks[0].shape[-1]),
        in_specs=smem(1) + vmem(len(blocks)),
        out_specs=vmem(1)[0],
        compiler_params=pltpu.CompilerParams(vmem_limit_bytes=2 * LIMIT),
        cost_estimate=cost(*blocks),
    )(table, *blocks)


def message_kernel(total, *refs):
    shares, (to_near, to_far, to_mate, to_y, to_y_other, summed) = refs[:-6], refs[-6:]
    _, _, _, _, flag, _, _, f_near = place_of_device()
    width = total.shape[1]

    def put(out, values):
        for i, value in enumerate(values):
            out[i * width:(i + 1) * width, :] = value.astype(BF16)

    def to_f_and_g(to_f, to_g):
        cross = total[CROSS].T
        nothing = jnp.zeros_like(cross)
        put(to_f, (total[XF].T, jnp.where(flag, cross, nothing), total[YF].T, total[YOF].T))
        put(to_g, (total[XG].T, jnp.where(flag, nothing, cross), nothing, nothing))

    @pl.when(f_near)
    def _():
        to_f_and_g(to_near, to_far)

    @pl.when(jnp.logical_not(f_near))
    def _():
        to_f_and_g(to_far, to_near)

    put(to_y, (total[XY].T, total[XYO].T, total[YF]))
    to_y[3 * width:, :] = jnp.zeros((to_y.shape[0] - 3 * width, width), BF16)
    put(to_y_other, (total[YOF],))
    to_mate[0] = total[XYO]
    to_mate[1] = total[CROSS]
    gathered = sum(share[...] for share in shares)
    summed[...] = gathered
    lines = gathered.shape[1] // width
    rest, rows = gathered, []
    for _ in range(3):
        part = rest.astype(BF16)
        rest = rest - part.astype(F32)
        rows += [part[:, i * width:(i + 1) * width].astype(F32) for i in range(lines)]
    rows.append(jnp.zeros((to_near.shape[0] - 4 * width - 3 * lines, width), F32))
    to_near[4 * width:, :] = jnp.concatenate(rows, axis=0).astype(BF16)


def messages(total, shares):
    width = total.shape[-1]
    lines = -(-3 * shares[0].shape[1] // width // 16) * 16
    flat = jax.ShapeDtypeStruct
    sent = lambda rows: flat((rows, width), BF16)
    return pl.pallas_call(
        message_kernel,
        out_shape=[
            sent(4 * width + lines + 16), sent(4 * width), squares(2, width), sent(4 * width + 16), sent(width),
            flat(shares[0].shape, F32),
        ],
        in_specs=vmem(1 + len(shares)),
        out_specs=vmem(6),
        compiler_params=pltpu.CompilerParams(vmem_limit_bytes=LIMIT),
        cost_estimate=cost(total, total),
    )(total, *shares)


def coulomb_kernel(own, own_side, share, from_near, out, summed):
    rows, half, width = own.shape
    odd = place_of_device()[3]
    lines = share.shape[1] // width
    parts = from_near[4 * width:, :].astype(F32)
    line = lambda i: jnp.concatenate([parts[i * lines + j:i * lines + j + 1] for j in range(lines)], axis=1)
    gathered = share[...] + (line(0) + line(1) + line(2))
    summed[...] = gathered
    low, high = gathered[:, :half], gathered[:, half:2 * half]
    gamma = jnp.where(odd == 1, high, low).astype(BF16)
    side_gamma = jnp.where(odd == 1, low, high).astype(BF16)
    for row in range(rows):
        part = jnp.dot(gamma, own[row], preferred_element_type=F32)
        out[row] = part + jnp.dot(side_gamma, own_side[row], preferred_element_type=F32)


def coulomb(own, own_side, share, from_near):
    rows, _, width = own.shape
    flat = jax.ShapeDtypeStruct
    out, summed = pl.pallas_call(
        coulomb_kernel,
        out_shape=[flat((rows, 1, width), F32), flat(share.shape, F32)],
        in_specs=vmem(4),
        out_specs=vmem(2),
        compiler_params=pltpu.CompilerParams(vmem_limit_bytes=LIMIT),
        cost_estimate=cost(own, own_side),
    )(own, own_side, share, from_near)
    return jnp.swapaxes(out, 0, 1), summed


def band_kernel(aux, pairs, summed, own, total, from_y, from_near, from_far, from_mate, from_y_other, band, made, sems):
    depth, width = pairs.shape[1], band.shape[1]
    me, core, _, odd, _, _, _, f_near = place_of_device()
    count = lax.axis_size("basis")
    sign, cross = 1 - 2 * odd, 1 - 2 * core
    copies = []

    def put(ahead, value):
        far = jnp.abs(ahead)
        slot = len(copies)
        if slot == 0:
            made[slot] = value
        else:
            lower = summed[0, aux + jnp.maximum(me - far, 0) * depth + far - 1] > 0.5
            upper = pairs[0, far - 1] == 1
            there = jnp.logical_or(jnp.logical_and(ahead > 0, upper), jnp.logical_and(ahead < 0, lower))
            there = jnp.logical_and(there, jnp.logical_and(me + ahead >= 0, me + ahead < count))
            made[slot] = jnp.where(there, value, 0.0)
        copies.append(pltpu.make_async_copy(made.at[slot], band.at[depth + ahead], sems.at[slot]))
        copies[-1].start()

    block = lambda ref, i: ref[i * width:(i + 1) * width, :].astype(F32)
    from_f = lambda i: jnp.where(f_near, block(from_far, i), block(from_near, i))
    from_g = lambda i: jnp.where(f_near, block(from_near, i), block(from_far, i))
    put(0, own[0])
    put(cross, own[1])
    put(2 * sign, total[XY] + block(from_y, 0))
    put(2 * sign + cross, from_mate[0] + block(from_y, 1))
    put(-2 * sign, block(from_y, 2) + from_f(2))
    put(-2 * sign + cross, block(from_y_other, 0) + from_f(3))
    put(4 * sign, total[XF] + from_g(0))
    put(-4 * sign, total[XG] + from_f(0))
    put(-3 * cross, from_mate[1] + from_f(1) + from_g(1))
    for copy in copies:
        copy.wait()


def finish(aux, pairs, summed, own, *partials):
    depth, width = pairs.shape[1], own.shape[-1]
    size = 2 * depth + 1
    return pl.pallas_call(
        functools.partial(band_kernel, aux),
        out_shape=squares(size, width),
        in_specs=smem(2) + vmem(1 + len(partials)),
        out_specs=pl.BlockSpec(memory_space=pl.ANY),
        scratch_shapes=[pltpu.VMEM((size, width, width), F32), pltpu.SemaphoreType.DMA((size,))],
        compiler_params=pltpu.CompilerParams(vmem_limit_bytes=LIMIT),
        cost_estimate=cost(own, *partials),
    )(pairs, summed, own, *partials)


def add_kernel(*refs):
    refs[-1][...] = sum(share[...] for share in refs[:-1])


def added(shares):
    return pl.pallas_call(
        add_kernel,
        out_shape=jax.ShapeDtypeStruct(shares[0].shape, F32),
        in_specs=vmem(len(shares)),
        out_specs=vmem(1)[0],
        compiler_params=pltpu.CompilerParams(vmem_limit_bytes=LIMIT),
        cost_estimate=cost(*shares),
    )(*shares)


def shares_of(values, count, step):
    return [values, lax.ppermute(values, "basis", [(i, i ^ step) for i in range(count)])]


def per_device(factors, coefs, domains, pairs):
    own = factors[0]
    _, aux, _ = own.shape
    count = lax.axis_size("basis")

    swap = chip_route(count, lambda c: c, swap=True)
    across = chip_route(count, lambda c: c ^ 1)
    to_near = chip_route(count, lambda c: c ^ 2)
    to_far = chip_route(count, lambda c: c - 2 if c & 2 == 0 else c + 2)
    senders = {source for source, _ in to_far}
    to_far += [(i, i ^ 1) for i in range(count) if i not in senders]
    send = lambda value, route: lax.ppermute(value, "basis", route)

    xo = send(own, swap)
    early, late, for_near, for_far, xj, xj_side = cut(own)
    yj = send(early, across), send(late, across)
    near, far = send(for_near, to_near), send(for_far, to_far)
    own_pairs, share, table = own_products(domains, pairs, xj, xj_side, xo, coefs[0])
    share = added(shares_of(share, count, 1))
    with_y = early_products(table, xj, xo, yj[0])
    part, _ = relay(yj[0], (yj[0].shape[1],), [share])
    yo = [send(part, swap)]
    first = LATE // 32 * 16 + LATE % 32
    *parts, share = relay(yj[1], (first, LATE - first), shares_of(share, count, 2), with_y, *yo)
    yo += [send(part, swap) for part in parts]
    shares, step = [share], 8
    while step < count:
        if len(shares) > 1:
            shares = [added(shares)]
        shares = shares_of(shares[0], count, step)
        step *= 2
    total = shared_products(table, xj, xj_side, xo, near, far, with_y, *yj, *yo)
    for_near, for_far, for_mate, for_y, for_y_other, share = messages(total, shares)
    from_near, from_far = send(for_near, to_near), send(for_far, to_far)
    from_y, from_y_other = send(for_y, across), send(for_y_other, chip_route(count, lambda c: c ^ 1, swap=True))
    from_mate = send(for_mate, swap)
    coulomb_half, summed = coulomb(xj, xj_side, share, from_near)
    band = finish(aux, pairs, summed, own_pairs, total, from_y, from_near, from_far, from_mate, from_y_other)
    return (band[None], coulomb_half)


def solution(mesh):
    placed = (
        P(("groups", "basis"), None, None, None),
        P(("groups", "basis"), None, None),
        P("groups", None),
        P(("groups", "basis"), None),
    )
    return jax.shard_map(
        per_device,
        mesh=mesh,
        in_specs=placed,
        out_specs=(P(("groups", "basis"), None, None, None), P(("groups", "basis"), None, None)),
        check_vma=False,
    )
```

```python
import functools

import jax
import jax.numpy as jnp
from jax import lax
from jax.experimental import pallas as pl
from jax.experimental.pallas import tpu as pltpu
from jax.sharding import PartitionSpec as P

F32 = jnp.float32
BF16 = jnp.bfloat16

XJ, XO, XJ_SIDE, YJ, YO, FJ, GJ = range(7)
XF, YF, YOF, XG, XY, XYO, CROSS, OWN = range(8)
PRODUCTS = ((XJ, FJ), (YJ, FJ), (YO, FJ), (XJ_SIDE, GJ), (XJ, YJ), (XO, YJ), (XO, None), (XJ, XO))
SHARED = (XF, YF, YOF, XG, XY, XYO, CROSS)
STACK, SHORT_STACK, OWN_STACK = 10, 8, 4
LIMIT = 12 * 2**20
LATE = 144


def cost(*arrays):
    return pl.CostEstimate(flops=1, bytes_accessed=sum(a.size * a.dtype.itemsize for a in arrays), transcendentals=0)


def smem(n):
    return [pl.BlockSpec(memory_space=pltpu.SMEM)] * n


def vmem(n):
    return [pl.BlockSpec(memory_space=pltpu.VMEM)] * n


def squares(n, width):
    return jax.ShapeDtypeStruct((n, width, width), F32)


def multiply(left, right):
    return lax.dot_general(left, right, (((0,), (0,)), ((), ())), preferred_element_type=F32)


def chip_route(count, target, swap=False):
    chips = count // 2
    route = []
    for chip in range(chips):
        to = target(chip)
        if 0 <= to < chips:
            for core in range(2):
                route.append((2 * chip + core, 2 * to + (1 - core if swap else core)))
    return route


def place_of_device():
    me = lax.axis_index("basis")
    core, chip = me & 1, me >> 1
    odd = chip & 1
    return me, core, chip, odd, core == odd, chip + 2 - 4 * odd, chip - 2 + 4 * odd, odd == ((chip >> 1) & 1)


def cut_kernel(size, wanted, own, *refs):
    outs, sems = refs[:-1], refs[-1]
    _, _, _, odd, _, _, _, f_near = place_of_device()
    side, main = (1 - odd) * size, odd * size
    near, far = jnp.where(f_near, side, main), jnp.where(f_near, main, side)
    starts = (side, side + size - LATE, near, far, main, side)
    copies = []
    for i, (out, at) in enumerate(zip(outs, wanted)):
        rows = pl.ds(pl.multiple_of(starts[at], 16), out.shape[1])
        copies.append(pltpu.make_async_copy(own.at[:, rows, :], out, sems.at[i]))
    for copy in copies:
        copy.start()
    for copy in copies:
        copy.wait()


def cut(own, wanted):
    rows, aux, width = own.shape
    half = aux // 2
    sizes = (half - LATE, LATE, half, half, half, half)
    return pl.pallas_call(
        functools.partial(cut_kernel, half, wanted),
        out_shape=[jax.ShapeDtypeStruct((rows, sizes[at], width), own.dtype) for at in wanted],
        in_specs=vmem(1),
        out_specs=vmem(len(wanted)),
        scratch_shapes=[pltpu.SemaphoreType.DMA((len(wanted),))],
        compiler_params=pltpu.CompilerParams(vmem_limit_bytes=LIMIT),
        cost_estimate=cost(own, own),
    )(own)


def lists_of(table):
    width = table.shape[1] // 2 - 4
    return lambda q: table[q, 2 * width], lambda q, slot: table[q, slot], lambda q, slot: table[q, width + slot]


def find_matches(domains, table, spot):
    count, rows = domains.shape
    width = table.shape[1] // 2 - 4
    _, core, chip, _, flag, f_chip, g_chip, _ = place_of_device()
    mine_first, other_first = (chip, core), (chip, 1 - core)
    block = {XJ: mine_first, XJ_SIDE: mine_first, XO: other_first, None: (jnp.where(flag, f_chip, g_chip), core)}
    block |= {YJ: (chip ^ 1, core), YO: (chip ^ 1, 1 - core), FJ: (f_chip, core), GJ: (g_chip, core)}

    for q, (left, right) in enumerate(PRODUCTS):
        there, ids = [], []
        for name in (left, right):
            at, one = block[name]
            there.append(jnp.logical_and(at >= 0, 2 * at < count))
            ids.append(2 * jnp.clip(at, 0, count // 2 - 1) + one)
        both = jnp.logical_and(*there)
        base = 2 * ids[1]

        def clear(i, carry):
            spot[i] = -1
            return carry

        def fill(row, carry):
            spot[domains[ids[1], row] - base] = row
            return carry

        def clean(slot, carry):
            table[q, slot] = 0
            table[q, width + slot] = 0
            return carry

        def scan(row, found):
            away = domains[ids[0], row] - base
            inside = jnp.logical_and(away >= 0, away < 2 * rows)
            other_row = spot[jnp.clip(away, 0, 2 * rows - 1)]
            hit = jnp.logical_and(jnp.logical_and(inside, both), other_row >= 0)
            table[q, found] = row
            table[q, width + found] = jnp.maximum(other_row, 0)
            return found + hit.astype(jnp.int32)

        lax.fori_loop(0, 2 * rows, clear, 0, unroll=10)
        lax.fori_loop(0, rows, fill, 0, unroll=10)
        lax.fori_loop(0, width, clean, 0, unroll=9)
        table[q, 2 * width] = lax.fori_loop(0, rows, scan, 0, unroll=5)


def own_kernel(domains, pairs, own, own_side, other, coef, out, share, table, spot):
    rows, half, width = own.shape
    me, _, _, odd, _, _, _, _ = place_of_device()
    find_matches(domains, table, spot)
    number, mine, theirs = lists_of(table)
    out[...] = jnp.zeros_like(out)
    size = max(n for n in range(1, 11) if rows % n == 0)

    def square(step, carry):
        for part in (own, own_side):
            left = part[pl.ds(size * step, size)].reshape(size * half, width)
            out[0] += multiply(left, left)
        return carry

    lax.fori_loop(0, rows // size, square, 0)

    def beside(step, carry):
        lefts, rights = [], []
        for i in range(OWN_STACK):
            slot = OWN_STACK * step + i
            for part, start in ((own, odd * half), (own_side, (1 - odd) * half)):
                left = part[mine(OWN, slot)]
                lefts.append(jnp.where(slot < number(OWN), left, jnp.zeros_like(left)))
                rights.append(other[theirs(OWN, slot), pl.ds(pl.multiple_of(start, 16), half), :])
        out[1] += multiply(jnp.concatenate(lefts, axis=0), jnp.concatenate(rights, axis=0))
        return carry

    lax.fori_loop(0, (number(OWN) + OWN_STACK - 1) // OWN_STACK, beside, 0)

    tile = 128
    parts = []
    for part in (own, own_side):
        sums = []
        for start in range(0, half, tile):
            total = jnp.zeros((tile, width), F32)
            for row in range(rows):
                total += part[row, start:start + tile, :].astype(F32) * coef[row:row + 1, :].astype(F32)
            sums.append(jnp.sum(total.T, axis=0, keepdims=True))
        parts.append(jnp.concatenate(sums, axis=1))
    share[:, :half] = jnp.where(odd == 1, parts[1], parts[0])
    share[:, half:2 * half] = jnp.where(odd == 1, parts[0], parts[1])
    depth = pairs.shape[1]
    lane = lax.broadcasted_iota(jnp.int32, (1, share.shape[1] - 2 * half), 1)
    marks = jnp.zeros(lane.shape, F32)
    for r in range(depth):
        marks = jnp.where(lane == me * depth + r, pairs[0, r].astype(F32), marks)
    share[:, 2 * half:] = marks


def own_products(domains, pairs, own, own_side, other, coef):
    rows, half, width = own.shape
    count = domains.shape[0]
    marks = -(-count * pairs.shape[1] // 128) * 128
    most = max(-(-rows // n) * n for n in (STACK, OWN_STACK))
    table = jax.ShapeDtypeStruct((len(PRODUCTS), 2 * most + 8), jnp.int32)
    return pl.pallas_call(
        own_kernel,
        out_shape=[
            squares(2, width),
            jax.ShapeDtypeStruct((1, 2 * half + marks), F32),
            table,
        ],
        in_specs=smem(2) + vmem(4),
        out_specs=vmem(2) + smem(1),
        scratch_shapes=[pltpu.SMEM((2 * rows,), jnp.int32)],
        compiler_params=pltpu.CompilerParams(vmem_limit_bytes=LIMIT),
        cost_estimate=cost(own, own_side, other),
    )(domains, pairs, own, own_side, other, coef)


def relay_kernel(count, parts, value, *refs):
    shares, (*outs, total, sems) = refs[:count], refs[-parts - 2:]
    copies, start = [], 0
    for i, out in enumerate(outs):
        size = out.shape[1]
        copies.append(pltpu.make_async_copy(value.at[:, start:start + size, :], out, sems.at[i]))
        start += size
    for copy in copies:
        copy.start()
    total[...] = sum(share[...] for share in shares)
    for copy in copies:
        copy.wait()


def relay(value, sizes, shares, *earlier):
    rows, _, width = value.shape
    parts = len(sizes)
    return pl.pallas_call(
        functools.partial(relay_kernel, len(shares), parts),
        out_shape=[jax.ShapeDtypeStruct((rows, size, width), value.dtype) for size in sizes] + [jax.ShapeDtypeStruct(shares[0].shape, F32)],
        in_specs=vmem(1 + len(shares) + len(earlier)),
        out_specs=vmem(parts + 1),
        scratch_shapes=[pltpu.SemaphoreType.DMA((parts,))],
        compiler_params=pltpu.CompilerParams(vmem_limit_bytes=LIMIT),
        cost_estimate=cost(value, value),
    )(value, *shares, *earlier)


def rows_product(table, q, first, size, left_of, right_of):
    number, mine, theirs = lists_of(table)
    lefts, rights = [], []
    for i in range(size):
        slot = first + i
        left = left_of(mine(q, slot))
        lefts.append(jnp.where(slot < number(q), left, jnp.zeros_like(left)))
        rights.append(right_of(theirs(q, slot)))
    return multiply(jnp.concatenate(lefts, axis=0), jnp.concatenate(rights, axis=0))


def early_kernel(table, xj, xo, yj, total):
    odd, (half, size) = place_of_device()[3], (xj.shape[1], yj.shape[1])
    main = pl.ds(pl.multiple_of(odd * half, 16), size)
    lefts = lambda row: xj[row, :size, :], lambda row: xo[row, main, :]
    number, _, _ = lists_of(table)
    for at, q in enumerate((XY, XYO)):
        total[at] = jnp.zeros(total.shape[1:], F32)

        def step(group, carry, at=at, q=q):
            total[at] += rows_product(table, q, group * STACK, STACK, lefts[at], lambda row: yj[row])
            return carry

        lax.fori_loop(0, (number(q) + STACK - 1) // STACK, step, 0)


def early_products(table, xj, xo, yj):
    return pl.pallas_call(
        early_kernel,
        out_shape=squares(2, xj.shape[-1]),
        in_specs=smem(1) + vmem(3),
        out_specs=vmem(1)[0],
        compiler_params=pltpu.CompilerParams(vmem_limit_bytes=2 * LIMIT),
        cost_estimate=cost(xj, xo, yj),
    )(table, xj, xo, yj)


def shared_kernel(table, xj, xj_side, xo, near, far, early, *refs):
    yj, yo, total = refs[:2], refs[2:-1], refs[-1]
    _, _, _, odd, flag, _, _, f_near = place_of_device()
    half, done = xj.shape[1], yj[0].shape[1]
    number, _, _ = lists_of(table)
    late = pl.ds(pl.multiple_of(odd * half + done, 16), half - done)
    cross = pl.ds(pl.multiple_of(jnp.where(flag, odd, 1 - odd) * half, 16), half)
    joined = lambda parts: lambda row: jnp.concatenate([part[row] for part in parts], axis=0)

    def product(q, first, size, block):
        left_of, right_of = {
            XF: (lambda row: xj[row], lambda row: block[FJ][row]),
            YF: (joined(yj), lambda row: block[FJ][row]),
            YOF: (joined(yo), lambda row: block[FJ][row]),
            XG: (lambda row: xj_side[row], lambda row: block[GJ][row]),
            XY: (lambda row: xj[row, done:, :], lambda row: yj[1][row]),
            XYO: (lambda row: xo[row, late, :], lambda row: yj[1][row]),
            CROSS: (lambda row: xo[row, cross, :], lambda row: jnp.where(flag, block[FJ][row], block[GJ][row])),
        }[q]
        return rows_product(table, q, first, size, left_of, right_of)

    def all_products(fj, gj):
        block = {FJ: fj, GJ: gj}
        most = number(SHARED[0])
        for at, q in enumerate(SHARED):
            most = jnp.maximum(most, number(q))
            total[at] = product(q, 0, STACK, block)
            if q in (XY, XYO):
                total[at] += early[(XY, XYO).index(q)]

        def steps(size):
            def step(i, carry):
                for at, q in enumerate(SHARED):
                    total[at] += product(q, STACK + i * size, size, block)
                return carry

            return step

        short = most <= STACK + SHORT_STACK
        more = jnp.maximum(most - STACK, 0)
        lax.fori_loop(0, jnp.where(short, jnp.minimum(more, 1), 0), steps(SHORT_STACK), 0)
        lax.fori_loop(0, jnp.where(short, 0, (more + STACK - 1) // STACK), steps(STACK), 0)

    @pl.when(f_near)
    def _():
        all_products(near, far)

    @pl.when(jnp.logical_not(f_near))
    def _():
        all_products(far, near)


def shared_products(table, *blocks):
    return pl.pallas_call(
        shared_kernel,
        out_shape=squares(len(SHARED), blocks[0].shape[-1]),
        in_specs=smem(1) + vmem(len(blocks)),
        out_specs=vmem(1)[0],
        compiler_params=pltpu.CompilerParams(vmem_limit_bytes=2 * LIMIT),
        cost_estimate=cost(*blocks),
    )(table, *blocks)


def message_kernel(total, *refs):
    shares, (to_near, to_far, to_mate, to_y, to_y_other, summed) = refs[:-6], refs[-6:]
    _, _, _, _, flag, _, _, f_near = place_of_device()
    width = total.shape[1]

    def put(out, values):
        for i, value in enumerate(values):
            out[i * width:(i + 1) * width, :] = value.astype(BF16)

    def to_f_and_g(to_f, to_g):
        cross = total[CROSS].T
        nothing = jnp.zeros_like(cross)
        put(to_f, (total[XF].T, jnp.where(flag, cross, nothing), total[YF].T, total[YOF].T))
        put(to_g, (total[XG].T, jnp.where(flag, nothing, cross), nothing, nothing))

    @pl.when(f_near)
    def _():
        to_f_and_g(to_near, to_far)

    @pl.when(jnp.logical_not(f_near))
    def _():
        to_f_and_g(to_far, to_near)

    put(to_y, (total[XY].T, total[XYO].T, total[YF]))
    to_y[3 * width:, :] = jnp.zeros((to_y.shape[0] - 3 * width, width), BF16)
    put(to_y_other, (total[YOF],))
    to_mate[0] = total[XYO]
    to_mate[1] = total[CROSS]
    gathered = sum(share[...] for share in shares)
    summed[...] = gathered
    lines = gathered.shape[1] // width
    rest, rows = gathered, []
    for _ in range(3):
        part = rest.astype(BF16)
        rest = rest - part.astype(F32)
        rows += [part[:, i * width:(i + 1) * width].astype(F32) for i in range(lines)]
    rows.append(jnp.zeros((to_near.shape[0] - 4 * width - 3 * lines, width), F32))
    to_near[4 * width:, :] = jnp.concatenate(rows, axis=0).astype(BF16)


def messages(total, shares):
    width = total.shape[-1]
    lines = -(-3 * shares[0].shape[1] // width // 16) * 16
    flat = jax.ShapeDtypeStruct
    sent = lambda rows: flat((rows, width), BF16)
    return pl.pallas_call(
        message_kernel,
        out_shape=[
            sent(4 * width + lines + 16), sent(4 * width), squares(2, width), sent(4 * width + 16), sent(width),
            flat(shares[0].shape, F32),
        ],
        in_specs=vmem(1 + len(shares)),
        out_specs=vmem(6),
        compiler_params=pltpu.CompilerParams(vmem_limit_bytes=LIMIT),
        cost_estimate=cost(total, total),
    )(total, *shares)


def coulomb_kernel(own, own_side, share, from_near, out, summed):
    rows, half, width = own.shape
    odd = place_of_device()[3]
    lines = share.shape[1] // width
    parts = from_near[4 * width:, :].astype(F32)
    line = lambda i: jnp.concatenate([parts[i * lines + j:i * lines + j + 1] for j in range(lines)], axis=1)
    gathered = share[...] + (line(0) + line(1) + line(2))
    summed[...] = gathered
    low, high = gathered[:, :half], gathered[:, half:2 * half]
    gamma = jnp.where(odd == 1, high, low).astype(BF16)
    side_gamma = jnp.where(odd == 1, low, high).astype(BF16)
    for row in range(rows):
        part = jnp.dot(gamma, own[row], preferred_element_type=F32)
        out[row] = part + jnp.dot(side_gamma, own_side[row], preferred_element_type=F32)


def coulomb(own, own_side, share, from_near):
    rows, _, width = own.shape
    flat = jax.ShapeDtypeStruct
    out, summed = pl.pallas_call(
        coulomb_kernel,
        out_shape=[flat((rows, 1, width), F32), flat(share.shape, F32)],
        in_specs=vmem(4),
        out_specs=vmem(2),
        compiler_params=pltpu.CompilerParams(vmem_limit_bytes=LIMIT),
        cost_estimate=cost(own, own_side),
    )(own, own_side, share, from_near)
    return jnp.swapaxes(out, 0, 1), summed


def band_kernel(aux, pairs, summed, own, total, from_y, from_near, from_far, from_mate, from_y_other, band, made, sems):
    depth, width = pairs.shape[1], band.shape[1]
    me, core, _, odd, _, _, _, f_near = place_of_device()
    count = lax.axis_size("basis")
    sign, cross = 1 - 2 * odd, 1 - 2 * core
    copies = []

    def put(ahead, value):
        far = jnp.abs(ahead)
        slot = len(copies)
        if slot == 0:
            made[slot] = value
        else:
            lower = summed[0, aux + jnp.maximum(me - far, 0) * depth + far - 1] > 0.5
            upper = pairs[0, far - 1] == 1
            there = jnp.logical_or(jnp.logical_and(ahead > 0, upper), jnp.logical_and(ahead < 0, lower))
            there = jnp.logical_and(there, jnp.logical_and(me + ahead >= 0, me + ahead < count))
            made[slot] = jnp.where(there, value, 0.0)
        copies.append(pltpu.make_async_copy(made.at[slot], band.at[depth + ahead], sems.at[slot]))
        copies[-1].start()

    block = lambda ref, i: ref[i * width:(i + 1) * width, :].astype(F32)
    from_f = lambda i: jnp.where(f_near, block(from_far, i), block(from_near, i))
    from_g = lambda i: jnp.where(f_near, block(from_near, i), block(from_far, i))
    put(0, own[0])
    put(cross, own[1])
    put(2 * sign, total[XY] + block(from_y, 0))
    put(2 * sign + cross, from_mate[0] + block(from_y, 1))
    put(-2 * sign, block(from_y, 2) + from_f(2))
    put(-2 * sign + cross, block(from_y_other, 0) + from_f(3))
    put(4 * sign, total[XF] + from_g(0))
    put(-4 * sign, total[XG] + from_f(0))
    put(-3 * cross, from_mate[1] + from_f(1) + from_g(1))
    for copy in copies:
        copy.wait()


def finish(aux, pairs, summed, own, *partials):
    depth, width = pairs.shape[1], own.shape[-1]
    size = 2 * depth + 1
    return pl.pallas_call(
        functools.partial(band_kernel, aux),
        out_shape=squares(size, width),
        in_specs=smem(2) + vmem(1 + len(partials)),
        out_specs=pl.BlockSpec(memory_space=pl.ANY),
        scratch_shapes=[pltpu.VMEM((size, width, width), F32), pltpu.SemaphoreType.DMA((size,))],
        compiler_params=pltpu.CompilerParams(vmem_limit_bytes=LIMIT),
        cost_estimate=cost(own, *partials),
    )(pairs, summed, own, *partials)


def add_kernel(*refs):
    refs[-1][...] = sum(share[...] for share in refs[:-1])


def added(shares):
    return pl.pallas_call(
        add_kernel,
        out_shape=jax.ShapeDtypeStruct(shares[0].shape, F32),
        in_specs=vmem(len(shares)),
        out_specs=vmem(1)[0],
        compiler_params=pltpu.CompilerParams(vmem_limit_bytes=LIMIT),
        cost_estimate=cost(*shares),
    )(*shares)


def shares_of(values, count, step):
    return [values, lax.ppermute(values, "basis", [(i, i ^ step) for i in range(count)])]


def per_device(factors, coefs, domains, pairs):
    own = factors[0]
    _, aux, _ = own.shape
    count = lax.axis_size("basis")

    swap = chip_route(count, lambda c: c, swap=True)
    across = chip_route(count, lambda c: c ^ 1)
    to_near = chip_route(count, lambda c: c ^ 2)
    to_far = chip_route(count, lambda c: c - 2 if c & 2 == 0 else c + 2)
    senders = {source for source, _ in to_far}
    to_far += [(i, i ^ 1) for i in range(count) if i not in senders]
    send = lambda value, route: lax.ppermute(value, "basis", route)

    xo = send(own, swap)
    (early,) = cut(own, (0,))
    late, for_near, for_far, xj, xj_side = cut(own, (1, 2, 3, 4, 5))
    yj = send(early, across), send(late, across)
    near, far = send(for_near, to_near), send(for_far, to_far)
    own_pairs, share, table = own_products(domains, pairs, xj, xj_side, xo, coefs[0])
    share = added(shares_of(share, count, 1))
    with_y = early_products(table, xj, xo, yj[0])
    part, _ = relay(yj[0], (yj[0].shape[1],), [share])
    yo = [send(part, swap)]
    first = LATE // 32 * 16 + LATE % 32
    *parts, share = relay(yj[1], (first, LATE - first), shares_of(share, count, 2), with_y, *yo)
    yo += [send(part, swap) for part in parts]
    shares, step = [share], 8
    while step < count:
        if len(shares) > 1:
            shares = [added(shares)]
        shares = shares_of(shares[0], count, step)
        step *= 2
    total = shared_products(table, xj, xj_side, xo, near, far, with_y, *yj, *yo)
    for_near, for_far, for_mate, for_y, for_y_other, share = messages(total, shares)
    from_near, from_far = send(for_near, to_near), send(for_far, to_far)
    from_y, from_y_other = send(for_y, across), send(for_y_other, chip_route(count, lambda c: c ^ 1, swap=True))
    from_mate = send(for_mate, swap)
    coulomb_half, summed = coulomb(xj, xj_side, share, from_near)
    band = finish(aux, pairs, summed, own_pairs, total, from_y, from_near, from_far, from_mate, from_y_other)
    return (band[None], coulomb_half)


def solution(mesh):
    placed = (
        P(("groups", "basis"), None, None, None),
        P(("groups", "basis"), None, None),
        P("groups", None),
        P(("groups", "basis"), None),
    )
    return jax.shard_map(
        per_device,
        mesh=mesh,
        in_specs=placed,
        out_specs=(P(("groups", "basis"), None, None, None), P(("groups", "basis"), None, None)),
        check_vma=False,
    )
```

```python
import functools

import jax
import jax.numpy as jnp
from jax import lax
from jax.experimental import pallas as pl
from jax.experimental.pallas import tpu as pltpu
from jax.sharding import PartitionSpec as P

F32 = jnp.float32
BF16 = jnp.bfloat16

XJ, XO, XJ_SIDE, YJ, YO, FJ, GJ = range(7)
XF, YF, YOF, XG, XY, XYO, CROSS, OWN = range(8)
PRODUCTS = ((XJ, FJ), (YJ, FJ), (YO, FJ), (XJ_SIDE, GJ), (XJ, YJ), (XO, YJ), (XO, None), (XJ, XO))
SHARED = (XF, YF, YOF, XG, XY, XYO, CROSS)
STACK, SHORT_STACK, OWN_STACK = 10, 8, 4
LIMIT = 12 * 2**20
LATE = 144


def cost(*arrays):
    return pl.CostEstimate(flops=1, bytes_accessed=sum(a.size * a.dtype.itemsize for a in arrays), transcendentals=0)


def smem(n):
    return [pl.BlockSpec(memory_space=pltpu.SMEM)] * n


def vmem(n):
    return [pl.BlockSpec(memory_space=pltpu.VMEM)] * n


def squares(n, width):
    return jax.ShapeDtypeStruct((n, width, width), F32)


def multiply(left, right):
    return lax.dot_general(left, right, (((0,), (0,)), ((), ())), preferred_element_type=F32)


def chip_route(count, target, swap=False):
    chips = count // 2
    route = []
    for chip in range(chips):
        to = target(chip)
        if 0 <= to < chips:
            for core in range(2):
                route.append((2 * chip + core, 2 * to + (1 - core if swap else core)))
    return route


def place_of_device():
    me = lax.axis_index("basis")
    core, chip = me & 1, me >> 1
    odd = chip & 1
    return me, core, chip, odd, core == odd, chip + 2 - 4 * odd, chip - 2 + 4 * odd, odd == ((chip >> 1) & 1)


def cut_kernel(size, wanted, own, *refs):
    outs, sems = refs[:-1], refs[-1]
    _, _, _, odd, _, _, _, f_near = place_of_device()
    side, main = (1 - odd) * size, odd * size
    near, far = jnp.where(f_near, side, main), jnp.where(f_near, main, side)
    starts = (side, side + size - LATE, near, far, main, side)
    copies = []
    for i, (out, at) in enumerate(zip(outs, wanted)):
        rows = pl.ds(pl.multiple_of(starts[at], 16), out.shape[1])
        copies.append(pltpu.make_async_copy(own.at[:, rows, :], out, sems.at[i]))
    for copy in copies:
        copy.start()
    for copy in copies:
        copy.wait()


def cut(own, wanted):
    rows, aux, width = own.shape
    half = aux // 2
    sizes = (half - LATE, LATE, half, half, half, half)
    return pl.pallas_call(
        functools.partial(cut_kernel, half, wanted),
        out_shape=[jax.ShapeDtypeStruct((rows, sizes[at], width), own.dtype) for at in wanted],
        in_specs=vmem(1),
        out_specs=vmem(len(wanted)),
        scratch_shapes=[pltpu.SemaphoreType.DMA((len(wanted),))],
        compiler_params=pltpu.CompilerParams(vmem_limit_bytes=LIMIT),
        cost_estimate=cost(own, own),
    )(own)


def lists_of(table):
    width = table.shape[1] // 2 - 4
    return lambda q: table[q, 2 * width], lambda q, slot: table[q, slot], lambda q, slot: table[q, width + slot]


def find_matches(domains, table, spot):
    count, rows = domains.shape
    width = table.shape[1] // 2 - 4
    _, core, chip, _, flag, f_chip, g_chip, _ = place_of_device()
    mine_first, other_first = (chip, core), (chip, 1 - core)
    block = {XJ: mine_first, XJ_SIDE: mine_first, XO: other_first, None: (jnp.where(flag, f_chip, g_chip), core)}
    block |= {YJ: (chip ^ 1, core), YO: (chip ^ 1, 1 - core), FJ: (f_chip, core), GJ: (g_chip, core)}

    for q, (left, right) in enumerate(PRODUCTS):
        there, ids = [], []
        for name in (left, right):
            at, one = block[name]
            there.append(jnp.logical_and(at >= 0, 2 * at < count))
            ids.append(2 * jnp.clip(at, 0, count // 2 - 1) + one)
        both = jnp.logical_and(*there)
        base = 2 * ids[1]

        def clear(i, carry):
            spot[i] = -1
            return carry

        def fill(row, carry):
            spot[domains[ids[1], row] - base] = row
            return carry

        def clean(slot, carry):
            table[q, slot] = 0
            table[q, width + slot] = 0
            return carry

        def scan(row, found):
            away = domains[ids[0], row] - base
            inside = jnp.logical_and(away >= 0, away < 2 * rows)
            other_row = spot[jnp.clip(away, 0, 2 * rows - 1)]
            hit = jnp.logical_and(jnp.logical_and(inside, both), other_row >= 0)
            table[q, found] = row
            table[q, width + found] = jnp.maximum(other_row, 0)
            return found + hit.astype(jnp.int32)

        lax.fori_loop(0, 2 * rows, clear, 0, unroll=10)
        lax.fori_loop(0, rows, fill, 0, unroll=10)
        lax.fori_loop(0, width, clean, 0, unroll=9)
        table[q, 2 * width] = lax.fori_loop(0, rows, scan, 0, unroll=5)


def own_kernel(domains, pairs, own, own_side, other, coef, out, share, table, spot):
    rows, half, width = own.shape
    me, _, _, odd, _, _, _, _ = place_of_device()
    find_matches(domains, table, spot)
    number, mine, theirs = lists_of(table)
    out[...] = jnp.zeros_like(out)
    size = max(n for n in range(1, 11) if rows % n == 0)

    def square(step, carry):
        for part in (own, own_side):
            left = part[pl.ds(size * step, size)].reshape(size * half, width)
            out[0] += multiply(left, left)
        return carry

    lax.fori_loop(0, rows // size, square, 0)

    def beside(step, carry):
        lefts, rights = [], []
        for i in range(OWN_STACK):
            slot = OWN_STACK * step + i
            for part, start in ((own, odd * half), (own_side, (1 - odd) * half)):
                left = part[mine(OWN, slot)]
                lefts.append(jnp.where(slot < number(OWN), left, jnp.zeros_like(left)))
                rights.append(other[theirs(OWN, slot), pl.ds(pl.multiple_of(start, 16), half), :])
        out[1] += multiply(jnp.concatenate(lefts, axis=0), jnp.concatenate(rights, axis=0))
        return carry

    lax.fori_loop(0, (number(OWN) + OWN_STACK - 1) // OWN_STACK, beside, 0)

    tile = 128
    parts = []
    for part in (own, own_side):
        sums = []
        for start in range(0, half, tile):
            total = jnp.zeros((tile, width), F32)
            for row in range(rows):
                total += part[row, start:start + tile, :].astype(F32) * coef[row:row + 1, :].astype(F32)
            sums.append(jnp.sum(total.T, axis=0, keepdims=True))
        parts.append(jnp.concatenate(sums, axis=1))
    share[:, :half] = jnp.where(odd == 1, parts[1], parts[0])
    share[:, half:2 * half] = jnp.where(odd == 1, parts[0], parts[1])
    depth = pairs.shape[1]
    lane = lax.broadcasted_iota(jnp.int32, (1, share.shape[1] - 2 * half), 1)
    marks = jnp.zeros(lane.shape, F32)
    for r in range(depth):
        marks = jnp.where(lane == me * depth + r, pairs[0, r].astype(F32), marks)
    share[:, 2 * half:] = marks


def own_products(domains, pairs, own, own_side, other, coef):
    rows, half, width = own.shape
    count = domains.shape[0]
    marks = -(-count * pairs.shape[1] // 128) * 128
    most = max(-(-rows // n) * n for n in (STACK, OWN_STACK))
    table = jax.ShapeDtypeStruct((len(PRODUCTS), 2 * most + 8), jnp.int32)
    return pl.pallas_call(
        own_kernel,
        out_shape=[
            squares(2, width),
            jax.ShapeDtypeStruct((1, 2 * half + marks), F32),
            table,
        ],
        in_specs=smem(2) + vmem(4),
        out_specs=vmem(2) + smem(1),
        scratch_shapes=[pltpu.SMEM((2 * rows,), jnp.int32)],
        compiler_params=pltpu.CompilerParams(vmem_limit_bytes=LIMIT),
        cost_estimate=cost(own, own_side, other),
    )(domains, pairs, own, own_side, other, coef)


def relay_kernel(count, parts, value, *refs):
    shares, (*outs, total, sems) = refs[:count], refs[-parts - 2:]
    copies, start = [], 0
    for i, out in enumerate(outs):
        size = out.shape[1]
        copies.append(pltpu.make_async_copy(value.at[:, start:start + size, :], out, sems.at[i]))
        start += size
    for copy in copies:
        copy.start()
    total[...] = sum(share[...] for share in shares)
    for copy in copies:
        copy.wait()


def relay(value, sizes, shares, *earlier):
    rows, _, width = value.shape
    parts = len(sizes)
    return pl.pallas_call(
        functools.partial(relay_kernel, len(shares), parts),
        out_shape=[jax.ShapeDtypeStruct((rows, size, width), value.dtype) for size in sizes] + [jax.ShapeDtypeStruct(shares[0].shape, F32)],
        in_specs=vmem(1 + len(shares) + len(earlier)),
        out_specs=vmem(parts + 1),
        scratch_shapes=[pltpu.SemaphoreType.DMA((parts,))],
        compiler_params=pltpu.CompilerParams(vmem_limit_bytes=LIMIT),
        cost_estimate=cost(value, value),
    )(value, *shares, *earlier)


def rows_product(table, q, first, size, left_of, right_of):
    number, mine, theirs = lists_of(table)
    lefts, rights = [], []
    for i in range(size):
        slot = first + i
        left = left_of(mine(q, slot))
        lefts.append(jnp.where(slot < number(q), left, jnp.zeros_like(left)))
        rights.append(right_of(theirs(q, slot)))
    return multiply(jnp.concatenate(lefts, axis=0), jnp.concatenate(rights, axis=0))


def early_kernel(table, xj, xo, yj, total):
    odd, (half, size) = place_of_device()[3], (xj.shape[1], yj.shape[1])
    main = pl.ds(pl.multiple_of(odd * half, 16), size)
    lefts = lambda row: xj[row, :size, :], lambda row: xo[row, main, :]
    number, _, _ = lists_of(table)
    for at, q in enumerate((XY, XYO)):
        total[at] = jnp.zeros(total.shape[1:], F32)

        def step(group, carry, at=at, q=q):
            total[at] += rows_product(table, q, group * STACK, STACK, lefts[at], lambda row: yj[row])
            return carry

        lax.fori_loop(0, (number(q) + STACK - 1) // STACK, step, 0)


def early_products(table, xj, xo, yj):
    return pl.pallas_call(
        early_kernel,
        out_shape=squares(2, xj.shape[-1]),
        in_specs=smem(1) + vmem(3),
        out_specs=vmem(1)[0],
        compiler_params=pltpu.CompilerParams(vmem_limit_bytes=2 * LIMIT),
        cost_estimate=cost(xj, xo, yj),
    )(table, xj, xo, yj)


def shared_kernel(table, xj, xj_side, xo, near, far, early, *refs):
    yj, yo, total = refs[:2], refs[2:-1], refs[-1]
    _, _, _, odd, flag, _, _, f_near = place_of_device()
    half, done = xj.shape[1], yj[0].shape[1]
    number, _, _ = lists_of(table)
    late = pl.ds(pl.multiple_of(odd * half + done, 16), half - done)
    cross = pl.ds(pl.multiple_of(jnp.where(flag, odd, 1 - odd) * half, 16), half)
    joined = lambda parts: lambda row: jnp.concatenate([part[row] for part in parts], axis=0)

    def product(q, first, size, block):
        left_of, right_of = {
            XF: (lambda row: xj[row], lambda row: block[FJ][row]),
            YF: (joined(yj), lambda row: block[FJ][row]),
            YOF: (joined(yo), lambda row: block[FJ][row]),
            XG: (lambda row: xj_side[row], lambda row: block[GJ][row]),
            XY: (lambda row: xj[row, done:, :], lambda row: yj[1][row]),
            XYO: (lambda row: xo[row, late, :], lambda row: yj[1][row]),
            CROSS: (lambda row: xo[row, cross, :], lambda row: jnp.where(flag, block[FJ][row], block[GJ][row])),
        }[q]
        return rows_product(table, q, first, size, left_of, right_of)

    def all_products(fj, gj):
        block = {FJ: fj, GJ: gj}
        most = number(SHARED[0])
        for at, q in enumerate(SHARED):
            most = jnp.maximum(most, number(q))
            total[at] = product(q, 0, STACK, block)
            if q in (XY, XYO):
                total[at] += early[(XY, XYO).index(q)]

        def steps(size):
            def step(i, carry):
                for at, q in enumerate(SHARED):
                    total[at] += product(q, STACK + i * size, size, block)
                return carry

            return step

        short = most <= STACK + SHORT_STACK
        more = jnp.maximum(most - STACK, 0)
        lax.fori_loop(0, jnp.where(short, jnp.minimum(more, 1), 0), steps(SHORT_STACK), 0)
        lax.fori_loop(0, jnp.where(short, 0, (more + STACK - 1) // STACK), steps(STACK), 0)

    @pl.when(f_near)
    def _():
        all_products(near, far)

    @pl.when(jnp.logical_not(f_near))
    def _():
        all_products(far, near)


def shared_products(table, *blocks):
    return pl.pallas_call(
        shared_kernel,
        out_shape=squares(len(SHARED), blocks[0].shape[-1]),
        in_specs=smem(1) + vmem(len(blocks)),
        out_specs=vmem(1)[0],
        compiler_params=pltpu.CompilerParams(vmem_limit_bytes=2 * LIMIT),
        cost_estimate=cost(*blocks),
    )(table, *blocks)


def message_kernel(total, *refs):
    shares, (to_near, to_far, to_mate, to_y, to_y_other, summed) = refs[:-6], refs[-6:]
    _, _, _, _, flag, _, _, f_near = place_of_device()
    width = total.shape[1]

    def put(out, values):
        for i, value in enumerate(values):
            out[i * width:(i + 1) * width, :] = value.astype(BF16)

    def to_f_and_g(to_f, to_g):
        cross = total[CROSS].T
        nothing = jnp.zeros_like(cross)
        put(to_f, (total[XF].T, jnp.where(flag, cross, nothing), total[YF].T, total[YOF].T))
        put(to_g, (total[XG].T, jnp.where(flag, nothing, cross), nothing, nothing))

    @pl.when(f_near)
    def _():
        to_f_and_g(to_near, to_far)

    @pl.when(jnp.logical_not(f_near))
    def _():
        to_f_and_g(to_far, to_near)

    put(to_y, (total[XY].T, total[XYO].T, total[YF]))
    to_y[3 * width:, :] = jnp.zeros((to_y.shape[0] - 3 * width, width), BF16)
    put(to_y_other, (total[YOF],))
    to_mate[0] = total[XYO]
    to_mate[1] = total[CROSS]
    gathered = sum(share[...] for share in shares)
    summed[...] = gathered
    lines = gathered.shape[1] // width
    rest, rows = gathered, []
    for _ in range(3):
        part = rest.astype(BF16)
        rest = rest - part.astype(F32)
        rows += [part[:, i * width:(i + 1) * width].astype(F32) for i in range(lines)]
    rows.append(jnp.zeros((to_near.shape[0] - 4 * width - 3 * lines, width), F32))
    to_near[4 * width:, :] = jnp.concatenate(rows, axis=0).astype(BF16)


def messages(total, shares):
    width = total.shape[-1]
    lines = -(-3 * shares[0].shape[1] // width // 16) * 16
    flat = jax.ShapeDtypeStruct
    sent = lambda rows: flat((rows, width), BF16)
    return pl.pallas_call(
        message_kernel,
        out_shape=[
            sent(4 * width + lines + 16), sent(4 * width), squares(2, width), sent(4 * width + 16), sent(width),
            flat(shares[0].shape, F32),
        ],
        in_specs=vmem(1 + len(shares)),
        out_specs=vmem(6),
        compiler_params=pltpu.CompilerParams(vmem_limit_bytes=LIMIT),
        cost_estimate=cost(total, total),
    )(total, *shares)


def coulomb_kernel(own, own_side, share, from_near, out, summed):
    rows, half, width = own.shape
    odd = place_of_device()[3]
    lines = share.shape[1] // width
    parts = from_near[4 * width:, :].astype(F32)
    line = lambda i: jnp.concatenate([parts[i * lines + j:i * lines + j + 1] for j in range(lines)], axis=1)
    gathered = share[...] + (line(0) + line(1) + line(2))
    summed[...] = gathered
    low, high = gathered[:, :half], gathered[:, half:2 * half]
    gamma = jnp.where(odd == 1, high, low).astype(BF16)
    side_gamma = jnp.where(odd == 1, low, high).astype(BF16)
    for row in range(rows):
        part = jnp.dot(gamma, own[row], preferred_element_type=F32)
        out[row] = part + jnp.dot(side_gamma, own_side[row], preferred_element_type=F32)


def coulomb(own, own_side, share, from_near):
    rows, _, width = own.shape
    flat = jax.ShapeDtypeStruct
    out, summed = pl.pallas_call(
        coulomb_kernel,
        out_shape=[flat((rows, 1, width), F32), flat(share.shape, F32)],
        in_specs=vmem(4),
        out_specs=vmem(2),
        compiler_params=pltpu.CompilerParams(vmem_limit_bytes=LIMIT),
        cost_estimate=cost(own, own_side),
    )(own, own_side, share, from_near)
    return jnp.swapaxes(out, 0, 1), summed


def band_kernel(aux, pairs, summed, own, total, from_y, from_near, from_far, from_mate, from_y_other, band, made, sems):
    depth, width = pairs.shape[1], band.shape[1]
    me, core, _, odd, _, _, _, f_near = place_of_device()
    count = lax.axis_size("basis")
    sign, cross = 1 - 2 * odd, 1 - 2 * core
    copies = []

    def put(ahead, value):
        far = jnp.abs(ahead)
        slot = len(copies)
        if slot == 0:
            made[slot] = value
        else:
            lower = summed[0, aux + jnp.maximum(me - far, 0) * depth + far - 1] > 0.5
            upper = pairs[0, far - 1] == 1
            there = jnp.logical_or(jnp.logical_and(ahead > 0, upper), jnp.logical_and(ahead < 0, lower))
            there = jnp.logical_and(there, jnp.logical_and(me + ahead >= 0, me + ahead < count))
            made[slot] = jnp.where(there, value, 0.0)
        copies.append(pltpu.make_async_copy(made.at[slot], band.at[depth + ahead], sems.at[slot]))
        copies[-1].start()

    block = lambda ref, i: ref[i * width:(i + 1) * width, :].astype(F32)
    from_f = lambda i: jnp.where(f_near, block(from_far, i), block(from_near, i))
    from_g = lambda i: jnp.where(f_near, block(from_near, i), block(from_far, i))
    put(0, own[0])
    put(cross, own[1])
    put(2 * sign, total[XY] + block(from_y, 0))
    put(2 * sign + cross, from_mate[0] + block(from_y, 1))
    put(-2 * sign, block(from_y, 2) + from_f(2))
    put(-2 * sign + cross, block(from_y_other, 0) + from_f(3))
    put(4 * sign, total[XF] + from_g(0))
    put(-4 * sign, total[XG] + from_f(0))
    put(-3 * cross, from_mate[1] + from_f(1) + from_g(1))
    for copy in copies:
        copy.wait()


def finish(aux, pairs, summed, own, *partials):
    depth, width = pairs.shape[1], own.shape[-1]
    size = 2 * depth + 1
    return pl.pallas_call(
        functools.partial(band_kernel, aux),
        out_shape=squares(size, width),
        in_specs=smem(2) + vmem(1 + len(partials)),
        out_specs=pl.BlockSpec(memory_space=pl.ANY),
        scratch_shapes=[pltpu.VMEM((size, width, width), F32), pltpu.SemaphoreType.DMA((size,))],
        compiler_params=pltpu.CompilerParams(vmem_limit_bytes=LIMIT),
        cost_estimate=cost(own, *partials),
    )(pairs, summed, own, *partials)


def add_kernel(*refs):
    refs[-1][...] = sum(share[...] for share in refs[:-1])


def added(shares):
    return pl.pallas_call(
        add_kernel,
        out_shape=jax.ShapeDtypeStruct(shares[0].shape, F32),
        in_specs=vmem(len(shares)),
        out_specs=vmem(1)[0],
        compiler_params=pltpu.CompilerParams(vmem_limit_bytes=LIMIT),
        cost_estimate=cost(*shares),
    )(*shares)


def shares_of(values, count, step):
    return [values, lax.ppermute(values, "basis", [(i, i ^ step) for i in range(count)])]


def per_device(factors, coefs, domains, pairs):
    own = factors[0]
    _, aux, _ = own.shape
    count = lax.axis_size("basis")

    swap = chip_route(count, lambda c: c, swap=True)
    across = chip_route(count, lambda c: c ^ 1)
    to_near = chip_route(count, lambda c: c ^ 2)
    to_far = chip_route(count, lambda c: c - 2 if c & 2 == 0 else c + 2)
    senders = {source for source, _ in to_far}
    to_far += [(i, i ^ 1) for i in range(count) if i not in senders]
    send = lambda value, route: lax.ppermute(value, "basis", route)

    xo = send(own, swap)
    (early,) = cut(own, (0,))
    late, for_near, for_far = cut(own, (1, 2, 3))
    xj, xj_side = cut(own, (4, 5))
    yj = send(early, across), send(late, across)
    near, far = send(for_near, to_near), send(for_far, to_far)
    own_pairs, share, table = own_products(domains, pairs, xj, xj_side, xo, coefs[0])
    share = added(shares_of(share, count, 1))
    with_y = early_products(table, xj, xo, yj[0])
    part, _ = relay(yj[0], (yj[0].shape[1],), [share])
    yo = [send(part, swap)]
    first = LATE // 32 * 16 + LATE % 32
    *parts, share = relay(yj[1], (first, LATE - first), shares_of(share, count, 2), with_y, *yo)
    yo += [send(part, swap) for part in parts]
    shares, step = [share], 8
    while step < count:
        if len(shares) > 1:
            shares = [added(shares)]
        shares = shares_of(shares[0], count, step)
        step *= 2
    total = shared_products(table, xj, xj_side, xo, near, far, with_y, *yj, *yo)
    for_near, for_far, for_mate, for_y, for_y_other, share = messages(total, shares)
    from_near, from_far = send(for_near, to_near), send(for_far, to_far)
    from_y, from_y_other = send(for_y, across), send(for_y_other, chip_route(count, lambda c: c ^ 1, swap=True))
    from_mate = send(for_mate, swap)
    coulomb_half, summed = coulomb(xj, xj_side, share, from_near)
    band = finish(aux, pairs, summed, own_pairs, total, from_y, from_near, from_far, from_mate, from_y_other)
    return (band[None], coulomb_half)


def solution(mesh):
    placed = (
        P(("groups", "basis"), None, None, None),
        P(("groups", "basis"), None, None),
        P("groups", None),
        P(("groups", "basis"), None),
    )
    return jax.shard_map(
        per_device,
        mesh=mesh,
        in_specs=placed,
        out_specs=(P(("groups", "basis"), None, None, None), P(("groups", "basis"), None, None)),
        check_vma=False,
    )
```
